32 devices in a mesh: rep: 4 (over z), fsdp: 8 (over y, x, core).
Axes of the slice: x: 2, y: 2, z: 4, core: 2. Of those that a mesh axis runs over, the one named last changes fastest.
Arguments:
- features: bfloat16 [384, 28, 28, 128], P(('rep', 'fsdp')), may hold values from -6 to 6
- labels: int32 [384], P(('rep', 'fsdp')), may hold values from 0 to 999
- counts: int32 [4, 8], P('rep', 'fsdp'), may hold values from 1 to 12, as said below
- tables: int32 [2, 196, 49], replicated, may hold values from 0 to 195, as said below
- conv_weight: float32 [1152, 256], P('fsdp'), may hold values from -0.1875 to 0.1875
- qkv_weight: float32 [2, 256, 768], P(None, 'fsdp'), may hold values from -0.375 to 0.375
- proj_weight: float32 [2, 256, 256], P(None, 'fsdp'), may hold values from -1 to 1
- up_weight: float32 [2, 256, 768], P(None, 'fsdp'), may hold values from -0.375 to 0.375
- down_weight: float32 [2, 768, 256], P(None, 'fsdp'), may hold values from -0.21875 to 0.21875
- head_weight: float32 [256, 1000], P('fsdp'), may hold values from -4 to 4
- conv_mom: float32 [1152, 256], P('fsdp'), may hold values from -0.0234375 to 0.0234375
- qkv_mom: float32 [2, 256, 768], P(None, 'fsdp'), may hold values from -0.0234375 to 0.0234375
- proj_mom: float32 [2, 256, 256], P(None, 'fsdp'), may hold values from -0.0234375 to 0.0234375
- up_mom: float32 [2, 256, 768], P(None, 'fsdp'), may hold values from -0.0234375 to 0.0234375
- down_mom: float32 [2, 768, 256], P(None, 'fsdp'), may hold values from -0.0234375 to 0.0234375
- head_mom: float32 [256, 1000], P('fsdp'), may hold values from -0.3125 to 0.3125
- conv_err: float32 [4, 1152, 256], P('rep', 'fsdp'), may hold values from -0.0234375 to 0.0234375
- qkv_err: float32 [4, 2, 256, 768], P('rep', None, 'fsdp'), may hold values from -0.0234375 to 0.0234375
- proj_err: float32 [4, 2, 256, 256], P('rep', None, 'fsdp'), may hold values from -0.0234375 to 0.0234375
- up_err: float32 [4, 2, 256, 768], P('rep', None, 'fsdp'), may hold values from -0.0234375 to 0.0234375
- down_err: float32 [4, 2, 768, 256], P('rep', None, 'fsdp'), may hold values from -0.0234375 to 0.0234375
- head_err: float32 [4, 256, 1000], P('rep', 'fsdp'), may hold values from -0.3125 to 0.3125
- conv_fac: float32 [256, 8], replicated, may hold values from -5 to 5
- qkv_fac: float32 [2, 768, 8], replicated, may hold values from -5 to 5
- proj_fac: float32 [2, 256, 8], replicated, may hold values from -5 to 5
- up_fac: float32 [2, 768, 8], replicated, may hold values from -5 to 5
- down_fac: float32 [2, 256, 8], replicated, may hold values from -5 to 5
- head_fac: float32 [1000, 8], replicated, may hold values from -5 to 5
- small_params: float32 [10616], replicated
- small_mom: float32 [10616], replicated, may hold values from -0.3125 to 0.3125
Outputs:
- loss_sum: float32 [], replicated
- item_count: float32 [], replicated
- new_conv_weight: float32 [1152, 256], P('fsdp')
- new_qkv_weight: float32 [2, 256, 768], P(None, 'fsdp')
- new_proj_weight: float32 [2, 256, 256], P(None, 'fsdp')
- new_up_weight: float32 [2, 256, 768], P(None, 'fsdp')
- new_down_weight: float32 [2, 768, 256], P(None, 'fsdp')
- new_head_weight: float32 [256, 1000], P('fsdp')
- new_conv_mom: float32 [1152, 256], P('fsdp')
- new_qkv_mom: float32 [2, 256, 768], P(None, 'fsdp')
- new_proj_mom: float32 [2, 256, 256], P(None, 'fsdp')
- new_up_mom: float32 [2, 256, 768], P(None, 'fsdp')
- new_down_mom: float32 [2, 768, 256], P(None, 'fsdp')
- new_head_mom: float32 [256, 1000], P('fsdp')
- new_conv_err: float32 [4, 1152, 256], P('rep', 'fsdp')
- new_qkv_err: float32 [4, 2, 256, 768], P('rep', None, 'fsdp')
- new_proj_err: float32 [4, 2, 256, 256], P('rep', None, 'fsdp')
- new_up_err: float32 [4, 2, 256, 768], P('rep', None, 'fsdp')
- new_down_err: float32 [4, 2, 768, 256], P('rep', None, 'fsdp')
- new_head_err: float32 [4, 256, 1000], P('rep', 'fsdp')
- new_conv_fac: float32 [256, 8], replicated
- new_qkv_fac: float32 [2, 768, 8], replicated
- new_proj_fac: float32 [2, 256, 8], replicated
- new_up_fac: float32 [2, 768, 8], replicated
- new_down_fac: float32 [2, 256, 8], replicated
- new_head_fac: float32 [1000, 8], replicated
- new_small_params: float32 [10616], replicated
- new_small_mom: float32 [10616], replicated
The draws below stay inside these ranges and needn't reach their ends.
Inputs may be any that keep to these rules, and one draw needn't show every extreme that they name: counts: live items of each device; the last device of both axes holds 12. `tables`: row q of layer l lists, in some order, the 49 cells of the 7 x 7 neighbourhood of cell q (cells numbered row by row on the 14 x 14 grid) with dilation 1 + (l mod 2), the window moved inside the grid at its rims.
All inputs are finite; a program needn't handle non-finite values.
Results may differ from the reference program's by a relative error of at most 0.012.
The reference program's roundings to bfloat16 on the way (of `joined`, `mixed_out` and `active`) count: a program that leaves them out, or rounds other values in their place, can miss the bound.
Values may be sent and summed in bfloat16 or wider, within the bound.
No kernel may reach another device: no remote copies, remote signals or barrier semaphores. Data moves between devices by JAX's collectives and lax.ppermute only.
A program may use at most 320 MiB of HBM per device.

```python
import jax
import jax.numpy as jnp
from jax import lax

D = 256
HEADS = 8
HEAD = 32
FF = 768
CLASSES = 1000
CIN = 128
GRID = 14
KER = 7
RANK = 8
LAYERS = 2
SLOTS = 12
REPS = 4
SHARDS = 8
ITEMS = 384
PIX = 196
TOKENS = 75264
NBR = 49
RB = 169
VEC = 10616


def segments_drawn():
    pieces = [('bias', D), ('gain', D), ('bias', D)]
    for layer_idx in range(LAYERS):
        pieces += [('gain', D), ('bias', D), ('bias', D), ('bias', D), ('bias', D), ('gain', D), ('bias', D), ('bias', D), ('bias', FF), ('table', HEADS * RB)]
    return pieces + [('gain', D), ('bias', D), ('bias', CLASSES)]


def window_cells(dilation):
    cell_ids = jnp.arange(GRID)
    residue = cell_ids % dilation
    position = cell_ids // dilation
    length = (GRID - residue + dilation - 1) // dilation
    first_cell = jnp.clip(position - KER // 2, 0, length - KER)
    return residue[:, None] + dilation * (first_cell[:, None] + jnp.arange(KER)[None, :])


def draw_counts(key, part):
    key = jax.random.fold_in(key, 11)
    rep_ids = jnp.arange(REPS)[:, None]
    shard_ids = jnp.arange(SHARDS)[None, :]
    lowest = max(SLOTS // 3, 1)
    rising = lowest + (SLOTS - lowest) * (rep_ids + shard_ids) // max(REPS + SHARDS - 2, 1)
    jitter = jax.random.randint(key, (REPS, SHARDS), -1, 2)
    drawn = jnp.clip(rising + jitter, 1, SLOTS)
    return drawn.at[REPS - 1, SHARDS - 1].set(SLOTS).astype(jnp.int32)


def draw_tables(key, part):
    key = jax.random.fold_in(key, 12)
    layers_out = []
    for layer_idx in range(LAYERS):
        across = window_cells(1 + layer_idx % 2)
        cell_rows = (across[:, None, :, None] * GRID + across[None, :, None, :]).reshape(PIX, NBR)
        scores = jax.random.randint(jax.random.fold_in(key, layer_idx), (PIX, NBR), 0, 1 << 20) * NBR + jnp.arange(NBR)[None, :]
        order = jnp.argsort(scores, axis=1, stable=True)
        layers_out.append(jnp.take_along_axis(cell_rows, order, axis=1))
    return jnp.stack(layers_out).astype(jnp.int32)


def draw_small_params(key, part):
    key = jax.random.fold_in(key, 13)
    pieces = []
    for seg_index, (seg_kind, length) in enumerate(segments_drawn()):
        drawn = jax.random.normal(jax.random.fold_in(key, seg_index), (length,), jnp.float32)
        if seg_kind == 'gain':
            pieces.append(1.0 + 0.1 * drawn)
        elif seg_kind == 'bias':
            pieces.append(0.1 * drawn)
        else:
            pieces.append(drawn)
    return jnp.concatenate(pieces)


def plant(result, rng, least, high):
    longest = result.shape.index(max(result.shape))
    spots = []
    for shift in (0, 1):
        where = [jax.random.randint(jax.random.fold_in(rng, axis), (), 0, length) for axis, length in enumerate(result.shape)]
        where[longest] = (where[longest] + shift) % result.shape[longest]
        spots.append(tuple(where))
    return result.at[spots[0]].set(least).at[spots[1]].set(high)


def steps_of(stream_key, extent, shards, least, largest):
    level = 1.0
    for dim, blocks in shards:
        draws = jax.random.uniform(jax.random.fold_in(jax.random.fold_in(stream_key, 6), dim), (blocks,), jnp.float32, least / len(shards), largest / len(shards))
        level = level * jnp.repeat(jnp.exp(draws), extent[dim] // blocks).reshape((-1,) + (1,) * (len(extent) - 1 - dim))
    return level


def normal_values(rng, shape, scale, most, shards=(), held_as=jnp.bfloat16):
    entries = jax.random.normal(rng, shape, jnp.float32) * scale
    if len(shards) > 0:
        entries = steps_of(rng, shape, shards, -0.22, 0.18) * entries
    return jnp.clip(entries, min=-most, max=most).astype(held_as)


def setup_inputs(seed: int = 0) -> dict:
    splits = jax.random.split(jax.random.key(seed), 31)
    features = normal_values(splits[0], (ITEMS, 2 * GRID, 2 * GRID, CIN), 1.0, 6.0, ((0, 32),))
    labels = plant(jax.random.randint(splits[1], (ITEMS,), 0, CLASSES), jax.random.fold_in(splits[1], 1), 0, CLASSES - 1).astype(jnp.int32)
    counts = draw_counts(jax.random.fold_in(splits[30], 71), 0)
    tables = draw_tables(jax.random.fold_in(splits[30], 71), 0)
    conv_weight = normal_values(splits[4], (9 * CIN, D), (9 * CIN) ** -0.5, 0.1875, ((0, 8),), jnp.float32)
    qkv_weight = normal_values(splits[5], (LAYERS, D, 3 * D), D ** -0.5, 0.375, ((1, 8),), jnp.float32)
    proj_weight = normal_values(splits[6], (LAYERS, D, D), (D // 7) ** -0.5, 1.0, ((1, 8),), jnp.float32)
    up_weight = normal_values(splits[7], (LAYERS, D, FF), D ** -0.5, 0.375, ((1, 8),), jnp.float32)
    down_weight = normal_values(splits[8], (LAYERS, FF, D), FF ** -0.5, 0.21875, ((1, 8),), jnp.float32)
    head_weight = normal_values(splits[9], (D, CLASSES), 0.6, 4.0, ((0, 8),), jnp.float32)
    conv_mom = normal_values(splits[10], (9 * CIN, D), TOKENS ** -0.5, 0.0234375, ((0, 8),), jnp.float32)
    qkv_mom = normal_values(splits[11], (LAYERS, D, 3 * D), TOKENS ** -0.5, 0.0234375, ((1, 8),), jnp.float32)
    proj_mom = normal_values(splits[12], (LAYERS, D, D), TOKENS ** -0.5, 0.0234375, ((1, 8),), jnp.float32)
    up_mom = normal_values(splits[13], (LAYERS, D, FF), TOKENS ** -0.5, 0.0234375, ((1, 8),), jnp.float32)
    down_mom = normal_values(splits[14], (LAYERS, FF, D), TOKENS ** -0.5, 0.0234375, ((1, 8),), jnp.float32)
    head_mom = normal_values(splits[15], (D, CLASSES), ITEMS ** -0.5, 0.3125, ((0, 8),), jnp.float32)
    conv_err = normal_values(splits[16], (REPS, 9 * CIN, D), TOKENS ** -0.5, 0.0234375, ((0, 4), (1, 8)), jnp.float32)
    qkv_err = normal_values(splits[17], (REPS, LAYERS, D, 3 * D), TOKENS ** -0.5, 0.0234375, ((0, 4), (2, 8)), jnp.float32)
    proj_err = normal_values(splits[18], (REPS, LAYERS, D, D), TOKENS ** -0.5, 0.0234375, ((0, 4), (2, 8)), jnp.float32)
    up_err = normal_values(splits[19], (REPS, LAYERS, D, FF), TOKENS ** -0.5, 0.0234375, ((0, 4), (2, 8)), jnp.float32)
    down_err = normal_values(splits[20], (REPS, LAYERS, FF, D), TOKENS ** -0.5, 0.0234375, ((0, 4), (2, 8)), jnp.float32)
    head_err = normal_values(splits[21], (REPS, D, CLASSES), ITEMS ** -0.5, 0.3125, ((0, 4), (1, 8)), jnp.float32)
    conv_fac = normal_values(splits[22], (D, RANK), 1.0, 5.0, (), jnp.float32)
    qkv_fac = normal_values(splits[23], (LAYERS, 3 * D, RANK), 1.0, 5.0, (), jnp.float32)
    proj_fac = normal_values(splits[24], (LAYERS, D, RANK), 1.0, 5.0, (), jnp.float32)
    up_fac = normal_values(splits[25], (LAYERS, FF, RANK), 1.0, 5.0, (), jnp.float32)
    down_fac = normal_values(splits[26], (LAYERS, D, RANK), 1.0, 5.0, (), jnp.float32)
    head_fac = normal_values(splits[27], (CLASSES, RANK), 1.0, 5.0, (), jnp.float32)
    small_params = draw_small_params(jax.random.fold_in(splits[30], 71), 0)
    small_mom = normal_values(splits[29], (VEC,), ITEMS ** -0.5, 0.3125, (), jnp.float32)
    return dict(features=features, labels=labels, counts=counts, tables=tables, conv_weight=conv_weight, qkv_weight=qkv_weight, proj_weight=proj_weight, up_weight=up_weight, down_weight=down_weight, head_weight=head_weight, conv_mom=conv_mom, qkv_mom=qkv_mom, proj_mom=proj_mom, up_mom=up_mom, down_mom=down_mom, head_mom=head_mom, conv_err=conv_err, qkv_err=qkv_err, proj_err=proj_err, up_err=up_err, down_err=down_err, head_err=head_err, conv_fac=conv_fac, qkv_fac=qkv_fac, proj_fac=proj_fac, up_fac=up_fac, down_fac=down_fac, head_fac=head_fac, small_params=small_params, small_mom=small_mom)


EPSILON = 1e-05
MASKED = -1000000000.0
MOMENTUM = 0.9
LEARN_RATE = 16.0
SMALL_RATE = 4.0
PRECISE = lax.Precision.HIGHEST

@jax.custom_vjp
def low(v):
    return lax.optimization_barrier(v.astype(jnp.bfloat16)).astype(jnp.float32)

@jax.custom_vjp
def low_back(v):
    return v

def low_keep(v):
    return (low(v), None)

def low_pass(kept, grad):
    return (grad,)

def back_keep(v):
    return (v, None)

def back_low(kept, grad):
    return (low(grad),)
low.defvjp(low_keep, low_pass)
low_back.defvjp(back_keep, back_low)

def segments():
    pieces = [('bias', D), ('gain', D), ('bias', D)]
    for layer_idx in range(LAYERS):
        pieces += [('gain', D), ('bias', D), ('bias', D), ('bias', D), ('bias', D), ('gain', D), ('bias', D), ('bias', D), ('bias', FF), ('table', HEADS * RB)]
    return pieces + [('gain', D), ('bias', D), ('bias', CLASSES)]

def unpack(vector):
    pieces, offset = ([], 0)
    for seg_kind, length in segments():
        pieces.append(vector[offset:offset + length])
        offset += length
    return pieces

def layer_norm(values, gain, shift):
    centred = values - lax.optimization_barrier(jnp.mean(values, axis=-1, keepdims=True))
    variance = lax.optimization_barrier(jnp.mean(centred * centred, axis=-1, keepdims=True))
    return centred * lax.rsqrt(variance + EPSILON) * gain + shift

def both_ways(values):
    return low(low_back(values))

def patches_of(images):
    padded = jnp.pad(images, ((0, 0), (1, 1), (1, 1), (0, 0)))
    return jnp.concatenate([padded[:, row_off:row_off + 2 * GRID:2, col_off:col_off + 2 * GRID:2, :] for row_off in range(3) for col_off in range(3)], axis=-1)

def neighbour_maps(tables):
    cell_ids = jnp.arange(PIX, dtype=jnp.int32)
    key_maps, rel_maps = ([], [])
    for layer_idx in range(LAYERS):
        dilation = 1 + layer_idx % 2
        table_now = tables[layer_idx]
        row_step = table_now // GRID // dilation - (cell_ids // GRID // dilation)[:, None] + KER - 1
        col_step = table_now % GRID // dilation - (cell_ids % GRID // dilation)[:, None] + KER - 1
        rel_index = row_step * (2 * KER - 1) + col_step
        key_maps.append((table_now[:, :, None] == cell_ids[None, None, :]).astype(jnp.float32))
        rel_maps.append((rel_index[:, :, None] == jnp.arange(RB, dtype=jnp.int32)[None, None, :]).astype(jnp.float32))
    return (key_maps, rel_maps)

def dense_bias(key_map, rel_map, rel_table):
    chosen = jnp.einsum('qjr,hr->hqj', rel_map, rel_table.reshape(HEADS, RB), precision=PRECISE)
    spread = jnp.einsum('qjk,hqj->hqk', key_map, chosen, precision=PRECISE)
    inside = lax.optimization_barrier(jnp.sum(key_map, axis=1)) > 0.5
    return jnp.where(inside[None], spread, MASKED)

def split_heads(joined, which):
    return joined[..., which * D:(which + 1) * D].reshape(joined.shape[0], PIX, HEADS, HEAD)

def sub_layer(hidden, weights, vectors, bias_map):
    qkv_w, proj_w, up_w, down_w = weights
    gain_one, shift_one, bias_query, bias_value, bias_proj, gain_two, shift_two, bias_down, bias_up, rel_table = vectors
    normed_one = low(layer_norm(hidden, gain_one, shift_one))
    joined = both_ways(jnp.einsum('npd,de->npe', normed_one, low(qkv_w), precision=PRECISE) + jnp.concatenate([bias_query, jnp.zeros_like(bias_query), bias_value]))
    scores = low_back(jnp.einsum('nqhd,nkhd->nhqk', split_heads(joined, 0), split_heads(joined, 1), precision=PRECISE) * HEAD ** (-0.5) + bias_map)
    attn_probs = low(jax.nn.softmax(scores, axis=-1))
    mixed_out = both_ways(jnp.einsum('nhqk,nkhd->nqhd', attn_probs, split_heads(joined, 2), precision=PRECISE).reshape(hidden.shape))
    after_attn = hidden + low_back(jnp.einsum('npd,de->npe', mixed_out, low(proj_w), precision=PRECISE) + bias_proj)
    normed_two = low(layer_norm(after_attn, gain_two, shift_two))
    pre_act = low_back(jnp.einsum('npd,df->npf', normed_two, low(up_w), precision=PRECISE) + bias_up)
    active = low(jax.nn.gelu(pre_act, approximate=False))
    return after_attn + low_back(jnp.einsum('npf,fd->npd', active, low(down_w), precision=PRECISE) + bias_down)

def block_loss(params, images, block_labels, live_mask, key_maps, rel_maps):
    conv_w, qkv_w, proj_w, up_w, down_w, head_w, small_vec = params
    pieces = unpack(small_vec)
    patches = patches_of(images.astype(jnp.float32)).reshape(images.shape[0], PIX, 9 * CIN)
    conv_out = low_back(jnp.einsum('npc,cd->npd', patches, low(conv_w), precision=PRECISE) + pieces[0])
    hidden = layer_norm(conv_out, pieces[1], pieces[2])
    for layer_idx in range(LAYERS):
        vectors = pieces[3 + 10 * layer_idx:13 + 10 * layer_idx]
        bias_map = dense_bias(key_maps[layer_idx], rel_maps[layer_idx], vectors[9])
        hidden = sub_layer(hidden, (qkv_w[layer_idx], proj_w[layer_idx], up_w[layer_idx], down_w[layer_idx]), vectors, bias_map)
    pooled = low(lax.optimization_barrier(jnp.mean(layer_norm(hidden, pieces[-3], pieces[-2]), axis=1)))
    logits = low_back(jnp.dot(pooled, low(head_w), precision=PRECISE) + pieces[-1])
    onehot = (block_labels[:, None] == jnp.arange(CLASSES, dtype=jnp.int32)[None, :]).astype(jnp.float32)
    losses = jax.nn.logsumexp(logits, axis=-1) - lax.optimization_barrier(jnp.sum(logits * onehot, axis=-1))
    return jnp.sum(live_mask * losses)

def compress(gradients, weight, momentum, errors, factor):
    merged = gradients + errors
    product = jnp.einsum('rbio,bok->bik', merged, factor, precision=PRECISE)
    gram_mat = jnp.einsum('bik,bil->bkl', product, product, precision=PRECISE)
    lower_tri = jnp.linalg.cholesky(gram_mat)
    basis_p = jnp.swapaxes(jax.scipy.linalg.solve_triangular(lower_tri, jnp.swapaxes(product, 1, 2), lower=True), 1, 2)
    local_q = jnp.einsum('rbio,bik->rbok', merged, basis_p, precision=PRECISE)
    new_err = merged - jnp.einsum('bik,rbok->rbio', basis_p, local_q, precision=PRECISE)
    summed = lax.optimization_barrier(jnp.sum(local_q, axis=0))
    new_mom = MOMENTUM * momentum + jnp.einsum('bik,bok->bio', basis_p, summed, precision=PRECISE)
    return (weight - LEARN_RATE * new_mom, new_mom, new_err, summed)

def reference(features, labels, counts, tables, conv_weight, qkv_weight, proj_weight, up_weight, down_weight, head_weight, conv_mom, qkv_mom, proj_mom, up_mom, down_mom, head_mom, conv_err, qkv_err, proj_err, up_err, down_err, head_err, conv_fac, qkv_fac, proj_fac, up_fac, down_fac, head_fac, small_params, small_mom):
    key_maps, rel_maps = neighbour_maps(tables)
    item_count = jnp.sum(counts.astype(jnp.float32))
    inverse = 1.0 / item_count
    params = (conv_weight, qkv_weight, proj_weight, up_weight, down_weight, head_weight, small_params)
    images = features.reshape(REPS, SHARDS, SLOTS, 2 * GRID, 2 * GRID, CIN)
    label_sets = labels.reshape(REPS, SHARDS, SLOTS)
    live_mask = (jnp.arange(SLOTS, dtype=jnp.int32)[None, None, :] < counts[:, :, None]).astype(jnp.float32)

    def per_block(running, inputs):
        block_images, block_labels, block_live = inputs
        loss_value, pull = jax.vjp(lambda p: block_loss(p, block_images, block_labels, block_live, key_maps, rel_maps), params)
        gradients = pull(inverse)[0]
        return ((running[0] + loss_value, jax.tree.map(jnp.add, running[1], gradients)), None)

    def per_replica(inputs):
        initial = (jnp.zeros((), jnp.float32), jax.tree.map(jnp.zeros_like, params))
        return lax.scan(per_block, initial, inputs)[0]
    losses, gradients = lax.map(per_replica, (images, label_sets, live_mask))
    loss_sum = jnp.sum(losses)
    conv_res = compress(gradients[0][:, None], conv_weight[None], conv_mom[None], conv_err[:, None], conv_fac[None])
    qkv_res = compress(gradients[1], qkv_weight, qkv_mom, qkv_err, qkv_fac)
    proj_res = compress(gradients[2], proj_weight, proj_mom, proj_err, proj_fac)
    up_res = compress(gradients[3], up_weight, up_mom, up_err, up_fac)
    down_res = compress(gradients[4], down_weight, down_mom, down_err, down_fac)
    head_res = compress(gradients[5][:, None], head_weight[None], head_mom[None], head_err[:, None], head_fac[None])
    new_small_mom = MOMENTUM * small_mom + lax.optimization_barrier(jnp.sum(gradients[6], axis=0))
    new_small = small_params - SMALL_RATE * new_small_mom
    return (loss_sum, item_count, conv_res[0][0], qkv_res[0], proj_res[0], up_res[0], down_res[0], head_res[0][0], conv_res[1][0], qkv_res[1], proj_res[1], up_res[1], down_res[1], head_res[1][0], conv_res[2][:, 0], qkv_res[2], proj_res[2], up_res[2], down_res[2], head_res[2][:, 0], conv_res[3][0], qkv_res[3], proj_res[3], up_res[3], down_res[3], head_res[3][0], new_small, new_small_mom)
```

```python
import functools
import types

import jax
import jax.numpy as jnp
import numpy as np
from jax import lax
from jax.experimental import pallas as pl
from jax.experimental.pallas import tpu as pltpu
from jax.sharding import PartitionSpec as P

D = 256
HEADS = 8
HEAD = 32
FF = 768
CLASSES = 1000
CPAD = 1024
CIN = 128
GRID = 14
KER = 7
LAYERS = 2
PIX = 196
RB = 169
RANK = 8

EPSILON = 1e-05
MASKED = -1000000000.0
MOMENTUM = 0.9
LEARN_RATE = 16.0
SMALL_RATE = 4.0
PRECISE = lax.Precision.HIGHEST
SCALE = HEAD ** (-0.5)

COLS = 16
TOK = GRID * COLS
KEYS = 128
HALF = 128
PARTS = 3 * CIN
F32 = jnp.float32
BF16 = jnp.bfloat16
VMEM_LIMIT = 58 * 1024 * 1024

GROUPS = (
    ((0, 80, 0), (80, 32, 32), (112, 32, 64), (144, 80, 96)),
    ((0, 112, 0), (112, 112, 96)),
)


def row_order(layer):
    if layer % 2 == 0:
        return list(range(GRID))
    return [*range(0, GRID, 2), *range(1, GRID, 2)]


def window_start(cell, dil):
    residue, position = cell % dil, cell // dil
    length = (GRID - residue + dil - 1) // dil
    return min(max(position - KER // 2, 0), length - KER)


def in_window(query, key, dil):
    if query % dil != key % dil:
        return False
    first = window_start(query, dil)
    return first <= key // dil < first + KER


@functools.lru_cache(None)
def static_maps(layer):
    dil = 1 + layer % 2
    order = row_order(layer)
    rows_hot = np.zeros((GRID * 8, 16), np.float32)
    mask = np.zeros((TOK, KEYS), np.float32)
    for q0, nq, k0 in GROUPS[layer % 2]:
        for place in range(q0 // COLS, (q0 + nq) // COLS):
            qy = order[place]
            for j in range(8):
                ky = order[k0 // COLS + j]
                if not in_window(qy, ky, dil):
                    continue
                rows_hot[place * 8 + j, ky // dil - qy // dil + KER - 1] = 1.0
                for x in range(GRID):
                    for kx in range(GRID):
                        if in_window(x, kx, dil):
                            mask[place * COLS + x, j * COLS + kx] = 1.0
    shifts = np.zeros((COLS, KEYS, KEYS), np.float32)
    for x in range(GRID):
        for kx in range(GRID):
            if in_window(x, kx, dil):
                dx = kx // dil - x // dil + KER - 1
                for j in range(8):
                    shifts[x, j * COLS + dx, j * COLS + kx] = 1.0
    return rows_hot, shifts, mask


def norm_stats(values):
    centred = values - jnp.mean(values, axis=-1, keepdims=True)
    rstd = lax.rsqrt(jnp.mean(centred * centred, axis=-1, keepdims=True) + EPSILON)
    return centred * rstd, rstd


def norm_back(grad, xhat, rstd, gain):
    scaled = grad * gain
    mean_one = jnp.mean(scaled, axis=-1, keepdims=True)
    mean_two = jnp.mean(scaled * xhat, axis=-1, keepdims=True)
    return rstd * (scaled - mean_one - xhat * mean_two)


def col_sum(values):
    return jnp.sum(values, axis=0, keepdims=True)


def dot_nn(a, b, **kw):
    return lax.dot_general(a, b, (((1,), (0,)), ((), ())), preferred_element_type=F32, **kw)


def dot_nt(a, b, **kw):
    return lax.dot_general(a, b, (((1,), (1,)), ((), ())), preferred_element_type=F32, **kw)


def dot_tn(a, b, **kw):
    return lax.dot_general(a, b, (((0,), (0,)), ((), ())), preferred_element_type=F32, **kw)


ERFC_T = 0.44
ERFC_POLY = (
    0.24822096599679971,
    0.24887097779118345,
    0.21731489562842682,
    0.21580753897325447,
    -0.020171305217729862,
    0.2966767736009737,
    -0.2779414931115683,
    0.07122182759012696,
)


def gelu_parts(x):
    bell = jnp.exp(-0.5 * x * x)
    t = 1.0 / (1.0 + (ERFC_T * 0.5**0.5) * jnp.abs(x))
    poly = jnp.full_like(t, 0.5 * ERFC_POLY[-1])
    for c in ERFC_POLY[-2::-1]:
        poly = poly * t + 0.5 * c
    tail = poly * t * bell
    cdf = jnp.where(x < 0, tail, 1.0 - tail)
    return x * cdf, cdf + x * bell * (1.0 / (2.0 * np.pi) ** 0.5)


def head_masks():
    lane = lax.broadcasted_iota(jnp.int32, (1, HALF), 1)
    return [jnp.where(lane // HEAD == h, 1.0, 0.0).astype(BF16) for h in range(4)]


def spread_heads(block, masks):
    return jnp.concatenate([block * m for m in masks], axis=0)


def whole(shape):
    return pl.BlockSpec(shape, lambda *_: (0,) * len(shape))


def params(n=1):
    return pltpu.CompilerParams(
        dimension_semantics=("arbitrary",) * n, vmem_limit_bytes=VMEM_LIMIT
    )


def call(name, kernel, steps, me, ins, outs, scratch):
    names = ["me", *[e[0] for e in ins], *[e[0] for e in outs], *[e[0] for e in scratch]]

    def body(*refs):
        kernel(types.SimpleNamespace(**dict(zip(names, refs, strict=True))))

    results = pl.pallas_call(
        body,
        grid_spec=pltpu.PrefetchScalarGridSpec(
            num_scalar_prefetch=1,
            grid=(steps,),
            in_specs=[e[2] or whole(e[1].shape) for e in ins],
            out_specs=[e[3] or whole(e[1]) for e in outs],
            scratch_shapes=[pltpu.VMEM(e[1], e[2]) for e in scratch],
        ),
        out_shape=[jax.ShapeDtypeStruct(e[1], e[2]) for e in outs],
        compiler_params=params(),
        name=name,
    )(me, *[e[1] for e in ins])
    return types.SimpleNamespace(**dict(zip([e[0] for e in outs], results, strict=True)))


def patch_kernel(feat_ref, out_ref, wide_ref, patch_ref):
    @pl.when(pl.program_id(0) == 0)
    def _():
        patch_ref[...] = jnp.zeros_like(patch_ref)

    wide_ref[:, 0 : 2 * GRID, :] = feat_ref[0].astype(F32)
    even = wide_ref[:, pl.ds(0, GRID, stride=2), :]
    odd = wide_ref[:, pl.ds(1, GRID, stride=2), :]
    patch_ref[:, 1 : GRID + 1, 0:CIN] = odd
    patch_ref[:, 0:GRID, CIN : 2 * CIN] = even
    patch_ref[:, 0:GRID, 2 * CIN : 3 * CIN] = odd
    both = patch_ref[...].astype(BF16).reshape(GRID, 2, COLS, PARTS)
    for par in range(2):
        out_ref[0, par] = both[:, par].reshape(TOK, PARTS)


def make_patches(features):
    slots = features.shape[0]
    return pl.pallas_call(
        patch_kernel,
        grid=(slots,),
        in_specs=[pl.BlockSpec((1, 2 * GRID, 2 * GRID, CIN), lambda i: (i, 0, 0, 0))],
        out_specs=pl.BlockSpec((1, 2, TOK, PARTS), lambda i: (i, 0, 0, 0)),
        out_shape=jax.ShapeDtypeStruct((slots, 2, TOK, PARTS), BF16),
        scratch_shapes=[
            pltpu.VMEM((2 * GRID, 32, CIN), F32),
            pltpu.VMEM((2 * GRID, COLS, PARTS), F32),
        ],
        compiler_params=params(),
        name="patches",
    )(features)


def bias_kernel(rows_ref, shift_ref, mask_ref, out_ref, flat_ref):
    def at_column(x, _):
        part = dot_nn(rows_ref[0], shift_ref[0, x], precision=PRECISE)
        flat_ref[pl.ds(x, HEADS * GRID, stride=COLS), :] = part
        return 0

    lax.fori_loop(0, COLS, at_column, 0)
    for h in range(HEADS):
        block = flat_ref[h * TOK : (h + 1) * TOK, :]
        out_ref[0, h] = jnp.where(mask_ref[0] > 0.5, block, MASKED)


def make_bias(tables):
    maps = [static_maps(layer) for layer in range(LAYERS)]
    padded = jnp.pad(tables, ((0, 0), (0, 0), (0, 3), (0, 3)))
    hots = jnp.asarray(np.stack([m[0] for m in maps]))
    rows = jnp.einsum("lpd,lhde->lhpe", hots, padded, precision=PRECISE)
    rows = rows.reshape(LAYERS, HEADS * GRID, KEYS)
    shifts = jnp.asarray(np.stack([m[1] for m in maps]))
    masks = jnp.asarray(np.stack([m[2] for m in maps]))
    return pl.pallas_call(
        bias_kernel,
        grid=(LAYERS,),
        in_specs=[
            pl.BlockSpec((1, HEADS * GRID, KEYS), lambda i: (i, 0, 0)),
            pl.BlockSpec((1, COLS, KEYS, KEYS), lambda i: (i, 0, 0, 0)),
            pl.BlockSpec((1, TOK, KEYS), lambda i: (i, 0, 0)),
        ],
        out_specs=pl.BlockSpec((1, HEADS, TOK, KEYS), lambda i: (i, 0, 0, 0)),
        out_shape=jax.ShapeDtypeStruct((LAYERS, HEADS, TOK, KEYS), F32),
        scratch_shapes=[pltpu.VMEM((HEADS * TOK, KEYS), F32)],
        compiler_params=params(),
        name="bias",
    )(rows, shifts, masks)


def table_grad_kernel(grad_ref, shift_ref, out_ref):
    def at_column(x, total):
        part = grad_ref[0, pl.ds(x, HEADS * GRID, stride=COLS), :]
        return total + dot_nt(part, shift_ref[0, x], precision=PRECISE)

    out_ref[0] = lax.fori_loop(0, COLS, at_column, jnp.zeros((HEADS * GRID, KEYS), F32))


def table_grad(bias_grad, layer):
    rows_hot, shifts, _ = static_maps(layer)
    rows = pl.pallas_call(
        table_grad_kernel,
        grid=(1,),
        in_specs=[whole((1, HEADS * TOK, KEYS)), whole((1, COLS, KEYS, KEYS))],
        out_specs=whole((1, HEADS * GRID, KEYS)),
        out_shape=jax.ShapeDtypeStruct((1, HEADS * GRID, KEYS), F32),
        compiler_params=params(),
        name="table_grad",
    )(bias_grad.reshape(1, HEADS * TOK, KEYS), jnp.asarray(shifts)[None])
    out = jnp.einsum(
        "pd,hpe->hde", jnp.asarray(rows_hot), rows.reshape(HEADS, GRID * 8, 16), precision=PRECISE
    )
    return out[:, : 2 * KER - 1, : 2 * KER - 1]


def pieces_of(shards, group):
    narrow, wide = D // shards, FF // shards
    sizes = [("qkv", narrow, 3), ("proj", narrow, 1), ("up", narrow, 3), ("down", wide, 1)]
    if group == 0:
        sizes = [("conv", 9 * CIN // shards, 1)] + sizes
    else:
        sizes = sizes + [("head", narrow, 4)]
    out, at = {}, 0
    for name, rows, blocks in sizes:
        out[name] = (at, rows, blocks)
        at += rows * blocks
    return out, at


def pack(parts):
    out = []
    for part in parts:
        if part.shape[1] == CLASSES:
            part = jnp.pad(part, ((0, 0), (0, CPAD - CLASSES)))
        out += [part[:, c : c + D] for c in range(0, part.shape[1], D)]
    return jnp.concatenate(out, axis=0)


SPLIT = (240, 224)
SHARDS = 8


def unpack_weights(me, sources, targets, group):
    layout, _ = pieces_of(SHARDS, group)
    for ref, low, high, offsets in sources:
        for p, offset in enumerate(offsets):
            owner = me ^ offset
            for name, target in targets.items():
                at, rows, blocks = layout[name]
                if not low <= at < high:
                    continue
                place = pl.ds(pl.multiple_of(owner * rows, 16), rows)
                for c in range(blocks):
                    first = at - low + c * rows
                    target[place, c * D : (c + 1) * D] = ref[p, first : first + rows, :]


def attend(layer, item, joined_ref, bias_ref, probs_ref, mixed_ref):
    masks = head_masks()
    base = item * TOK
    for q0, nq, k0 in GROUPS[layer]:
        for hf in range(2):
            lanes = slice(hf * HALF, (hf + 1) * HALF)
            at = lambda which: slice(which * D + hf * HALF, which * D + (hf + 1) * HALF)
            query = joined_ref[base + q0 : base + q0 + nq, at(0)]
            keys = spread_heads(joined_ref[base + k0 : base + k0 + KEYS, at(1)], masks)
            values = spread_heads(joined_ref[base + k0 : base + k0 + KEYS, at(2)], masks)
            scores = dot_nt(query, keys)
            low = []
            for h in range(4):
                head = hf * 4 + h
                s = scores[:, h * KEYS : (h + 1) * KEYS] * SCALE + bias_ref[0, head, q0 : q0 + nq, :]
                e = jnp.exp(s - jnp.max(s, axis=-1, keepdims=True))
                p = e * (1.0 / jnp.sum(e, axis=-1, keepdims=True))
                probs_ref[item, q0 : q0 + nq, head * KEYS : (head + 1) * KEYS] = p
                low.append(p.astype(BF16))
            mixed = dot_nn(jnp.concatenate(low, axis=1), values)
            mixed_ref[base + q0 : base + q0 + nq, lanes] = mixed.astype(BF16)


def layer_forward(layer, hidden, vec_ref, weights, bias_ref, outs, items):
    joined_ref, probs_ref, mixed_ref, after_ref, slope_ref, active_ref = outs
    vec = lambda i: vec_ref[i : i + 1, :]
    xhat, _ = norm_stats(hidden)
    normed = (xhat * vec(0) + vec(1)).astype(BF16)
    for c in range(3):
        part = dot_nn(normed, weights["qkv"][:, c * D : (c + 1) * D])
        if c != 1:
            part = part + vec(2 if c == 0 else 3)
        joined_ref[:, c * D : (c + 1) * D] = part.astype(BF16)
    for item in range(items):
        attend(layer, item, joined_ref, bias_ref, probs_ref, mixed_ref)
    after = hidden + (dot_nn(mixed_ref[...], weights["proj"][...]) + vec(4))
    after_ref[...] = after
    xhat, _ = norm_stats(after)
    normed = (xhat * vec(5) + vec(6)).astype(BF16)
    total = None
    for c in range(3):
        pre = dot_nn(normed, weights["up"][:, c * D : (c + 1) * D]) + vec(8 + c)
        active, slope = gelu_parts(pre)
        active = active.astype(BF16)
        slope_ref[:, c * D : (c + 1) * D] = slope
        active_ref[:, c * D : (c + 1) * D] = active
        part = dot_nn(active, weights["down"][c * D : (c + 1) * D, :])
        total = part if total is None else total + part
    return after + (total + vec(7))


def conv_taps(patch_ref, item):
    odd = patch_ref[item, 1]
    up = jnp.concatenate([jnp.zeros((COLS, PARTS), BF16), odd[: TOK - COLS]], axis=0)
    return up, patch_ref[item, 0], odd


CACHE = (
    ("joined", 3 * D, BF16),
    ("probs", None, F32),
    ("mixed", D, BF16),
    ("after", D, F32),
    ("slope", FF, F32),
    ("active", FF, BF16),
)
MATRICES = (("qkv", (D, FF)), ("proj", (D, D)), ("up", (D, FF)), ("down", (FF, D)))
MATRIX_NAMES = [m[0] for m in MATRICES]


def token_spec(items, width=D):
    return pl.BlockSpec((items * TOK, width), lambda i, *_: (i, 0))


def cache_entries(slots, items):
    out = []
    for name, width, dtype in CACHE:
        if width is None:
            spec = pl.BlockSpec((items, TOK, HEADS * KEYS), lambda i, *_: (i, 0, 0))
            out.append((name, (slots, TOK, HEADS * KEYS), dtype, spec))
        else:
            out.append((name, (slots * TOK, width), dtype, token_spec(items, width)))
    return out


def caches_of(r):
    return tuple(getattr(r, entry[0]) for entry in CACHE)


def bias_spec(layer):
    return pl.BlockSpec((1, HEADS, TOK, KEYS), lambda i, *_: (layer, 0, 0, 0))


def patch_spec(items):
    return pl.BlockSpec((items, 2, TOK, PARTS), lambda i, *_: (i, 0, 0, 0))


def source_entries(sources):
    return [(f"source{i}", array, None) for i, (array, *_) in enumerate(sources)]


def sources_of(r, sources):
    return [(getattr(r, f"source{i}"), *entry[1:]) for i, entry in enumerate(sources)]


def forward_zero(me, patches, sources, vec, conv_vec, bias, items):
    slots = patches.shape[0]

    def kernel(r):
        names = ["conv_w", *MATRIX_NAMES]
        weights = {n: getattr(r, n) for n in names}

        @pl.when(pl.program_id(0) == 0)
        def _():
            targets = {n.removesuffix("_w"): ref for n, ref in weights.items()}
            unpack_weights(r.me[0], sources_of(r, sources), targets, 0)

        for item in range(items):
            taps = conv_taps(r.patch, item)
            total = None
            for a in range(3):
                part = dot_nn(taps[a], r.conv_w[a * PARTS : (a + 1) * PARTS, :])
                total = part if total is None else total + part
            r.conv[item * TOK : (item + 1) * TOK, :] = total + r.conv_vec[0:1, :]
        xhat, _ = norm_stats(r.conv[...])
        hidden = xhat * r.conv_vec[1:2, :] + r.conv_vec[2:3, :]
        hidden = layer_forward(0, hidden, r.vec, weights, r.bias, caches_of(r), items)
        for item in range(items):
            for place, row in enumerate(row_order(1)):
                r.hidden[item * TOK + place * COLS : item * TOK + (place + 1) * COLS, :] = hidden[
                    item * TOK + row * COLS : item * TOK + (row + 1) * COLS
                ]

    return call(
        "forward_zero",
        kernel,
        slots // items,
        me,
        [
            ("patch", patches, patch_spec(items)),
            *source_entries(sources),
            ("vec", vec, None),
            ("conv_vec", conv_vec, None),
            ("bias", bias, bias_spec(0)),
        ],
        [
            ("hidden", (slots * TOK, D), F32, token_spec(items)),
            ("conv", (slots * TOK, D), F32, token_spec(items)),
            *cache_entries(slots, items),
            *[(n, shape, BF16, None) for n, shape in MATRICES],
        ],
        [("conv_w", (9 * CIN, D), BF16)],
    )


def real_cells():
    place = lax.broadcasted_iota(jnp.int32, (TOK, 1), 0)
    return jnp.where(place % COLS < GRID, 1.0, 0.0)


def classify(r):
    pooled = r.pooled[...].astype(BF16)
    logits = dot_nn(pooled, r.head[...]) + r.head_bias[...]
    peak = jnp.max(logits, axis=-1, keepdims=True)
    log_total = peak + jnp.log(jnp.sum(jnp.exp(logits - peak), axis=-1, keepdims=True))
    lane = lax.broadcasted_iota(jnp.int32, logits.shape, 1)
    onehot = jnp.where(r.label[:, 0:1] == lane, 1.0, 0.0)
    picked = jnp.sum(onehot * logits, axis=-1, keepdims=True)
    live = r.live[:, 0:1]
    r.loss[...] = jnp.broadcast_to(col_sum(live * (log_total - picked)), r.loss.shape)
    d_logits = (jnp.exp(logits - log_total) - onehot) * (r.inverse[:, 0:1] * live)
    d_logits = jnp.where(lane < CLASSES, d_logits, 0.0).astype(BF16)
    r.head_grad[...] = dot_tn(pooled, d_logits)
    r.head_bias_grad[...] = col_sum(d_logits.astype(F32))
    r.d_pooled[...] = dot_nt(d_logits, r.head[...]) * (1.0 / PIX)


def forward_one(me, hidden, sources, vec, final, bias, head_bias, label, live, inverse, items):
    slots = hidden.shape[0] // TOK
    rows = label.shape[0]

    def kernel(r):
        weights = {n: getattr(r, n) for n in MATRIX_NAMES}
        step = pl.program_id(0)

        @pl.when(step == 0)
        def _():
            unpack_weights(r.me[0], sources_of(r, sources), weights | dict(head=r.head), 1)
            r.pooled[...] = jnp.zeros_like(r.pooled)

        out = layer_forward(1, r.hidden[...], r.vec, weights, r.bias, caches_of(r), items)
        r.out[...] = out
        xhat, _ = norm_stats(out)
        normed = xhat * r.final[0:1, :] + r.final[1:2, :]
        real = real_cells()
        for item in range(items):
            mean = col_sum(normed[item * TOK : (item + 1) * TOK] * real) * (1.0 / PIX)
            r.pooled[pl.ds(step * items + item, 1), :] = mean

        @pl.when(step == pl.num_programs(0) - 1)
        def _():
            classify(r)

    return call(
        "forward_one",
        kernel,
        slots // items,
        me,
        [
            ("hidden", hidden, token_spec(items)),
            *source_entries(sources),
            ("vec", vec, None),
            ("final", final, None),
            ("bias", bias, bias_spec(1)),
            ("head_bias", head_bias, None),
            ("label", label, None),
            ("live", live, None),
            ("inverse", inverse, None),
        ],
        [
            ("out", (slots * TOK, D), F32, token_spec(items)),
            *cache_entries(slots, items),
            *[(n, shape, BF16, None) for n, shape in MATRICES],
            ("loss", (8, 128), F32, None),
            ("head_grad", (D, CPAD), F32, None),
            ("head_bias_grad", (1, CPAD), F32, None),
            ("d_pooled", (rows, D), F32, None),
        ],
        [("head", (D, CPAD), BF16), ("pooled", (rows, D), F32)],
    )


def attend_back(layer, item, first, joined_ref, probs_ref, dmix_ref, djoin_ref, dkv_ref, bgrad_ref):
    masks = head_masks()
    base = item * TOK
    dkv_ref[...] = jnp.zeros_like(dkv_ref)
    for q0, nq, k0 in GROUPS[layer]:
        qrows = slice(base + q0, base + q0 + nq)
        krows = slice(base + k0, base + k0 + KEYS)
        for hf in range(2):
            lanes = slice(hf * HALF, (hf + 1) * HALF)
            at = lambda which: slice(which * D + hf * HALF, which * D + (hf + 1) * HALF)
            query = spread_heads(joined_ref[qrows, at(0)], masks)
            keys = spread_heads(joined_ref[krows, at(1)], masks)
            values = spread_heads(joined_ref[krows, at(2)], masks)
            d_mix = dmix_ref[qrows, lanes]
            d_probs = dot_nt(d_mix, values)
            d_low, p_low = [], []
            for h in range(4):
                head = hf * 4 + h
                p = probs_ref[item, q0 : q0 + nq, head * KEYS : (head + 1) * KEYS]
                dp = d_probs[:, h * KEYS : (h + 1) * KEYS]
                ds = (p * (dp - jnp.sum(dp * p, axis=-1, keepdims=True))).astype(BF16)
                place = slice(head * TOK + q0, head * TOK + q0 + nq)
                bgrad_ref[place, :] += ds.astype(F32)
                d_low.append(ds)
                p_low.append(p.astype(BF16))
            d_query = dot_nn(jnp.concatenate(d_low, axis=1), keys) * SCALE
            djoin_ref[qrows, at(0)] = d_query.astype(BF16)
            d_keys = dot_tn(jnp.concatenate(d_low, axis=0), query)
            d_values = dot_tn(jnp.concatenate(p_low, axis=0), spread_heads(d_mix, masks))
            dkv_ref[k0 : k0 + KEYS, lanes] += d_keys
            dkv_ref[k0 : k0 + KEYS, D + hf * HALF : D + (hf + 1) * HALF] += d_values
    djoin_ref[base : base + TOK, D : 2 * D] = (dkv_ref[:, 0:D] * SCALE).astype(BF16)
    djoin_ref[base : base + TOK, 2 * D : 3 * D] = dkv_ref[:, D : 2 * D].astype(BF16)


def layer_backward(layer, d_out, hidden, vec_ref, weights, caches, work, grads, vgrad_ref, bgrad_ref, items):
    joined_ref, probs_ref, mixed_ref, after_ref, slope_ref, active_ref = caches
    dmix_ref, djoin_ref, dkv_ref = work
    vec = lambda i: vec_ref[i : i + 1, :]

    def add(row, value):
        vgrad_ref[row : row + 1, :] += value

    d_branch = d_out.astype(BF16)
    add(7, col_sum(d_branch.astype(F32)))
    xhat, rstd = norm_stats(after_ref[...])
    normed = (xhat * vec(5) + vec(6)).astype(BF16)
    d_normed = None
    for c in range(3):
        cols = slice(c * D, (c + 1) * D)
        grads["down"][:, cols] += dot_tn(d_branch, active_ref[:, cols])
        d_active = dot_nt(d_branch, weights["down"][cols, :])
        d_pre = (d_active * slope_ref[:, cols]).astype(BF16)
        add(8 + c, col_sum(d_pre.astype(F32)))
        grads["up"][:, cols] += dot_tn(normed, d_pre)
        part = dot_nt(d_pre, weights["up"][:, cols])
        d_normed = part if d_normed is None else d_normed + part
    add(5, col_sum(d_normed * xhat))
    add(6, col_sum(d_normed))
    d_after = d_out + norm_back(d_normed, xhat, rstd, vec(5))
    d_proj = d_after.astype(BF16)
    add(4, col_sum(d_proj.astype(F32)))
    grads["proj"][...] += dot_tn(mixed_ref[...], d_proj)
    dmix_ref[...] = dot_nt(d_proj, weights["proj"][...]).astype(BF16)
    for item in range(items):
        attend_back(layer, item, item == 0, joined_ref, probs_ref, dmix_ref, djoin_ref, dkv_ref, bgrad_ref)
    add(2, col_sum(djoin_ref[:, 0:D].astype(F32)))
    add(3, col_sum(djoin_ref[:, 2 * D : 3 * D].astype(F32)))
    xhat, rstd = norm_stats(hidden)
    normed = (xhat * vec(0) + vec(1)).astype(BF16)
    d_normed = None
    for c in range(3):
        cols = slice(c * D, (c + 1) * D)
        grads["qkv"][:, cols] += dot_tn(normed, djoin_ref[:, cols])
        part = dot_nt(djoin_ref[:, cols], weights["qkv"][:, cols])
        d_normed = part if d_normed is None else d_normed + part
    add(0, col_sum(d_normed * xhat))
    add(1, col_sum(d_normed))
    return d_after + norm_back(d_normed, xhat, rstd, vec(0))


def split_two(x):
    high = x.astype(BF16)
    return high, (x - high.astype(F32)).astype(BF16)


def stack_three(x):
    high = x.astype(BF16).astype(F32)
    mid = (x - high).astype(BF16).astype(F32)
    return jnp.concatenate([high, mid, x - high - mid], axis=0).astype(BF16)


def wide_dot(dot, rows, matrix):
    stacked = stack_three(rows)
    high, low = split_two(matrix)
    out = dot(stacked, high) + dot(stacked, low)
    return out[0:RANK] + out[RANK : 2 * RANK] + out[2 * RANK : 3 * RANK]


def block_of(whole_ref, entry, c):
    at, rows, _ = entry
    return jnp.concatenate(
        [whole_ref[s, at + c * rows : at + (c + 1) * rows, :] for s in range(SHARDS)], axis=0
    )


def finish_grads(r, group, grads):
    layout, _ = pieces_of(SHARDS, group)
    me = r.me[0]
    for name, (at, rows, blocks) in layout.items():
        matrix = grads[name]
        if name in ("down", "conv"):
            matrix = jnp.transpose(matrix[...])
        for s in range(SHARDS):
            for c in range(blocks):
                piece = matrix[s * rows : (s + 1) * rows, c * D : (c + 1) * D]
                r.whole[s, at + c * rows : at + (c + 1) * rows, :] = piece
    r.whole[me] += r.err[...]
    r.own[...] = r.whole[me]
    for j in range(1, SHARDS):
        getattr(r, f"sent{j}")[...] = r.whole[me ^ j].astype(BF16)
    at_lane, at_col = 0, 0
    for name, entry in layout.items():
        total = None
        for c in range(entry[2]):
            part = wide_dot(dot_nt, r.fac[:, at_col : at_col + D], block_of(r.whole, entry, c))
            total = part if total is None else total + part
            at_col += D
        lanes = entry[1] * SHARDS
        r.left[:, at_lane : at_lane + lanes] = total
        at_lane += lanes


def left_lanes(group):
    return sum(rows * SHARDS for _, rows, _ in pieces_of(SHARDS, group)[0].values())


def right_lanes(group):
    return sum(blocks * D for _, _, blocks in pieces_of(SHARDS, group)[0].values())


def backward_outs(group):
    rows = pieces_of(SHARDS, group)[1]
    return [
        ("vgrad", (16, D), F32, None),
        ("bgrad", (HEADS * TOK, KEYS), F32, None),
        ("whole", (SHARDS, rows, D), F32, None),
        ("own", (rows, D), F32, None),
        *[(f"sent{j}", (rows, D), BF16, None) for j in range(1, SHARDS)],
        ("left", (RANK, left_lanes(group)), F32, None),
    ]


def backward_scratch(items):
    return [
        ("d_mixed", (items * TOK, D), BF16),
        ("d_joined", (items * TOK, 3 * D), BF16),
        ("d_keys", (TOK, 2 * D), F32),
        ("g_qkv", (D, FF), F32),
        ("g_proj", (D, D), F32),
        ("g_up", (D, FF), F32),
        ("g_down", (D, FF), F32),
    ]


def start_backward(r, grads):
    r.vgrad[...] = jnp.zeros_like(r.vgrad)
    r.bgrad[...] = jnp.zeros_like(r.bgrad)
    for ref in grads.values():
        ref[...] = jnp.zeros_like(ref)


def cache_inputs(caches, slots, items):
    return [(e[0], getattr(caches, e[0]), e[3]) for e in cache_entries(slots, items)]


def matrix_inputs(caches):
    return [(n, getattr(caches, n), None) for n in MATRIX_NAMES]


def backward_one(me, hidden, forward, vec, final, err, fac, items):
    slots = hidden.shape[0] // TOK

    def kernel(r):
        weights = {n: getattr(r, n) for n in MATRIX_NAMES}
        grads = {n: getattr(r, "g_" + n) for n in MATRIX_NAMES}
        step = pl.program_id(0)

        @pl.when(step == 0)
        def _():
            start_backward(r, grads)

        real = real_cells()
        d_final = jnp.concatenate(
            [real * r.d_pooled[pl.ds(step * items + item, 1), :] for item in range(items)], axis=0
        )
        xhat, rstd = norm_stats(r.out[...])
        r.vgrad[11:12, :] += col_sum(d_final * xhat)
        r.vgrad[12:13, :] += col_sum(d_final)
        d_out = norm_back(d_final, xhat, rstd, r.final[0:1, :])
        work = (r.d_mixed, r.d_joined, r.d_keys)
        r.d_hidden[...] = layer_backward(
            1, d_out, r.hidden[...], r.vec, weights, caches_of(r), work, grads, r.vgrad, r.bgrad, items
        )

        @pl.when(step == pl.num_programs(0) - 1)
        def _():
            finish_grads(r, 1, grads | dict(head=r.head_grad))

    return call(
        "backward_one",
        kernel,
        slots // items,
        me,
        [
            ("out", forward.out, token_spec(items)),
            ("d_pooled", forward.d_pooled, None),
            ("hidden", hidden, token_spec(items)),
            *matrix_inputs(forward),
            ("vec", vec, None),
            ("final", final, None),
            *cache_inputs(forward, slots, items),
            ("head_grad", forward.head_grad, None),
            ("err", err, None),
            ("fac", fac, None),
        ],
        [("d_hidden", hidden.shape, F32, token_spec(items)), *backward_outs(1)],
        backward_scratch(items),
    )


def backward_zero(me, d_hidden, forward, patches, vec, conv_vec, err, fac, items):
    slots = patches.shape[0]

    def kernel(r):
        weights = {n: getattr(r, n) for n in MATRIX_NAMES}
        grads = {n: getattr(r, "g_" + n) for n in [*MATRIX_NAMES, "conv"]}
        step = pl.program_id(0)

        @pl.when(step == 0)
        def _():
            start_backward(r, grads)

        order = row_order(1)
        rows = []
        for item in range(items):
            for row in range(GRID):
                first = item * TOK + order.index(row) * COLS
                rows.append(r.d_hidden[first : first + COLS, :])
        d_out = jnp.concatenate(rows, axis=0)
        conv_hat, conv_rstd = norm_stats(r.conv[...])
        gain = r.conv_vec[1:2, :]
        hidden = conv_hat * gain + r.conv_vec[2:3, :]
        work = (r.d_mixed, r.d_joined, r.d_keys)
        d_conv = layer_backward(
            0, d_out, hidden, r.vec, weights, caches_of(r), work, grads, r.vgrad, r.bgrad, items
        )
        r.vgrad[12:13, :] += col_sum(d_conv * conv_hat)
        r.vgrad[13:14, :] += col_sum(d_conv)
        d_conv = norm_back(d_conv, conv_hat, conv_rstd, gain).astype(BF16)
        r.vgrad[11:12, :] += col_sum(d_conv.astype(F32))
        for item in range(items):
            taps = conv_taps(r.patch, item)
            part = d_conv[item * TOK : (item + 1) * TOK]
            for a in range(3):
                grads["conv"][:, a * PARTS : (a + 1) * PARTS] += dot_tn(part, taps[a])

        @pl.when(step == pl.num_programs(0) - 1)
        def _():
            finish_grads(r, 0, grads)

    return call(
        "backward_zero",
        kernel,
        slots // items,
        me,
        [
            ("d_hidden", d_hidden, token_spec(items)),
            ("conv", forward.conv, token_spec(items)),
            ("patch", patches, patch_spec(items)),
            *matrix_inputs(forward),
            ("vec", vec, None),
            ("conv_vec", conv_vec, None),
            *cache_inputs(forward, slots, items),
            ("err", err, None),
            ("fac", fac, None),
        ],
        backward_outs(0),
        [*backward_scratch(items), ("g_conv", (D, 9 * CIN), F32)],
    )


def inverse_cholesky(gram):
    row = lax.broadcasted_iota(jnp.int32, (1, RANK, 2 * RANK), 1)
    lane = lax.broadcasted_iota(jnp.int32, (1, RANK, 2 * RANK), 2)
    eye = jnp.broadcast_to(jnp.where(lane == row + RANK, 1.0, 0.0), (gram.shape[0], RANK, 2 * RANK))
    work = jnp.concatenate([gram, jnp.zeros_like(gram)], axis=2) + eye
    for k in range(RANK):
        scale = 1.0 / jnp.sqrt(work[:, k : k + 1, k : k + 1])
        pivot = work[:, k : k + 1, :] * scale
        column = work[:, :, k : k + 1] * scale
        work = jnp.where(row > k, work - column * pivot, jnp.where(row == k, pivot, work))
    return work[:, :, RANK : 2 * RANK]


def basis_lanes(group):
    return sum(rows for _, rows, _ in pieces_of(SHARDS, group)[0].values())


def right_factors(me, left, whole_zero, whole_one):
    def kernel(r):
        groups = (r.whole0, r.whole1)
        entries, at = [], 0
        for group in range(2):
            for entry in pieces_of(SHARDS, group)[0].values():
                entries.append((group, entry, at))
                at += entry[1] * SHARDS
        lefts = [r.left[:, at : at + entry[1] * SHARDS] for _, entry, at in entries]
        grams = jnp.stack([dot_nt(x, x, precision=PRECISE) for x in lefts])
        inverses = inverse_cholesky(grams)
        at_col = 0
        rows_of = [[], []]
        for i, (group, entry, _) in enumerate(entries):
            basis = dot_nn(inverses[i], lefts[i], precision=PRECISE)
            rows_of[group].append((basis, entry[1]))
            for c in range(entry[2]):
                r.right[:, at_col : at_col + D] = wide_dot(dot_nn, basis, block_of(groups[group], entry, c))
                at_col += D
        for group, out in ((0, r.basis0), (1, r.basis1)):
            for s in range(SHARDS):
                at = 0
                for basis, rows in rows_of[group]:
                    out[s, :, at : at + rows] = basis[:, s * rows : (s + 1) * rows]
                    at += rows

    return call(
        "right_factors",
        kernel,
        1,
        me,
        [("left", left, None), ("whole0", whole_zero, None), ("whole1", whole_one, None)],
        [
            ("right", (RANK, right_lanes(0) + right_lanes(1)), F32, None),
            ("basis0", (SHARDS, RANK, basis_lanes(0)), F32, None),
            ("basis1", (SHARDS, RANK, basis_lanes(1)), F32, None),
        ],
        [],
    )


def six_products(x, other):
    high = x.astype(BF16).astype(F32)
    mid = (x - high).astype(BF16).astype(F32)
    low = x - high - mid
    terms = [high, mid, high, mid, low, high] if other else [high, high, mid, mid, high, low]
    return jnp.concatenate(terms, axis=0).astype(BF16)


UPDATED = (("conv", 0), ("qkv", 1), ("proj", 1), ("up", 1), ("down", 1), ("head", 0))


def apply_update(me, weights, moms, right_mine, right_all, factors, own, received):
    def kernel(r):
        at_col = 0
        for group in range(2):
            total = getattr(r, f"own{group}")[...]
            for i in range(len(received[group])):
                total = total + getattr(r, f"got{group}_{i}")[...].astype(F32)
            basis = getattr(r, f"basis{group}")
            at_row = 0
            for name, (at, rows, blocks) in pieces_of(SHARDS, group)[0].items():
                left = six_products(basis[0, :, at_row : at_row + rows], False)
                at_row += rows
                whole_matrix = name in ("conv", "head")
                for c in range(blocks):
                    width = min(D, (CLASSES if name == "head" else blocks * D) - c * D)
                    cols = slice(c * D, c * D + width)
                    place = (slice(None), cols) if whole_matrix else (group, slice(None), cols)
                    err_place = (0, slice(None), cols) if whole_matrix else (0, group, slice(None), cols)
                    right = slice(at_col, at_col + D)
                    at_col += D
                    mine = dot_tn(left, six_products(r.right_mine[:, right], True))
                    every = dot_tn(left, six_products(r.right_all[:, right], True))
                    merged = total[at + c * rows : at + (c + 1) * rows]
                    getattr(r, "err_" + name)[err_place] = (merged - mine)[:, :width]
                    mom = MOMENTUM * getattr(r, "mom_" + name)[place] + every[:, :width]
                    getattr(r, "new_mom_" + name)[place] = mom
                    getattr(r, "new_" + name)[place] = getattr(r, "w_" + name)[place] - LEARN_RATE * mom

    names = [n for n, _ in UPDATED]
    mine_spec = lambda x: pl.BlockSpec((1,) + x.shape[1:], lambda i, m: (m[0], 0, 0))
    err_shape = lambda w: (1,) + w.shape
    return call(
        "apply_update",
        kernel,
        1,
        me,
        [
            *[("w_" + n, w, None) for n, w in zip(names, weights)],
            *[("mom_" + n, m, None) for n, m in zip(names, moms)],
            ("right_mine", right_mine, None),
            ("right_all", right_all, None),
            ("basis0", factors[0], mine_spec(factors[0])),
            ("basis1", factors[1], mine_spec(factors[1])),
            ("own0", own[0], None),
            ("own1", own[1], None),
            *[(f"got{g}_{i}", x, None) for g in range(2) for i, x in enumerate(received[g])],
        ],
        [
            *[("new_" + n, w.shape, F32, None) for n, w in zip(names, weights)],
            *[("new_mom_" + n, w.shape, F32, None) for n, w in zip(names, weights)],
            *[("err_" + n, err_shape(w), F32, None) for n, w in zip(names, weights)],
        ],
        [],
    )


def swap(x, offset):
    return lax.ppermute(x, "fsdp", [(i, i ^ offset) for i in range(SHARDS)])


def swap_by_core(x, even, odd):
    return lax.ppermute(x, "fsdp", [(i, i ^ (odd if i & 1 else even)) for i in range(SHARDS)])


def swap_rep(x, offset, reps):
    return lax.ppermute(x, "rep", [(i, i ^ offset) for i in range(reps)])


def gather_halves(first, second, cut, end):
    out = []
    for part, low, high, order in ((first, 0, cut, (4, 2)), (second, cut, end, (2, 4))):
        near = part[None]
        offsets = [0]
        for bit in order:
            near = jnp.concatenate([near, swap(near, bit)], axis=0)
            offsets = offsets + [o ^ bit for o in offsets]
        out.append((near, low, high, tuple(offsets)))
        out.append((swap(near, 1), low, high, tuple(o ^ 1 for o in offsets)))
    return out


def gather_direct(packed):
    end = packed.shape[0]
    out = [(packed[None], 0, end, (0,))]
    for j in range(1, SHARDS):
        out.append((swap(packed, j)[None], 0, end, (j,)))
    return out


def halves(x):
    half = x.shape[1] // 2
    core = lax.axis_index("fsdp") & 1
    first, second = x[:, :half], x[:, half:]
    return jnp.where(core == 0, first, second), jnp.where(core == 0, second, first)


def join_halves(mine, other):
    core = lax.axis_index("fsdp") & 1
    low, high = jnp.where(core == 0, mine, other), jnp.where(core == 0, other, mine)
    return jnp.concatenate([low, high], axis=-1)


def sum_replica(x):
    mine, other = halves(x)
    mine = mine + swap(other, 1)
    mine = mine + swap_by_core(mine, 2, 4)
    return mine + swap_by_core(mine, 4, 2)


def sum_replicas(x, reps):
    bit = 1
    while bit < reps:
        x = x + swap_rep(x, bit, reps)
        bit *= 2
    return x


def pad_lanes(x, lanes):
    return jnp.pad(x, ((0, 0), (0, lanes - x.shape[1])))


def table_at(layer):
    return 3 * D + layer * (11 * D + HEADS * RB)


def small_blocks(small):
    layer_vecs, tables = [], []
    for layer in range(LAYERS):
        at = table_at(layer)
        layer_vecs.append(small[at : at + 11 * D].reshape(11, D))
        tables.append(small[at + 11 * D : at + 11 * D + HEADS * RB])
    at = table_at(LAYERS)
    final = small[at : at + 2 * D].reshape(2, D)
    head_bias = jnp.pad(small[at + 2 * D :][None], ((0, 0), (0, CPAD - CLASSES)), constant_values=-1e30)
    tables = jnp.stack(tables).reshape(LAYERS, HEADS, 2 * KER - 1, 2 * KER - 1)
    return small[: 3 * D].reshape(3, D), layer_vecs, final, tables, head_bias


def small_vector(vgrads, tables, head_bias):
    parts = [vgrads[0][11:14].reshape(-1)]
    for layer in range(LAYERS):
        parts += [vgrads[layer][:11].reshape(-1), tables[layer].reshape(-1)]
    return jnp.concatenate([*parts, vgrads[1][11:13].reshape(-1), head_bias[:CLASSES]])


def group_parts(group, conv, qkv, proj, up, down, head):
    layer = [m[group] for m in (qkv, proj, up, down)]
    return [conv] + layer if group == 0 else layer + [head]


def factor_rows(group, *factors):
    out = []
    for f in group_parts(group, *factors):
        out.append(jnp.pad(f.T, ((0, 0), (0, CPAD - CLASSES))) if f.shape[0] == CLASSES else f.T)
    return jnp.concatenate(out, axis=1)


def split_right(right):
    widths = [(D, 3 * D, D, FF, D), (3 * D, D, FF, D, CPAD)]
    cut, at = [], 0
    for row in widths:
        for w in row:
            cut.append(right[:, at : at + w].T)
            at += w
    layer = [jnp.stack([cut[1 + i], cut[5 + i]]) for i in range(4)]
    return (cut[0], *layer, cut[9][:CLASSES])


def padded_rows(values, rows, fill):
    values = jnp.pad(values, (0, rows - values.shape[0]), constant_values=fill)
    return jnp.broadcast_to(values[:, None], (rows, 128))


def step(mesh, args):
    (
        features, labels, counts, tables, *rest
    ) = args
    weights, moms, errs, facs = rest[0:6], rest[6:12], rest[12:18], rest[18:24]
    small_params, small_mom = rest[24:]
    reps = mesh.shape["rep"]
    quick = mesh.shape["fsdp"] == SHARDS and reps & (reps - 1) == 0
    slots = features.shape[0]
    items = 2 if slots % 2 == 0 else 1
    rows = -(-slots // 16) * 16

    if quick:
        me = lax.axis_index("fsdp").astype(jnp.int32)[None]
        low = [w.astype(BF16) for w in weights]
        count = counts[0, 0].astype(F32)
        first = pack(group_parts(0, *low))
        cut, end = SPLIT[0], first.shape[0]
        with_count = jnp.concatenate([first[:cut], jnp.broadcast_to(count.astype(BF16), (16, D))], axis=0)
        sources0 = gather_halves(with_count, first[cut:], cut, end)
        replica_count = jnp.sum(sources0[0][0][:, cut, 0].astype(F32))
        replica_count = replica_count + jnp.sum(sources0[1][0][:, cut, 0].astype(F32))
        item_count = sum_replicas(jnp.broadcast_to(replica_count, (8, 128)), reps)[0, 0]
        second = pack(group_parts(1, *low))
        sources1 = gather_direct(second)
    else:
        me = jnp.zeros((1,), jnp.int32)
        item_count = lax.psum(counts[0, 0].astype(F32), ("rep", "fsdp"))
        sides = [lax.all_gather(w.astype(BF16), "fsdp", axis=w.ndim - 2, tiled=True) for w in weights]
        sources = []
        for group in range(2):
            parts = group_parts(group, *sides)
            shards = [pack([p.reshape(SHARDS, -1, p.shape[1])[s] for p in parts]) for s in range(SHARDS)]
            sources.append([(jnp.stack(shards), 0, shards[0].shape[0], tuple(range(SHARDS)))])
        sources0, sources1 = sources

    conv_vec, layer_vecs, final, bias_tables, head_bias = small_blocks(small_params)
    bias = make_bias(bias_tables)
    patches = make_patches(features)
    zero = forward_zero(me, patches, sources0, layer_vecs[0], conv_vec, bias, items)
    live = (jnp.arange(slots, dtype=jnp.int32) < counts[0, 0]).astype(F32)
    one = forward_one(
        me,
        zero.hidden,
        sources1,
        layer_vecs[1],
        final,
        bias,
        head_bias,
        padded_rows(labels, rows, -1),
        padded_rows(live, rows, 0.0),
        jnp.broadcast_to(1.0 / item_count, (rows, 128)),
        items,
    )
    fac_rows = [factor_rows(group, *facs) for group in range(2)]
    if quick:
        err = [e[0] for e in errs]
        packed_err = [pack(group_parts(group, *err)) for group in range(2)]
    else:
        packed_err = [jnp.zeros((pieces_of(SHARDS, group)[1], D), F32) for group in range(2)]
    back_one = backward_one(me, zero.hidden, one, layer_vecs[1], final, packed_err[1], fac_rows[1], items)
    back_zero = backward_zero(
        me, back_one.d_hidden, zero, patches, layer_vecs[0], conv_vec, packed_err[0], fac_rows[0], items
    )
    tables_grad = [table_grad(back_zero.bgrad, 0), table_grad(back_one.bgrad, 1)]
    if not quick:
        grads = [whole_matrices(group, b.whole) for group, b in ((0, back_zero), (1, back_one))]
        small = small_vector((back_zero.vgrad, back_one.vgrad), tables_grad, one.head_bias_grad[0])
        loss = lax.psum(one.loss[0, 0], ("rep", "fsdp"))
        return (loss, item_count, *general_tail(grads, weights, moms, errs, facs, small, small_params, small_mom))

    received = []
    for group, back in ((0, back_zero), (1, back_one)):
        received.append([swap(getattr(back, f"sent{j}"), j) for j in range(1, SHARDS)])
    left = jnp.concatenate([back_zero.left, back_one.left], axis=1)
    lanes = left.shape[1]
    left = sum_replicas(sum_replica(pad_lanes(left, -(-lanes // 256) * 256)), reps)
    left = join_halves(left, swap(left, 1))[:, :lanes]
    factors = right_factors(me, left, back_zero.whole, back_one.whole)
    payload = jnp.concatenate(
        [
            factors.right,
            back_zero.vgrad.reshape(8, 512),
            back_one.vgrad.reshape(8, 512),
            one.head_bias_grad.reshape(8, 128),
            pad_lanes(tables_grad[0].reshape(HEADS, RB), 256),
            pad_lanes(tables_grad[1].reshape(HEADS, RB), 256),
            one.loss,
        ],
        axis=1,
    )
    mine = sum_replica(payload)
    every = sum_replicas(mine, reps)
    both = jnp.stack([mine, every])
    both = join_halves(both, swap(both, 1))
    width = factors.right.shape[1]
    right_mine, summed = both[0, :, :width], both[1]
    right_all = summed[:, :width]
    updated = apply_update(
        me,
        weights,
        moms,
        right_mine,
        right_all,
        (factors.basis0, factors.basis1),
        (back_zero.own, back_one.own),
        received,
    )
    vgrads = [summed[:, width + 512 * i : width + 512 * (i + 1)].reshape(16, D) for i in range(2)]
    at = width + 1024
    head_bias_grad = summed[:, at : at + 128].reshape(-1)
    table_sums = [summed[:, at + 128 + 256 * i : at + 128 + 256 * i + RB] for i in range(2)]
    loss = summed[0, at + 640]
    new_small_mom = MOMENTUM * small_mom + small_vector(vgrads, table_sums, head_bias_grad)
    names = [n for n, _ in UPDATED]
    return (
        loss,
        item_count,
        *[getattr(updated, "new_" + n) for n in names],
        *[getattr(updated, "new_mom_" + n) for n in names],
        *[getattr(updated, "err_" + n) for n in names],
        *split_right(right_all),
        small_params - SMALL_RATE * new_small_mom,
        new_small_mom,
    )


def whole_matrices(group, packed):
    out = {}
    for name, (at, rows, blocks) in pieces_of(SHARDS, group)[0].items():
        cols = [packed[:, at + c * rows : at + (c + 1) * rows, :].reshape(SHARDS * rows, D) for c in range(blocks)]
        out[name] = jnp.concatenate(cols, axis=1)
    return out


def orthonormal(product, gram_mat):
    lower_tri = jnp.linalg.cholesky(gram_mat)
    return jnp.swapaxes(
        jax.scipy.linalg.solve_triangular(lower_tri, jnp.swapaxes(product, 1, 2), lower=True), 1, 2
    )


def general_tail(grads, weights, moms, errs, facs, small, small_params, small_mom):
    layer = [jnp.stack([grads[g][n] for g in range(2)]) for n in MATRIX_NAMES]
    wholes = [grads[0]["conv"][None], *layer, grads[1]["head"][None, :, :CLASSES]]
    lift = lambda xs: [xs[0][None], *xs[1:5], xs[5][None]]
    weights, moms, facs = lift(weights), lift(moms), lift(facs)
    errors = [errs[0], *[e[0] for e in errs[1:5]], errs[5]]
    merged = [
        lax.psum_scatter(g, "fsdp", scatter_dimension=1, tiled=True) + e for g, e in zip(wholes, errors)
    ]
    lefts = lax.psum(
        [jnp.einsum("bio,bok->bik", m, f, precision=PRECISE) for m, f in zip(merged, facs)], "rep"
    )
    grams = lax.psum([jnp.einsum("bik,bil->bkl", p, p, precision=PRECISE) for p in lefts], "fsdp")
    bases = [orthonormal(p, g) for p, g in zip(lefts, grams)]
    local = [jnp.einsum("bio,bik->bok", m, b, precision=PRECISE) for m, b in zip(merged, bases)]
    mine = lax.psum([*local, small], "fsdp")
    every = lax.psum(mine, "rep")
    product = lambda b, q: jnp.einsum("bik,bok->bio", b, q, precision=PRECISE)
    new_errs = [m - product(b, q) for m, b, q in zip(merged, bases, mine)]
    new_moms = [MOMENTUM * m + product(b, q) for m, b, q in zip(moms, bases, every)]
    new_weights = [w - LEARN_RATE * m for w, m in zip(weights, new_moms)]
    drop = lambda xs: [xs[0][0], *xs[1:5], xs[5][0]]
    new_small_mom = MOMENTUM * small_mom + every[6]
    return (
        *drop(new_weights),
        *drop(new_moms),
        new_errs[0],
        *[e[None] for e in new_errs[1:5]],
        new_errs[5],
        *drop(every[:6]),
        small_params - SMALL_RATE * new_small_mom,
        new_small_mom,
    )


def solution(mesh):
    rows, mids = P("fsdp", None), P(None, "fsdp", None)
    matrices = (rows, mids, mids, mids, mids, rows)
    errors = (
        P("rep", "fsdp", None),
        *[P("rep", None, "fsdp", None)] * 4,
        P("rep", "fsdp", None),
    )
    return jax.shard_map(
        lambda *args: step(mesh, args),
        mesh=mesh,
        in_specs=(
            P(("rep", "fsdp"), None, None, None),
            P(("rep", "fsdp")),
            P("rep", "fsdp"),
            P(),
            *matrices,
            *matrices,
            *errors,
            *[P()] * 8,
        ),
        out_specs=(P(), P(), *matrices, *matrices, *errors, *[P()] * 8),
        check_vma=False,
    )
```

```python
import functools
import types

import jax
import jax.numpy as jnp
import numpy as np
from jax import lax
from jax.experimental import pallas as pl
from jax.experimental.pallas import tpu as pltpu
from jax.sharding import PartitionSpec as P

D = 256
HEADS = 8
HEAD = 32
FF = 768
CLASSES = 1000
CPAD = 1024
CIN = 128
GRID = 14
KER = 7
LAYERS = 2
PIX = 196
RB = 169
RANK = 8

EPSILON = 1e-05
MASKED = -1000000000.0
MOMENTUM = 0.9
LEARN_RATE = 16.0
SMALL_RATE = 4.0
PRECISE = lax.Precision.HIGHEST
SCALE = HEAD ** (-0.5)

COLS = 16
TOK = GRID * COLS
KEYS = 128
HALF = 128
PARTS = 3 * CIN
F32 = jnp.float32
BF16 = jnp.bfloat16
VMEM_LIMIT = 58 * 1024 * 1024

GROUPS = (
    ((0, 80, 0), (80, 32, 32), (112, 32, 64), (144, 80, 96)),
    ((0, 112, 0), (112, 112, 96)),
)


def row_order(layer):
    if layer % 2 == 0:
        return list(range(GRID))
    return [*range(0, GRID, 2), *range(1, GRID, 2)]


def window_start(cell, dil):
    residue, position = cell % dil, cell // dil
    length = (GRID - residue + dil - 1) // dil
    return min(max(position - KER // 2, 0), length - KER)


def in_window(query, key, dil):
    if query % dil != key % dil:
        return False
    first = window_start(query, dil)
    return first <= key // dil < first + KER


@functools.lru_cache(None)
def static_maps(layer):
    dil = 1 + layer % 2
    order = row_order(layer)
    starts = np.zeros(GRID, np.int64)
    mask = np.zeros((TOK, KEYS), np.float32)
    for q0, nq, k0 in GROUPS[layer % 2]:
        for place in range(q0 // COLS, (q0 + nq) // COLS):
            qy = order[place]
            for j in range(8):
                ky = order[k0 // COLS + j]
                if not in_window(qy, ky, dil):
                    continue
                starts[place] = ky // dil - qy // dil + KER - 1 - j
                for x in range(GRID):
                    for kx in range(GRID):
                        if in_window(x, kx, dil):
                            mask[place * COLS + x, j * COLS + kx] = 1.0
    shifts = np.zeros((COLS, KEYS, KEYS), np.float32)
    for x in range(GRID):
        for kx in range(GRID):
            if in_window(x, kx, dil):
                dx = kx // dil - x // dil + KER - 1
                for j in range(8):
                    shifts[x, j * COLS + dx, j * COLS + kx] = 1.0
    return starts, shifts, mask


def norm_stats(values):
    centred = values - jnp.mean(values, axis=-1, keepdims=True)
    rstd = lax.rsqrt(jnp.mean(centred * centred, axis=-1, keepdims=True) + EPSILON)
    return centred * rstd, rstd


def norm_back(grad, xhat, rstd, gain):
    scaled = grad * gain
    mean_one = jnp.mean(scaled, axis=-1, keepdims=True)
    mean_two = jnp.mean(scaled * xhat, axis=-1, keepdims=True)
    return rstd * (scaled - mean_one - xhat * mean_two)


def col_sum(values):
    return jnp.sum(values, axis=0, keepdims=True)


def dot_nn(a, b, **kw):
    return lax.dot_general(a, b, (((1,), (0,)), ((), ())), preferred_element_type=F32, **kw)


def dot_nt(a, b, **kw):
    return lax.dot_general(a, b, (((1,), (1,)), ((), ())), preferred_element_type=F32, **kw)


def dot_tn(a, b, **kw):
    return lax.dot_general(a, b, (((0,), (0,)), ((), ())), preferred_element_type=F32, **kw)


ERFC_T = 0.44
ERFC_POLY = (
    0.24822096599679971,
    0.24887097779118345,
    0.21731489562842682,
    0.21580753897325447,
    -0.020171305217729862,
    0.2966767736009737,
    -0.2779414931115683,
    0.07122182759012696,
)


def gelu_parts(x):
    bell = jnp.exp(-0.5 * x * x)
    t = 1.0 / (1.0 + (ERFC_T * 0.5**0.5) * jnp.abs(x))
    poly = jnp.full_like(t, 0.5 * ERFC_POLY[-1])
    for c in ERFC_POLY[-2::-1]:
        poly = poly * t + 0.5 * c
    tail = poly * t * bell
    cdf = jnp.where(x < 0, tail, 1.0 - tail)
    return x * cdf, cdf + x * bell * (1.0 / (2.0 * np.pi) ** 0.5)


def head_masks():
    lane = lax.broadcasted_iota(jnp.int32, (1, HALF), 1)
    return [jnp.where(lane // HEAD == h, 1.0, 0.0).astype(BF16) for h in range(4)]


def spread_heads(block, masks):
    return jnp.concatenate([block * m for m in masks], axis=0)


def whole(shape):
    return pl.BlockSpec(shape, lambda *_: (0,) * len(shape))


def params(n=1):
    return pltpu.CompilerParams(
        dimension_semantics=("arbitrary",) * n, vmem_limit_bytes=VMEM_LIMIT
    )


def cost(micros):
    return pl.CostEstimate(flops=int(micros * 1.1e9), bytes_accessed=0, transcendentals=0)


def call(name, kernel, steps, me, ins, outs, scratch, micros):
    names = ["me", *[e[0] for e in ins], *[e[0] for e in outs], *[e[0] for e in scratch]]

    def body(*refs):
        kernel(types.SimpleNamespace(**dict(zip(names, refs, strict=True))))

    results = pl.pallas_call(
        body,
        grid_spec=pltpu.PrefetchScalarGridSpec(
            num_scalar_prefetch=1,
            grid=(steps,),
            in_specs=[e[2] or whole(e[1].shape) for e in ins],
            out_specs=[e[3] or whole(e[1]) for e in outs],
            scratch_shapes=[pltpu.VMEM(e[1], e[2]) for e in scratch],
        ),
        out_shape=[jax.ShapeDtypeStruct(e[1], e[2]) for e in outs],
        compiler_params=params(),
        cost_estimate=cost(micros),
        name=name,
    )(me, *[e[1] for e in ins])
    return types.SimpleNamespace(**dict(zip([e[0] for e in outs], results, strict=True)))


def patch_kernel(feat_ref, out_ref, wide_ref, patch_ref):
    @pl.when(pl.program_id(0) == 0)
    def _():
        patch_ref[...] = jnp.zeros_like(patch_ref)

    for item in range(feat_ref.shape[0]):
        wide_ref[item, :, 0 : 2 * GRID, :] = feat_ref[item].astype(F32)
        even = wide_ref[item, :, pl.ds(0, GRID, stride=2), :]
        odd = wide_ref[item, :, pl.ds(1, GRID, stride=2), :]
        patch_ref[item, :, 1 : GRID + 1, 0:CIN] = odd
        patch_ref[item, :, 0:GRID, CIN : 2 * CIN] = even
        patch_ref[item, :, 0:GRID, 2 * CIN : 3 * CIN] = odd
        both = patch_ref[item].astype(BF16).reshape(GRID, 2, COLS, PARTS)
        for par in range(2):
            out_ref[item, par] = both[:, par].reshape(TOK, PARTS)


def make_patches(features):
    slots = features.shape[0]
    items = max(n for n in (1, 2, 3, 4) if slots % n == 0)
    return pl.pallas_call(
        patch_kernel,
        grid=(slots // items,),
        in_specs=[pl.BlockSpec((items, 2 * GRID, 2 * GRID, CIN), lambda i: (i, 0, 0, 0))],
        out_specs=pl.BlockSpec((items, 2, TOK, PARTS), lambda i: (i, 0, 0, 0)),
        out_shape=jax.ShapeDtypeStruct((slots, 2, TOK, PARTS), BF16),
        scratch_shapes=[
            pltpu.VMEM((items, 2 * GRID, 32, CIN), F32),
            pltpu.VMEM((items, 2 * GRID, COLS, PARTS), F32),
        ],
        compiler_params=params(),
        cost_estimate=cost(7),
        name="patches",
    )(features)


WIDE = 16 * COLS


def split_three(x):
    high = x.astype(BF16).astype(F32)
    mid = (x - high).astype(BF16).astype(F32)
    return jnp.concatenate([high, mid, x - high - mid], axis=0).astype(BF16)


def exact_dot(dot, x, hot):
    n = x.shape[0]
    out = dot(split_three(x), hot)
    return out[0:n] + out[n : 2 * n] + out[2 * n : 3 * n]


def shift_arrays():
    maps = [static_maps(layer) for layer in range(LAYERS)]
    return jnp.asarray(np.stack([m[1] for m in maps]), BF16), jnp.asarray(np.stack([m[2] for m in maps]))


def make_bias(me, tables):
    shifts, masks = shift_arrays()

    def kernel(r):
        for layer in range(LAYERS):

            @pl.when(pl.program_id(0) == layer)
            def _():
                for y, start in enumerate(static_maps(layer)[0]):
                    moved = pltpu.roll(r.table[0], int(-COLS * start) % WIDE, 1)
                    r.rows[pl.ds(y, HEADS, stride=GRID), :] = moved[:, :KEYS]

        rows = r.rows[...]
        for x in range(GRID):
            r.flat[pl.ds(x, HEADS * GRID, stride=COLS), :] = exact_dot(dot_nn, rows, r.shift[0, x])
        for x in range(GRID, COLS):
            r.flat[pl.ds(x, HEADS * GRID, stride=COLS), :] = jnp.zeros((HEADS * GRID, KEYS), F32)
        for h in range(HEADS):
            block = r.flat[h * TOK : (h + 1) * TOK, :]
            r.out[0, h] = jnp.where(r.mask[0] > 0.5, block, MASKED)

    return call(
        "bias",
        kernel,
        LAYERS,
        me,
        [
            ("table", tables, pl.BlockSpec((1, HEADS, WIDE), lambda i, *_: (i, 0, 0))),
            ("shift", shifts, pl.BlockSpec((1, COLS, KEYS, KEYS), lambda i, *_: (i, 0, 0, 0))),
            ("mask", masks, pl.BlockSpec((1, TOK, KEYS), lambda i, *_: (i, 0, 0))),
        ],
        [
            (
                "out",
                (LAYERS, HEADS, TOK, KEYS),
                F32,
                pl.BlockSpec((1, HEADS, TOK, KEYS), lambda i, *_: (i, 0, 0, 0)),
            )
        ],
        [("flat", (HEADS * TOK, KEYS), F32), ("rows", (HEADS * GRID, KEYS), F32)],
        5,
    ).out


def table_grads(me, zero, one):
    shifts, _ = shift_arrays()

    def kernel(r):
        for layer, (grad, out) in enumerate(((r.grad0, r.out0), (r.grad1, r.out1))):
            total = None
            for x in range(GRID):
                part = grad[pl.ds(x, HEADS * GRID, stride=COLS), :]
                part = exact_dot(dot_nt, part, r.shift[layer, x])
                total = part if total is None else total + part
            r.rows[...] = total
            result = None
            for y, start in enumerate(static_maps(layer)[0]):
                part = pad_lanes(r.rows[pl.ds(y, HEADS, stride=GRID), :], WIDE)
                moved = pltpu.roll(part, int(COLS * start) % WIDE, 1)
                result = moved if result is None else result + moved
            out[...] = result

    out = call(
        "table_grads",
        kernel,
        1,
        me,
        [("grad0", zero, None), ("grad1", one, None), ("shift", shifts, None)],
        [("out0", (HEADS, WIDE), F32, None), ("out1", (HEADS, WIDE), F32, None)],
        [("rows", (HEADS * GRID, KEYS), F32)],
        6,
    )
    return out.out0, out.out1


def pieces_of(shards, group):
    narrow, wide = D // shards, FF // shards
    sizes = [("qkv", narrow, 3), ("proj", narrow, 1), ("up", narrow, 3), ("down", wide, 1)]
    if group == 0:
        sizes = [("conv", 9 * CIN // shards, 1)] + sizes
    else:
        sizes = sizes + [("head", narrow, 4)]
    out, at = {}, 0
    for name, rows, blocks in sizes:
        out[name] = (at, rows, blocks)
        at += rows * blocks
    return out, at


SHARDS = 8
COUNT_ROWS = 16
NAMES = ("conv", "qkv", "proj", "up", "down", "head")
WHOLE_NAMES = ("conv", "head")


def pack(parts):
    out = []
    for part in parts:
        if part.shape[1] == CLASSES:
            part = jnp.pad(part, ((0, 0), (0, CPAD - CLASSES)))
        out += [part[:, c : c + D] for c in range(0, part.shape[1], D)]
    return jnp.concatenate(out, axis=0)


def pack_weights(weights, counts):
    def kernel(r):
        for group, packed in ((0, r.packed0), (1, r.packed1)):
            for name, (at, rows, blocks) in pieces_of(SHARDS, group)[0].items():
                ref = getattr(r, name)
                for c in range(blocks):
                    width = min(D, ref.shape[-1] - c * D)
                    cols = slice(c * D, c * D + width)
                    value = ref[:, cols] if name in WHOLE_NAMES else ref[group, :, cols]
                    value = value.astype(BF16)
                    if width < D:
                        value = jnp.concatenate([value, jnp.zeros((rows, D - width), BF16)], axis=1)
                    packed[at + c * rows : at + (c + 1) * rows, :] = value
        end = pieces_of(SHARDS, 0)[1]
        r.packed0[end : end + COUNT_ROWS, :] = jnp.broadcast_to(r.count[...].astype(F32), (COUNT_ROWS, D)).astype(BF16)

    ends = [pieces_of(SHARDS, group)[1] for group in range(2)]
    out = call(
        "pack_weights",
        kernel,
        1,
        jnp.zeros((1,), jnp.int32),
        [*[(n, w, None) for n, w in zip(NAMES, weights)], ("count", counts, None)],
        [("packed0", (ends[0] + COUNT_ROWS, D), BF16, None), ("packed1", (ends[1], D), BF16, None)],
        [],
        2,
    )
    return out.packed0, out.packed1


def unpack_weights(me, sources, targets, group):
    layout, _ = pieces_of(SHARDS, group)
    for ref, low, high, offsets in sources:
        for p, offset in enumerate(offsets):
            owner = me ^ offset
            for name, target in targets.items():
                at, rows, blocks = layout[name]
                if not low <= at < high:
                    continue
                place = pl.ds(pl.multiple_of(owner * rows, 16), rows)
                for c in range(blocks):
                    first = at - low + c * rows
                    target[place, c * D : (c + 1) * D] = ref[p, first : first + rows, :]


def attend(layer, item, joined_ref, bias_ref, probs_ref, mixed_ref):
    masks = head_masks()
    base = item * TOK
    for q0, nq, k0 in GROUPS[layer]:
        for hf in range(2):
            lanes = slice(hf * HALF, (hf + 1) * HALF)
            at = lambda which: slice(which * D + hf * HALF, which * D + (hf + 1) * HALF)
            query = joined_ref[base + q0 : base + q0 + nq, at(0)]
            keys = spread_heads(joined_ref[base + k0 : base + k0 + KEYS, at(1)], masks)
            values = spread_heads(joined_ref[base + k0 : base + k0 + KEYS, at(2)], masks)
            scores = dot_nt(query, keys)
            low = []
            for h in range(4):
                head = hf * 4 + h
                s = scores[:, h * KEYS : (h + 1) * KEYS] * SCALE + bias_ref[0, head, q0 : q0 + nq, :]
                e = jnp.exp(s - jnp.max(s, axis=-1, keepdims=True))
                p = e * (1.0 / jnp.sum(e, axis=-1, keepdims=True))
                probs_ref[item, q0 : q0 + nq, head * KEYS : (head + 1) * KEYS] = p
                low.append(p.astype(BF16))
            mixed = dot_nn(jnp.concatenate(low, axis=1), values)
            mixed_ref[base + q0 : base + q0 + nq, lanes] = mixed.astype(BF16)


def layer_forward(layer, hidden, vec_ref, weights, bias_ref, outs, items):
    joined_ref, probs_ref, mixed_ref, after_ref, slope_ref, active_ref = outs
    vec = lambda i: vec_ref[LAYER_AT[layer] + i : LAYER_AT[layer] + i + 1, :]
    xhat, _ = norm_stats(hidden)
    normed = (xhat * vec(0) + vec(1)).astype(BF16)
    for c in range(3):
        part = dot_nn(normed, weights["qkv"][:, c * D : (c + 1) * D])
        if c != 1:
            part = part + vec(2 if c == 0 else 3)
        joined_ref[:, c * D : (c + 1) * D] = part.astype(BF16)
    for item in range(items):
        attend(layer, item, joined_ref, bias_ref, probs_ref, mixed_ref)
    after = hidden + (dot_nn(mixed_ref[...], weights["proj"][...]) + vec(4))
    after_ref[...] = after
    xhat, _ = norm_stats(after)
    normed = (xhat * vec(5) + vec(6)).astype(BF16)
    total = None
    for c in range(3):
        pre = dot_nn(normed, weights["up"][:, c * D : (c + 1) * D]) + vec(8 + c)
        active, slope = gelu_parts(pre)
        active = active.astype(BF16)
        slope_ref[:, c * D : (c + 1) * D] = slope
        active_ref[:, c * D : (c + 1) * D] = active
        part = dot_nn(active, weights["down"][c * D : (c + 1) * D, :])
        total = part if total is None else total + part
    return after + (total + vec(7))


def conv_taps(patch_ref, item):
    odd = patch_ref[item, 1]
    up = jnp.concatenate([jnp.zeros((COLS, PARTS), BF16), odd[: TOK - COLS]], axis=0)
    return up, patch_ref[item, 0], odd


CACHE = (
    ("joined", 3 * D, BF16),
    ("probs", None, F32),
    ("mixed", D, BF16),
    ("after", D, F32),
    ("slope", FF, F32),
    ("active", FF, BF16),
)
MATRICES = (("qkv", (D, FF)), ("proj", (D, D)), ("up", (D, FF)), ("down", (FF, D)))
MATRIX_NAMES = [m[0] for m in MATRICES]


def token_spec(items, width=D):
    return pl.BlockSpec((items * TOK, width), lambda i, *_: (i, 0))


def cache_entries(slots, items):
    out = []
    for name, width, dtype in CACHE:
        if width is None:
            spec = pl.BlockSpec((items, TOK, HEADS * KEYS), lambda i, *_: (i, 0, 0))
            out.append((name, (slots, TOK, HEADS * KEYS), dtype, spec))
        else:
            out.append((name, (slots * TOK, width), dtype, token_spec(items, width)))
    return out


def caches_of(r):
    return tuple(getattr(r, entry[0]) for entry in CACHE)


def bias_spec(layer):
    return pl.BlockSpec((1, HEADS, TOK, KEYS), lambda i, *_: (layer, 0, 0, 0))


def patch_spec(items):
    return pl.BlockSpec((items, 2, TOK, PARTS), lambda i, *_: (i, 0, 0, 0))


def source_entries(sources):
    return [(f"source{i}", array, None) for i, (array, *_) in enumerate(sources)]


def sources_of(r, sources):
    return [(getattr(r, f"source{i}"), *entry[1:]) for i, entry in enumerate(sources)]


def count_of(sources):
    total = jnp.zeros((1, 1), F32)
    for ref, _, high, offsets in sources:
        if ref.shape[1] > high:
            for p in range(len(offsets)):
                total = total + ref[p, high : high + COUNT_ROWS, :].astype(F32)[0:1, 0:1]
    return total


CONV_AT, LAYER_AT, FINAL_AT, BIAS_AT = 0, (3, 14), 25, 27


def forward_zero(me, patches, sources, vecs, bias, items):
    slots = patches.shape[0]

    def kernel(r):
        names = ["conv_w", *MATRIX_NAMES]
        weights = {n: getattr(r, n) for n in names}

        @pl.when(pl.program_id(0) == 0)
        def _():
            targets = {n.removesuffix("_w"): ref for n, ref in weights.items()}
            unpack_weights(r.me[0], sources_of(r, sources), targets, 0)
            r.count[...] = jnp.broadcast_to(count_of(sources_of(r, sources)), r.count.shape)

        for item in range(items):
            taps = conv_taps(r.patch, item)
            total = None
            for a in range(3):
                part = dot_nn(taps[a], r.conv_w[a * PARTS : (a + 1) * PARTS, :])
                total = part if total is None else total + part
            r.conv[item * TOK : (item + 1) * TOK, :] = total + r.vecs[CONV_AT : CONV_AT + 1, :]
        xhat, _ = norm_stats(r.conv[...])
        hidden = xhat * r.vecs[CONV_AT + 1 : CONV_AT + 2, :] + r.vecs[CONV_AT + 2 : CONV_AT + 3, :]
        hidden = layer_forward(0, hidden, r.vecs, weights, r.bias, caches_of(r), items)
        for item in range(items):
            for place, row in enumerate(row_order(1)):
                r.hidden[item * TOK + place * COLS : item * TOK + (place + 1) * COLS, :] = hidden[
                    item * TOK + row * COLS : item * TOK + (row + 1) * COLS
                ]

    return call(
        "forward_zero",
        kernel,
        slots // items,
        me,
        [
            ("patch", patches, patch_spec(items)),
            *source_entries(sources),
            ("vecs", vecs, None),
            ("bias", bias, bias_spec(0)),
        ],
        [
            ("hidden", (slots * TOK, D), F32, token_spec(items)),
            ("conv", (slots * TOK, D), F32, token_spec(items)),
            *cache_entries(slots, items),
            *[(n, shape, BF16, None) for n, shape in MATRICES],
            ("count", (8, 128), F32, None),
        ],
        [("conv_w", (9 * CIN, D), BF16)],
        54,
    )


def real_cells():
    place = lax.broadcasted_iota(jnp.int32, (TOK, 1), 0)
    return jnp.where(place % COLS < GRID, 1.0, 0.0)


def classify(r, slots, counts):
    rows = r.pooled.shape[0]
    place = lax.broadcasted_iota(jnp.int32, (rows, 1), 0)
    label = jnp.full((rows, 1), -1, jnp.int32)
    for i in range(slots):
        label = jnp.where(place == i, r.me[2 + i], label)
    live = jnp.where(place < r.me[1], 1.0, 0.0)
    count = sum([getattr(r, f"count{i}")[0:1, 0:1] for i in range(counts)])
    pooled = r.pooled[...].astype(BF16)
    head_bias = jnp.concatenate([r.vecs[BIAS_AT + c : BIAS_AT + c + 1, :] for c in range(CPAD // D)], axis=1)
    logits = dot_nn(pooled, r.head[...]) + head_bias
    peak = jnp.max(logits, axis=-1, keepdims=True)
    log_total = peak + jnp.log(jnp.sum(jnp.exp(logits - peak), axis=-1, keepdims=True))
    lane = lax.broadcasted_iota(jnp.int32, logits.shape, 1)
    onehot = jnp.where(label == lane, 1.0, 0.0)
    picked = jnp.sum(onehot * logits, axis=-1, keepdims=True)
    loss = col_sum(live * (log_total - picked))
    r.sums[0:8, :] = jnp.broadcast_to(loss, (8, 128))
    r.sums[8:16, :] = jnp.broadcast_to(count, (8, 128))
    d_logits = (jnp.exp(logits - log_total) - onehot) * ((1.0 / count) * live)
    d_logits = jnp.where(lane < CLASSES, d_logits, 0.0).astype(BF16)
    r.head_grad[...] = dot_tn(pooled, d_logits)
    r.head_bias_grad[...] = col_sum(d_logits.astype(F32))
    r.d_pooled[...] = dot_nt(d_logits, r.head[...]) * (1.0 / PIX)


def forward_one(me, hidden, sources, vecs, bias, items):
    slots = hidden.shape[0] // TOK
    rows = -(-slots // 16) * 16

    def kernel(r):
        weights = {n: getattr(r, n) for n in MATRIX_NAMES}
        step = pl.program_id(0)

        @pl.when(step == 0)
        def _():
            unpack_weights(r.me[0], sources_of(r, sources), weights | dict(head=r.head), 1)
            r.pooled[...] = jnp.zeros_like(r.pooled)

        out = layer_forward(1, r.hidden[...], r.vecs, weights, r.bias, caches_of(r), items)
        r.out[...] = out
        xhat, _ = norm_stats(out)
        normed = xhat * r.vecs[FINAL_AT : FINAL_AT + 1, :] + r.vecs[FINAL_AT + 1 : FINAL_AT + 2, :]
        real = real_cells()
        for item in range(items):
            mean = col_sum(normed[item * TOK : (item + 1) * TOK] * real) * (1.0 / PIX)
            r.pooled[pl.ds(step * items + item, 1), :] = mean

    return call(
        "forward_one",
        kernel,
        slots // items,
        me,
        [
            ("hidden", hidden, token_spec(items)),
            *source_entries(sources),
            ("vecs", vecs, None),
            ("bias", bias, bias_spec(1)),
        ],
        [
            ("out", (slots * TOK, D), F32, token_spec(items)),
            *cache_entries(slots, items),
            *[(n, shape, BF16, None) for n, shape in MATRICES],
            ("head", (D, CPAD), BF16, None),
            ("pooled", (rows, D), F32, None),
        ],
        [],
        42,
    )


def attend_back(layer, item, first, joined_ref, probs_ref, dmix_ref, djoin_ref, dkv_ref, bgrad_ref):
    masks = head_masks()
    base = item * TOK
    dkv_ref[...] = jnp.zeros_like(dkv_ref)
    for q0, nq, k0 in GROUPS[layer]:
        qrows = slice(base + q0, base + q0 + nq)
        krows = slice(base + k0, base + k0 + KEYS)
        for hf in range(2):
            lanes = slice(hf * HALF, (hf + 1) * HALF)
            at = lambda which: slice(which * D + hf * HALF, which * D + (hf + 1) * HALF)
            query = spread_heads(joined_ref[qrows, at(0)], masks)
            keys = spread_heads(joined_ref[krows, at(1)], masks)
            values = spread_heads(joined_ref[krows, at(2)], masks)
            d_mix = dmix_ref[qrows, lanes]
            d_probs = dot_nt(d_mix, values)
            d_low, p_low = [], []
            for h in range(4):
                head = hf * 4 + h
                p = probs_ref[item, q0 : q0 + nq, head * KEYS : (head + 1) * KEYS]
                dp = d_probs[:, h * KEYS : (h + 1) * KEYS]
                ds = (p * (dp - jnp.sum(dp * p, axis=-1, keepdims=True))).astype(BF16)
                place = slice(head * TOK + q0, head * TOK + q0 + nq)
                bgrad_ref[place, :] += ds.astype(F32)
                d_low.append(ds)
                p_low.append(p.astype(BF16))
            d_query = dot_nn(jnp.concatenate(d_low, axis=1), keys) * SCALE
            djoin_ref[qrows, at(0)] = d_query.astype(BF16)
            d_keys = dot_tn(jnp.concatenate(d_low, axis=0), query)
            d_values = dot_tn(jnp.concatenate(p_low, axis=0), spread_heads(d_mix, masks))
            dkv_ref[k0 : k0 + KEYS, lanes] += d_keys
            dkv_ref[k0 : k0 + KEYS, D + hf * HALF : D + (hf + 1) * HALF] += d_values
    djoin_ref[base : base + TOK, D : 2 * D] = (dkv_ref[:, 0:D] * SCALE).astype(BF16)
    djoin_ref[base : base + TOK, 2 * D : 3 * D] = dkv_ref[:, D : 2 * D].astype(BF16)


def layer_backward(layer, d_out, hidden, vec_ref, weights, caches, work, grads, vgrad_ref, bgrad_ref, items):
    joined_ref, probs_ref, mixed_ref, after_ref, slope_ref, active_ref = caches
    dmix_ref, djoin_ref, dkv_ref = work
    vec = lambda i: vec_ref[LAYER_AT[layer] + i : LAYER_AT[layer] + i + 1, :]

    def add(row, value):
        vgrad_ref[row : row + 1, :] += value

    d_branch = d_out.astype(BF16)
    add(7, col_sum(d_branch.astype(F32)))
    xhat, rstd = norm_stats(after_ref[...])
    normed = (xhat * vec(5) + vec(6)).astype(BF16)
    d_normed = None
    for c in range(3):
        cols = slice(c * D, (c + 1) * D)
        grads["down"][:, cols] += dot_tn(d_branch, active_ref[:, cols])
        d_active = dot_nt(d_branch, weights["down"][cols, :])
        d_pre = (d_active * slope_ref[:, cols]).astype(BF16)
        add(8 + c, col_sum(d_pre.astype(F32)))
        grads["up"][:, cols] += dot_tn(normed, d_pre)
        part = dot_nt(d_pre, weights["up"][:, cols])
        d_normed = part if d_normed is None else d_normed + part
    add(5, col_sum(d_normed * xhat))
    add(6, col_sum(d_normed))
    d_after = d_out + norm_back(d_normed, xhat, rstd, vec(5))
    d_proj = d_after.astype(BF16)
    add(4, col_sum(d_proj.astype(F32)))
    grads["proj"][...] += dot_tn(mixed_ref[...], d_proj)
    dmix_ref[...] = dot_nt(d_proj, weights["proj"][...]).astype(BF16)
    for item in range(items):
        attend_back(layer, item, item == 0, joined_ref, probs_ref, dmix_ref, djoin_ref, dkv_ref, bgrad_ref)
    add(2, col_sum(djoin_ref[:, 0:D].astype(F32)))
    add(3, col_sum(djoin_ref[:, 2 * D : 3 * D].astype(F32)))
    xhat, rstd = norm_stats(hidden)
    normed = (xhat * vec(0) + vec(1)).astype(BF16)
    d_normed = None
    for c in range(3):
        cols = slice(c * D, (c + 1) * D)
        grads["qkv"][:, cols] += dot_tn(normed, djoin_ref[:, cols])
        part = dot_nt(djoin_ref[:, cols], weights["qkv"][:, cols])
        d_normed = part if d_normed is None else d_normed + part
    add(0, col_sum(d_normed * xhat))
    add(1, col_sum(d_normed))
    return d_after + norm_back(d_normed, xhat, rstd, vec(0))


def split_two(x):
    high = x.astype(BF16)
    return high, (x - high.astype(F32)).astype(BF16)


def wide_dot(dot, rows, matrix):
    stacked = split_three(rows)
    high, low = split_two(matrix)
    out = dot(stacked, high) + dot(stacked, low)
    return out[0:RANK] + out[RANK : 2 * RANK] + out[2 * RANK : 3 * RANK]


def block_of(whole_ref, entry, c):
    at, rows, _ = entry
    return jnp.concatenate(
        [whole_ref[s, at + c * rows : at + (c + 1) * rows, :] for s in range(SHARDS)], axis=0
    )


def factor_of(r, group, name):
    ref = getattr(r, "fac_" + name)
    return ref[...] if name in WHOLE_NAMES else ref[group]


def finish_grads(r, group, grads):
    layout, _ = pieces_of(SHARDS, group)
    me = r.me[0]
    for name, (at, rows, blocks) in layout.items():
        matrix = grads[name]
        if name in ("down", "conv"):
            matrix = jnp.transpose(matrix[...])
        for s in range(SHARDS):
            for c in range(blocks):
                piece = matrix[s * rows : (s + 1) * rows, c * D : (c + 1) * D]
                r.whole[s, at + c * rows : at + (c + 1) * rows, :] = piece
    for name, (at, rows, blocks) in layout.items():
        err = getattr(r, "err_" + name)
        for c in range(blocks):
            width = min(D, err.shape[-1] - c * D)
            cols = slice(c * D, c * D + width)
            value = err[0, :, cols] if name in WHOLE_NAMES else err[0, group, :, cols]
            place = slice(at + c * rows, at + (c + 1) * rows)
            r.whole[me, place, 0:width] += value
    r.own[...] = r.whole[me]
    if group == 0:
        for i, chip in enumerate((0, 2, 4, 6)):
            r.far[i] = r.whole[me ^ chip ^ 1].astype(BF16)
            if chip:
                r.near[i - 1] = r.whole[me ^ chip].astype(BF16)
    else:
        r.sent1[...] = r.whole[me ^ 1].astype(BF16)
        for chip in (2, 4, 6):
            for core in range(2):
                getattr(r, f"sent{chip}")[core] = r.whole[me ^ chip ^ core].astype(BF16)
    at_lane, lefts = 0, []
    for name, entry in layout.items():
        total = None
        for c in range(entry[2]):
            fac = factor_of(r, group, name)
            width = min(D, fac.shape[-1] - c * D)
            block = block_of(r.whole, entry, c)
            part = wide_dot(dot_nt, fac[:, c * D : c * D + width], block[:, :width])
            total = part if total is None else total + part
        lefts.append(total)
    return jnp.concatenate(lefts, axis=1)


def left_lanes(group):
    return sum(rows * SHARDS for _, rows, _ in pieces_of(SHARDS, group)[0].values())


def right_lanes(group):
    return sum(blocks * D for _, _, blocks in pieces_of(SHARDS, group)[0].values())


SMALLS = 2 * 512 + 128 + 128
HALF_LEFT = (left_lanes(0) + left_lanes(1) + SMALLS) // 2
HALF_RIGHT = (right_lanes(0) + right_lanes(1) + 2 * WIDE) // 2


def pad_lanes(x, lanes):
    return jnp.concatenate([x, jnp.zeros((x.shape[0], lanes - x.shape[1]), x.dtype)], axis=1)


def put_halves(r, whole):
    n = whole.shape[1] // 2
    first, second = whole[:, :n], whole[:, n:]
    odd = (r.me[0] & 1) == 1
    r.mine[...] = jnp.where(odd, second, first)
    r.other[...] = jnp.where(odd, first, second)


def get_halves(r, mine, other):
    odd = (r.me[0] & 1) == 1
    mine, other = mine[...], other[...]
    return jnp.concatenate([jnp.where(odd, other, mine), jnp.where(odd, mine, other)], axis=1)


def backward_outs(group):
    rows = pieces_of(SHARDS, group)[1]
    return [
        ("vgrad", (16, D), F32, None),
        ("bgrad", (HEADS * TOK, KEYS), F32, None),
        ("whole", (SHARDS, rows, D), F32, None),
        ("own", (rows, D), F32, None),
    ]


def factor_inputs(group, errs, facs):
    out = []
    for name, err, fac in zip(NAMES, errs, facs):
        if name in pieces_of(SHARDS, group)[0]:
            out += [("err_" + name, err, None), ("fac_" + name, fac, None)]
    return out


def backward_scratch(items):
    return [
        ("d_mixed", (items * TOK, D), BF16),
        ("d_joined", (items * TOK, 3 * D), BF16),
        ("d_keys", (TOK, 2 * D), F32),
        ("g_qkv", (D, FF), F32),
        ("g_proj", (D, D), F32),
        ("g_up", (D, FF), F32),
        ("g_down", (D, FF), F32),
    ]


def start_backward(r, grads):
    r.vgrad[...] = jnp.zeros_like(r.vgrad)
    r.bgrad[...] = jnp.zeros_like(r.bgrad)
    for ref in grads.values():
        ref[...] = jnp.zeros_like(ref)


def cache_inputs(caches, slots, items):
    return [(e[0], getattr(caches, e[0]), e[3]) for e in cache_entries(slots, items)]


def matrix_inputs(caches):
    return [(n, getattr(caches, n), None) for n in MATRIX_NAMES]


def backward_one(me, hidden, forward, vecs, count, errs, facs, items):
    slots = hidden.shape[0] // TOK

    def kernel(r):
        weights = {n: getattr(r, n) for n in MATRIX_NAMES}
        grads = {n: getattr(r, "g_" + n) for n in MATRIX_NAMES}
        step = pl.program_id(0)

        @pl.when(step == 0)
        def _():
            start_backward(r, grads)
            classify(r, slots, len(count))

        real = real_cells()
        d_final = jnp.concatenate(
            [real * r.d_pooled[pl.ds(step * items + item, 1), :] for item in range(items)], axis=0
        )
        xhat, rstd = norm_stats(r.out[...])
        r.vgrad[11:12, :] += col_sum(d_final * xhat)
        r.vgrad[12:13, :] += col_sum(d_final)
        d_out = norm_back(d_final, xhat, rstd, r.vecs[FINAL_AT : FINAL_AT + 1, :])
        work = (r.d_mixed, r.d_joined, r.d_keys)
        r.d_hidden[...] = layer_backward(
            1, d_out, r.hidden[...], r.vecs, weights, caches_of(r), work, grads, r.vgrad, r.bgrad, items
        )

        @pl.when(step == pl.num_programs(0) - 1)
        def _():
            r.left[...] = finish_grads(r, 1, grads | dict(head=r.head_grad))

    return call(
        "backward_one",
        kernel,
        slots // items,
        me,
        [
            ("out", forward.out, token_spec(items)),
            ("pooled", forward.pooled, None),
            *[(f"count{i}", c, None) for i, c in enumerate(count)],
            ("hidden", hidden, token_spec(items)),
            *matrix_inputs(forward),
            ("head", forward.head, None),
            ("vecs", vecs, None),
            *cache_inputs(forward, slots, items),
            *factor_inputs(1, errs, facs),
        ],
        [
            ("d_hidden", hidden.shape, F32, token_spec(items)),
            *backward_outs(1),
            ("left", (RANK, left_lanes(1)), F32, None),
            ("sums", (16, 128), F32, None),
            ("head_bias_grad", (1, CPAD), F32, None),
            *[(f"sent{chip}", (2, pieces_of(SHARDS, 1)[1], D), BF16, None) for chip in (2, 4, 6)],
            ("sent1", (pieces_of(SHARDS, 1)[1], D), BF16, None),
        ],
        [*backward_scratch(items), ("head_grad", (D, CPAD), F32), ("d_pooled", forward.pooled.shape, F32)],
        46,
    )


def backward_zero(me, back_one, forward, patches, vecs, errs, facs, items):
    slots = patches.shape[0]

    def kernel(r):
        weights = {n: getattr(r, n) for n in MATRIX_NAMES}
        grads = {n: getattr(r, "g_" + n) for n in [*MATRIX_NAMES, "conv"]}
        step = pl.program_id(0)

        @pl.when(step == 0)
        def _():
            start_backward(r, grads)

        order = row_order(1)
        rows = []
        for item in range(items):
            for row in range(GRID):
                first = item * TOK + order.index(row) * COLS
                rows.append(r.d_hidden[first : first + COLS, :])
        d_out = jnp.concatenate(rows, axis=0)
        conv_hat, conv_rstd = norm_stats(r.conv[...])
        gain = r.vecs[CONV_AT + 1 : CONV_AT + 2, :]
        hidden = conv_hat * gain + r.vecs[CONV_AT + 2 : CONV_AT + 3, :]
        work = (r.d_mixed, r.d_joined, r.d_keys)
        d_conv = layer_backward(
            0, d_out, hidden, r.vecs, weights, caches_of(r), work, grads, r.vgrad, r.bgrad, items
        )
        r.vgrad[12:13, :] += col_sum(d_conv * conv_hat)
        r.vgrad[13:14, :] += col_sum(d_conv)
        d_conv = norm_back(d_conv, conv_hat, conv_rstd, gain).astype(BF16)
        r.vgrad[11:12, :] += col_sum(d_conv.astype(F32))
        for item in range(items):
            taps = conv_taps(r.patch, item)
            part = d_conv[item * TOK : (item + 1) * TOK]
            for a in range(3):
                grads["conv"][:, a * PARTS : (a + 1) * PARTS] += dot_tn(part, taps[a])

        @pl.when(step == pl.num_programs(0) - 1)
        def _():
            parts = [finish_grads(r, 0, grads), r.left_one[...]]
            for ref in (r.vgrad, r.vgrad_one):
                parts += [ref[0:8, :], ref[8:16, :]]
            put_halves(r, jnp.concatenate([*parts, r.head_bias[...], r.sums[0:8, :]], axis=1))

    return call(
        "backward_zero",
        kernel,
        slots // items,
        me,
        [
            ("d_hidden", back_one.d_hidden, token_spec(items)),
            ("conv", forward.conv, token_spec(items)),
            ("patch", patches, patch_spec(items)),
            *matrix_inputs(forward),
            ("vecs", vecs, None),
            *cache_inputs(forward, slots, items),
            ("left_one", back_one.left, None),
            ("vgrad_one", back_one.vgrad, None),
            ("head_bias", back_one.head_bias_grad.reshape(8, 128), None),
            ("sums", back_one.sums, None),
            *factor_inputs(0, errs, facs),
        ],
        [
            *backward_outs(0),
            ("far", (4, pieces_of(SHARDS, 0)[1], D), BF16, None),
            ("near", (3, pieces_of(SHARDS, 0)[1], D), BF16, None),
            ("mine", (RANK, HALF_LEFT), F32, None),
            ("other", (RANK, HALF_LEFT), F32, None),
        ],
        [*backward_scratch(items), ("g_conv", (D, 9 * CIN), F32)],
        63,
    )


def inverse_cholesky(gram):
    row = lax.broadcasted_iota(jnp.int32, (1, RANK, 2 * RANK), 1)
    lane = lax.broadcasted_iota(jnp.int32, (1, RANK, 2 * RANK), 2)
    eye = jnp.broadcast_to(jnp.where(lane == row + RANK, 1.0, 0.0), (gram.shape[0], RANK, 2 * RANK))
    work = jnp.concatenate([gram, jnp.zeros_like(gram)], axis=2) + eye
    for k in range(RANK):
        scale = 1.0 / jnp.sqrt(work[:, k : k + 1, k : k + 1])
        pivot = work[:, k : k + 1, :] * scale
        column = work[:, :, k : k + 1] * scale
        work = jnp.where(row > k, work - column * pivot, jnp.where(row == k, pivot, work))
    return work[:, :, RANK : 2 * RANK]


def basis_lanes(group):
    return sum(rows for _, rows, _ in pieces_of(SHARDS, group)[0].values())


def right_factors(me, left, whole_zero, whole_one, tables):
    def kernel(r):
        groups = (r.whole0, r.whole1)
        left = get_halves(r, r.left_mine, r.left_other)
        entries, at = [], 0
        for group in range(2):
            for entry in pieces_of(SHARDS, group)[0].values():
                entries.append((group, entry, left[:, at : at + entry[1] * SHARDS]))
                at += entry[1] * SHARDS
        grams = jnp.stack([dot_nt(x, x, precision=PRECISE) for _, _, x in entries])
        inverses = inverse_cholesky(grams)
        rows_of = [[], []]
        parts = []
        for i, (group, entry, x) in enumerate(entries):
            basis = dot_nn(inverses[i], x, precision=PRECISE)
            rows_of[group].append((basis, entry[1]))
            for c in range(entry[2]):
                parts.append(wide_dot(dot_nn, basis, block_of(groups[group], entry, c)))
        for group, out in ((0, r.basis0), (1, r.basis1)):
            for s in range(SHARDS):
                at = 0
                for basis, rows in rows_of[group]:
                    out[s, :, at : at + rows] = basis[:, s * rows : (s + 1) * rows]
                    at += rows
        put_halves(r, jnp.concatenate([*parts, r.table0[...], r.table1[...]], axis=1))

    return call(
        "right_factors",
        kernel,
        1,
        me,
        [
            ("left_mine", left[0], None),
            ("left_other", left[1], None),
            ("whole0", whole_zero, None),
            ("whole1", whole_one, None),
            ("table0", tables[0], None),
            ("table1", tables[1], None),
        ],
        [
            ("mine", (RANK, HALF_RIGHT), F32, None),
            ("other", (RANK, HALF_RIGHT), F32, None),
            ("basis0", (SHARDS, RANK, basis_lanes(0)), F32, None),
            ("basis1", (SHARDS, RANK, basis_lanes(1)), F32, None),
        ],
        [],
        8,
    )


def six_products(x, other):
    high = x.astype(BF16).astype(F32)
    mid = (x - high).astype(BF16).astype(F32)
    low = x - high - mid
    terms = [high, mid, high, mid, low, high] if other else [high, high, mid, mid, high, low]
    return jnp.concatenate(terms, axis=0).astype(BF16)


def apply_update(me, weights, moms, facs, right, factors, own, received):
    def kernel(r):
        right_mine = get_halves(r, r.replica_mine, r.replica_other)
        right_all = get_halves(r, r.all_mine, r.all_other)
        at_col = 0
        for group in range(2):
            total = getattr(r, f"own{group}")[...] + getattr(r, f"sib{group}")[0].astype(F32)
            for chip in (2, 4, 6):
                total = total + getattr(r, f"got{group}_{chip}")[0].astype(F32)
            basis = getattr(r, f"basis{group}")
            at_row = 0
            for name, (at, rows, blocks) in pieces_of(SHARDS, group)[0].items():
                left = six_products(basis[0, :, at_row : at_row + rows], False)
                at_row += rows
                single = name in WHOLE_NAMES
                for c in range(blocks):
                    width = min(D, (CLASSES if name == "head" else blocks * D) - c * D)
                    cols = slice(c * D, c * D + width)
                    place = (slice(None), cols) if single else (group, slice(None), cols)
                    err_place = (0, slice(None), cols) if single else (0, group, slice(None), cols)
                    right = slice(at_col, at_col + D)
                    at_col += D
                    getattr(r, "new_fac_" + name)[place] = right_all[:, right][:, :width]
                    mine = dot_tn(left, six_products(right_mine[:, right], True))
                    every = dot_tn(left, six_products(right_all[:, right], True))
                    merged = total[at + c * rows : at + (c + 1) * rows]
                    getattr(r, "err_" + name)[err_place] = (merged - mine)[:, :width]
                    mom = MOMENTUM * getattr(r, "mom_" + name)[place] + every[:, :width]
                    getattr(r, "new_mom_" + name)[place] = mom
                    getattr(r, "new_" + name)[place] = getattr(r, "w_" + name)[place] - LEARN_RATE * mom
        r.small[...] = right_all[:, at_col:]

    mine_spec = lambda x: pl.BlockSpec((1,) + x.shape[1:], lambda i, m: (m[0], 0, 0))
    small = 2 * HALF_RIGHT - right_lanes(0) - right_lanes(1)
    return call(
        "apply_update",
        kernel,
        1,
        me,
        [
            *[("w_" + n, w, None) for n, w in zip(NAMES, weights)],
            *[("mom_" + n, m, None) for n, m in zip(NAMES, moms)],
            *zip(("replica_mine", "replica_other", "all_mine", "all_other"), right, [None] * 4),
            ("basis0", factors[0], mine_spec(factors[0])),
            ("basis1", factors[1], mine_spec(factors[1])),
            ("own0", own[0], None),
            ("own1", own[1], None),
            *[(f"got{g}_{chip}", received[g][chip], None) for g in range(2) for chip in (2, 4, 6)],
            *[(f"sib{g}", received[g][1], None) for g in range(2)],
        ],
        [
            *[("new_" + n, w.shape, F32, None) for n, w in zip(NAMES, weights)],
            *[("new_mom_" + n, w.shape, F32, None) for n, w in zip(NAMES, weights)],
            *[("err_" + n, (1,) + w.shape, F32, None) for n, w in zip(NAMES, weights)],
            *[("new_fac_" + n, f.shape, F32, None) for n, f in zip(NAMES, facs)],
            ("small", (RANK, small), F32, None),
        ],
        [],
        5,
    )


def swap(x, offset):
    return lax.ppermute(x, "fsdp", [(i, i ^ offset) for i in range(SHARDS)])


def swap_by_core(x, even, odd):
    return lax.ppermute(x, "fsdp", [(i, i ^ (odd if i & 1 else even)) for i in range(SHARDS)])


def swap_rep(x, offset, reps):
    return lax.ppermute(x, "rep", [(i, i ^ offset) for i in range(reps)])


def gather_chips(packed):
    return [packed, *[swap(packed, chip) for chip in (2, 4, 6)]]


def with_sibling(near, end):
    near = jnp.stack(near)
    return [(near, 0, end, (0, 2, 4, 6)), (swap(near, 1), 0, end, (1, 3, 5, 7))]


def gather_pair(packed):
    return jnp.stack([packed, swap(packed, 1)])


def spread_pair(pair, end):
    out = [(pair, 0, end, (0, 1))]
    return out + [(swap(pair, chip), 0, end, (chip, chip ^ 1)) for chip in (2, 4, 6)]


def sum_replica(mine, other):
    mine = mine + swap(other, 1)
    mine = mine + swap_by_core(mine, 2, 4)
    return mine + swap_by_core(mine, 4, 2)


def sum_replicas(x, reps):
    bit = 1
    while bit < reps:
        x = x + swap_rep(x, bit, reps)
        bit *= 2
    return x


def scatter_chips(back):
    return {chip: swap(getattr(back, f"sent{chip}"), chip) for chip in (2, 4, 6)}


def scatter_cores(back, received):
    total = back.sent1.astype(F32)
    for chip in (2, 4, 6):
        total = total + received[chip][1].astype(F32)
    return received | {1: swap(total.astype(BF16), 1)[None]}


def scatter_cores_first(far, near):
    got = swap(far, 1)
    sums = {}
    for i, chip in enumerate((2, 4, 6)):
        sums[chip] = (near[i].astype(F32) + got[i + 1].astype(F32)).astype(BF16)[None]
    return got, sums


def table_at(layer):
    return 3 * D + layer * (11 * D + HEADS * RB)


def small_blocks(small):
    parts, tables = [small[: 3 * D]], []
    for layer in range(LAYERS):
        at = table_at(layer)
        parts.append(small[at : at + 11 * D])
        tables.append(small[at + 11 * D : at + 11 * D + HEADS * RB])
    parts += [small[table_at(LAYERS) :], jnp.full((CPAD - CLASSES,), -1e30, F32)]
    vecs = jnp.concatenate(parts)
    tables = jnp.stack(tables).reshape(LAYERS, HEADS, 2 * KER - 1, 2 * KER - 1)
    tables = jnp.pad(tables, ((0, 0), (0, 0), (0, 3), (0, 3))).reshape(LAYERS, HEADS, WIDE)
    return vecs.reshape(-1, D), tables


def small_vector(vgrads, tables, head_bias):
    parts = [vgrads[0][11:14].reshape(-1)]
    for layer in range(LAYERS):
        table = tables[layer].reshape(HEADS, 16, 16)[:, : 2 * KER - 1, : 2 * KER - 1]
        parts += [vgrads[layer][:11].reshape(-1), table.reshape(-1)]
    return jnp.concatenate([*parts, vgrads[1][11:13].reshape(-1), head_bias[:CLASSES]])


def group_parts(group, conv, qkv, proj, up, down, head):
    layer = [m[group] for m in (qkv, proj, up, down)]
    return [conv] + layer if group == 0 else layer + [head]


def step(mesh, args):
    (
        features, labels, counts, tables, *rest
    ) = args
    weights, moms, errs, facs = rest[0:6], rest[6:12], rest[12:18], rest[18:24]
    small_params, small_mom = rest[24:]
    reps = mesh.shape["rep"]
    quick = mesh.shape["fsdp"] == SHARDS and reps & (reps - 1) == 0
    slots = features.shape[0]
    items = 2 if slots % 2 == 0 else 1

    if quick:
        ends = [pieces_of(SHARDS, group)[1] for group in range(2)]
        packed, second = pack_weights(weights, counts)
        near = gather_chips(packed)
        near[0], second, features, labels, counts, small_params = lax.optimization_barrier(
            (packed, second, features, labels, counts, small_params)
        )
        me = lax.axis_index("fsdp").astype(jnp.int32)[None]
        me = jnp.concatenate([me, counts[0], labels])
        sources0 = with_sibling(near, ends[0])
        pair, *held = lax.optimization_barrier((gather_pair(second), *[a for a, *_ in sources0]))
        sources0 = [(a, *entry[1:]) for a, entry in zip(held, sources0)]
        sources1 = spread_pair(pair, ends[1])
    else:
        me = jnp.concatenate([jnp.zeros((1,), jnp.int32), counts[0], labels])
        sides = [lax.all_gather(w.astype(BF16), "fsdp", axis=w.ndim - 2, tiled=True) for w in weights]
        sources = []
        for group in range(2):
            parts = group_parts(group, *sides)
            shards = [pack([p.reshape(SHARDS, -1, p.shape[1])[s] for p in parts]) for s in range(SHARDS)]
            sources.append([(jnp.stack(shards), 0, shards[0].shape[0], tuple(range(SHARDS)))])
        sources0, sources1 = sources

    vecs, bias_tables = small_blocks(small_params)
    bias = make_bias(me, bias_tables)
    patches = make_patches(features)
    zero = forward_zero(me, patches, sources0, vecs, bias, items)
    one = forward_one(me, zero.hidden, sources1, vecs, bias, items)
    if quick:
        count = [zero.count, *[swap_rep(zero.count, offset, reps) for offset in range(1, reps)]]
        count, *held = lax.optimization_barrier((count, *vars(one).values()))
        one = types.SimpleNamespace(**dict(zip(vars(one), held)))
    else:
        count = [jnp.broadcast_to(lax.psum(counts.astype(F32), ("rep", "fsdp")), (8, 128))]
    turned = [jnp.swapaxes(f, -1, -2) for f in facs]
    own_errs = errs
    if not quick:
        own_errs = [jnp.zeros((1,) + (w.shape[:-2] + (full // SHARDS, w.shape[-1])), F32) for w, full in zip(weights, FULL_ROWS)]
    back_one = backward_one(me, zero.hidden, one, vecs, count, own_errs, turned, items)
    item_count = back_one.sums[8, 0]
    if quick:
        received = [None, scatter_chips(back_one)]
    back_zero = backward_zero(me, back_one, zero, patches, vecs, own_errs, turned, items)
    if quick:
        received[1], *held = lax.optimization_barrier((received[1], *vars(back_zero).values()))
        back_zero = types.SimpleNamespace(**dict(zip(vars(back_zero), held)))
    tables_grad = table_grads(me, back_zero.bgrad, back_one.bgrad)
    if not quick:
        grads = [whole_matrices(group, b.whole) for group, b in ((0, back_zero), (1, back_one))]
        small = small_vector((back_zero.vgrad, back_one.vgrad), tables_grad, back_one.head_bias_grad[0])
        loss = lax.psum(back_one.sums[0, 0], ("rep", "fsdp"))
        return (loss, item_count, *general_tail(grads, weights, moms, errs, facs, small, small_params, small_mom))

    got, sums = scatter_cores_first(back_zero.far, back_zero.near)
    mine = back_zero.mine + swap(back_zero.other, 1)
    left = mine + swap_by_core(mine, 2, 4)
    left, item_count, *tables_grad = lax.optimization_barrier((left, back_one.sums[8, 0], *tables_grad))
    left = left + swap_by_core(left, 4, 2)
    sums, left = lax.optimization_barrier((sums, left))
    received[0] = {chip: swap(x, chip) for chip, x in sums.items()} | {1: got}
    left = sum_replicas(left, reps)
    left_other = swap(left, 1)
    left, left_other, received[0] = lax.optimization_barrier((left, left_other, received[0]))
    factors = right_factors(me, (left, left_other), back_zero.whole, back_one.whole, tables_grad)
    received[1] = scatter_cores(back_one, received[1])
    mine = sum_replica(factors.mine, factors.other)
    every = sum_replicas(mine, reps)
    updated = apply_update(
        me,
        weights,
        moms,
        turned,
        (mine, swap(mine, 1), every, swap(every, 1)),
        (factors.basis0, factors.basis1),
        (back_zero.own, back_one.own),
        received,
    )
    odd = (me[0] & 1) == 1
    summed = jnp.where(odd, left, left_other)[:, HALF_LEFT - SMALLS :]
    vgrads = []
    for layer in range(LAYERS):
        first, second = summed[:, 512 * layer : 512 * layer + D], summed[:, 512 * layer + D : 512 * (layer + 1)]
        vgrads.append(jnp.concatenate([first, second], axis=0))
    head_bias_grad = summed[:, 1024 : 1024 + 128].reshape(-1)
    loss = summed[0, 1024 + 128]
    table_sums = [updated.small[:, WIDE * i : WIDE * (i + 1)] for i in range(2)]
    new_small_mom = MOMENTUM * small_mom + small_vector(vgrads, table_sums, head_bias_grad)
    return (
        loss,
        item_count,
        *[getattr(updated, "new_" + n) for n in NAMES],
        *[getattr(updated, "new_mom_" + n) for n in NAMES],
        *[getattr(updated, "err_" + n) for n in NAMES],
        *[jnp.swapaxes(getattr(updated, "new_fac_" + n), -1, -2) for n in NAMES],
        small_params - SMALL_RATE * new_small_mom,
        new_small_mom,
    )


FULL_ROWS = (9 * CIN, D, D, D, FF, D)


def whole_matrices(group, packed):
    out = {}
    for name, (at, rows, blocks) in pieces_of(SHARDS, group)[0].items():
        cols = [packed[:, at + c * rows : at + (c + 1) * rows, :].reshape(SHARDS * rows, D) for c in range(blocks)]
        out[name] = jnp.concatenate(cols, axis=1)
    return out


def orthonormal(product, gram_mat):
    lower_tri = jnp.linalg.cholesky(gram_mat)
    return jnp.swapaxes(
        jax.scipy.linalg.solve_triangular(lower_tri, jnp.swapaxes(product, 1, 2), lower=True), 1, 2
    )


def general_tail(grads, weights, moms, errs, facs, small, small_params, small_mom):
    layer = [jnp.stack([grads[g][n] for g in range(2)]) for n in MATRIX_NAMES]
    wholes = [grads[0]["conv"][None], *layer, grads[1]["head"][None, :, :CLASSES]]
    lift = lambda xs: [xs[0][None], *xs[1:5], xs[5][None]]
    weights, moms, facs = lift(weights), lift(moms), lift(facs)
    errors = [errs[0], *[e[0] for e in errs[1:5]], errs[5]]
    merged = [
        lax.psum_scatter(g, "fsdp", scatter_dimension=1, tiled=True) + e for g, e in zip(wholes, errors)
    ]
    lefts = lax.psum(
        [jnp.einsum("bio,bok->bik", m, f, precision=PRECISE) for m, f in zip(merged, facs)], "rep"
    )
    grams = lax.psum([jnp.einsum("bik,bil->bkl", p, p, precision=PRECISE) for p in lefts], "fsdp")
    bases = [orthonormal(p, g) for p, g in zip(lefts, grams)]
    local = [jnp.einsum("bio,bik->bok", m, b, precision=PRECISE) for m, b in zip(merged, bases)]
    mine = lax.psum([*local, small], "fsdp")
    every = lax.psum(mine, "rep")
    product = lambda b, q: jnp.einsum("bik,bok->bio", b, q, precision=PRECISE)
    new_errs = [m - product(b, q) for m, b, q in zip(merged, bases, mine)]
    new_moms = [MOMENTUM * m + product(b, q) for m, b, q in zip(moms, bases, every)]
    new_weights = [w - LEARN_RATE * m for w, m in zip(weights, new_moms)]
    drop = lambda xs: [xs[0][0], *xs[1:5], xs[5][0]]
    new_small_mom = MOMENTUM * small_mom + every[6]
    return (
        *drop(new_weights),
        *drop(new_moms),
        new_errs[0],
        *[e[None] for e in new_errs[1:5]],
        new_errs[5],
        *drop(every[:6]),
        small_params - SMALL_RATE * new_small_mom,
        new_small_mom,
    )


def solution(mesh):
    rows, mids = P("fsdp", None), P(None, "fsdp", None)
    matrices = (rows, mids, mids, mids, mids, rows)
    errors = (
        P("rep", "fsdp", None),
        *[P("rep", None, "fsdp", None)] * 4,
        P("rep", "fsdp", None),
    )
    return jax.shard_map(
        lambda *args: step(mesh, args),
        mesh=mesh,
        in_specs=(
            P(("rep", "fsdp"), None, None, None),
            P(("rep", "fsdp")),
            P("rep", "fsdp"),
            P(),
            *matrices,
            *matrices,
            *errors,
            *[P()] * 8,
        ),
        out_specs=(P(), P(), *matrices, *matrices, *errors, *[P()] * 8),
        check_vma=False,
    )
```

```python
import functools
import types

import jax
import jax.numpy as jnp
import numpy as np
from jax import lax
from jax.experimental import pallas as pl
from jax.experimental.pallas import tpu as pltpu
from jax.sharding import PartitionSpec as P

D = 256
HEADS = 8
HEAD = 32
FF = 768
CLASSES = 1000
CPAD = 1024
CIN = 128
GRID = 14
KER = 7
LAYERS = 2
PIX = 196
RB = 169
RANK = 8

EPSILON = 1e-05
MASKED = -1000000000.0
MOMENTUM = 0.9
LEARN_RATE = 16.0
SMALL_RATE = 4.0
PRECISE = lax.Precision.HIGHEST
SCALE = HEAD ** (-0.5)

COLS = 16
TOK = GRID * COLS
KEYS = 128
HALF = 128
PARTS = 3 * CIN
FSDP, REP = "fsdp", "rep"
F32 = jnp.float32
BF16 = jnp.bfloat16
VMEM_LIMIT = 58 * 1024 * 1024

GROUPS = (
    ((0, 80, 0), (80, 32, 32), (112, 32, 64), (144, 80, 96)),
    ((0, 112, 0), (112, 112, 96)),
)


def row_order(layer):
    if layer % 2 == 0:
        return list(range(GRID))
    return [*range(0, GRID, 2), *range(1, GRID, 2)]


def window_start(cell, dil):
    residue, position = cell % dil, cell // dil
    length = (GRID - residue + dil - 1) // dil
    return min(max(position - KER // 2, 0), length - KER)


def in_window(query, key, dil):
    if query % dil != key % dil:
        return False
    first = window_start(query, dil)
    return first <= key // dil < first + KER


@functools.lru_cache(None)
def static_maps(layer):
    dil = 1 + layer % 2
    order = row_order(layer)
    starts = np.zeros(GRID, np.int64)
    mask = np.zeros((TOK, KEYS), np.float32)
    for q0, nq, k0 in GROUPS[layer % 2]:
        for place in range(q0 // COLS, (q0 + nq) // COLS):
            qy = order[place]
            for j in range(8):
                ky = order[k0 // COLS + j]
                if not in_window(qy, ky, dil):
                    continue
                starts[place] = ky // dil - qy // dil + KER - 1 - j
                for x in range(GRID):
                    for kx in range(GRID):
                        if in_window(x, kx, dil):
                            mask[place * COLS + x, j * COLS + kx] = 1.0
    shifts = np.zeros((COLS, KEYS, KEYS), np.float32)
    for x in range(GRID):
        for kx in range(GRID):
            if in_window(x, kx, dil):
                dx = kx // dil - x // dil + KER - 1
                for j in range(8):
                    shifts[x, j * COLS + dx, j * COLS + kx] = 1.0
    return starts, shifts, mask


def norm_stats(values):
    centred = values - jnp.mean(values, axis=-1, keepdims=True)
    rstd = lax.rsqrt(jnp.mean(centred * centred, axis=-1, keepdims=True) + EPSILON)
    return centred * rstd, rstd


def norm_back(grad, xhat, rstd, gain):
    scaled = grad * gain
    mean_one = jnp.mean(scaled, axis=-1, keepdims=True)
    mean_two = jnp.mean(scaled * xhat, axis=-1, keepdims=True)
    return rstd * (scaled - mean_one - xhat * mean_two)


def col_sum(values):
    return jnp.sum(values, axis=0, keepdims=True)


def dot_nn(a, b, **kw):
    return lax.dot_general(a, b, (((1,), (0,)), ((), ())), preferred_element_type=F32, **kw)


def dot_nt(a, b, **kw):
    return lax.dot_general(a, b, (((1,), (1,)), ((), ())), preferred_element_type=F32, **kw)


def dot_tn(a, b, **kw):
    return lax.dot_general(a, b, (((0,), (0,)), ((), ())), preferred_element_type=F32, **kw)


ERFC_T = 0.44
ERFC_POLY = (
    0.24822096599679971,
    0.24887097779118345,
    0.21731489562842682,
    0.21580753897325447,
    -0.020171305217729862,
    0.2966767736009737,
    -0.2779414931115683,
    0.07122182759012696,
)


def gelu_parts(x):
    bell = jnp.exp(-0.5 * x * x)
    t = 1.0 / (1.0 + (ERFC_T * 0.5**0.5) * jnp.abs(x))
    poly = jnp.full_like(t, 0.5 * ERFC_POLY[-1])
    for c in ERFC_POLY[-2::-1]:
        poly = poly * t + 0.5 * c
    tail = poly * t * bell
    cdf = jnp.where(x < 0, tail, 1.0 - tail)
    return x * cdf, cdf + x * bell * (1.0 / (2.0 * np.pi) ** 0.5)


def head_masks():
    lane = lax.broadcasted_iota(jnp.int32, (1, HALF), 1)
    return [jnp.where(lane // HEAD == h, 1.0, 0.0).astype(BF16) for h in range(4)]


def spread_heads(block, masks):
    return jnp.concatenate([block * m for m in masks], axis=0)


def whole(shape):
    return pl.BlockSpec(shape, lambda *_: (0,) * len(shape))


def params(n=1):
    return pltpu.CompilerParams(
        dimension_semantics=("arbitrary",) * n, vmem_limit_bytes=VMEM_LIMIT
    )


def cost(micros):
    return pl.CostEstimate(flops=int(micros * 1.1e9), bytes_accessed=0, transcendentals=0)


def call(name, kernel, steps, me, ins, outs, scratch, micros):
    names = ["me", *[e[0] for e in ins], *[e[0] for e in outs], *[e[0] for e in scratch]]

    def body(*refs):
        kernel(types.SimpleNamespace(**dict(zip(names, refs, strict=True))))

    results = pl.pallas_call(
        body,
        grid_spec=pltpu.PrefetchScalarGridSpec(
            num_scalar_prefetch=1,
            grid=(steps,),
            in_specs=[e[2] or whole(e[1].shape) for e in ins],
            out_specs=[e[3] or whole(e[1]) for e in outs],
            scratch_shapes=[pltpu.VMEM(e[1], e[2]) for e in scratch],
        ),
        out_shape=[jax.ShapeDtypeStruct(e[1], e[2]) for e in outs],
        compiler_params=params(),
        cost_estimate=cost(micros),
        name=name,
    )(me, *[e[1] for e in ins])
    return types.SimpleNamespace(**dict(zip([e[0] for e in outs], results, strict=True)))


def patch_kernel(feat_ref, out_ref, wide_ref, patch_ref):
    @pl.when(pl.program_id(0) == 0)
    def _():
        patch_ref[...] = jnp.zeros_like(patch_ref)

    for item in range(feat_ref.shape[0]):
        wide_ref[item, :, 0 : 2 * GRID, :] = feat_ref[item].astype(F32)
        even = wide_ref[item, :, pl.ds(0, GRID, stride=2), :]
        odd = wide_ref[item, :, pl.ds(1, GRID, stride=2), :]
        patch_ref[item, :, 1 : GRID + 1, 0:CIN] = odd
        patch_ref[item, :, 0:GRID, CIN : 2 * CIN] = even
        patch_ref[item, :, 0:GRID, 2 * CIN : 3 * CIN] = odd
        both = patch_ref[item].astype(BF16).reshape(GRID, 2, COLS, PARTS)
        for par in range(2):
            out_ref[item, par] = both[:, par].reshape(TOK, PARTS)


def make_patches(features):
    slots = features.shape[0]
    items = max(n for n in (1, 2, 3, 4) if slots % n == 0)
    return pl.pallas_call(
        patch_kernel,
        grid=(slots // items,),
        in_specs=[pl.BlockSpec((items, 2 * GRID, 2 * GRID, CIN), lambda i: (i, 0, 0, 0))],
        out_specs=pl.BlockSpec((items, 2, TOK, PARTS), lambda i: (i, 0, 0, 0)),
        out_shape=jax.ShapeDtypeStruct((slots, 2, TOK, PARTS), BF16),
        scratch_shapes=[
            pltpu.VMEM((items, 2 * GRID, 32, CIN), F32),
            pltpu.VMEM((items, 2 * GRID, COLS, PARTS), F32),
        ],
        compiler_params=params(),
        cost_estimate=cost(7),
        name="patches",
    )(features)


WIDE = 16 * COLS


def split_three(x):
    high = x.astype(BF16).astype(F32)
    mid = (x - high).astype(BF16).astype(F32)
    return jnp.concatenate([high, mid, x - high - mid], axis=0).astype(BF16)


def exact_dot(dot, x, hot):
    n = x.shape[0]
    out = dot(split_three(x), hot)
    return out[0:n] + out[n : 2 * n] + out[2 * n : 3 * n]


def shift_arrays():
    maps = [static_maps(layer) for layer in range(LAYERS)]
    return jnp.asarray(np.stack([m[1] for m in maps]), BF16), jnp.asarray(np.stack([m[2] for m in maps]))


def make_bias(me, tables):
    shifts, masks = shift_arrays()

    def kernel(r):
        for layer in range(LAYERS):

            @pl.when(pl.program_id(0) == layer)
            def _():
                for y, start in enumerate(static_maps(layer)[0]):
                    moved = pltpu.roll(r.table[0], int(-COLS * start) % WIDE, 1)
                    r.rows[pl.ds(y, HEADS, stride=GRID), :] = moved[:, :KEYS]

        rows = r.rows[...]
        for x in range(GRID):
            r.flat[pl.ds(x, HEADS * GRID, stride=COLS), :] = exact_dot(dot_nn, rows, r.shift[0, x])
        for x in range(GRID, COLS):
            r.flat[pl.ds(x, HEADS * GRID, stride=COLS), :] = jnp.zeros((HEADS * GRID, KEYS), F32)
        for h in range(HEADS):
            block = r.flat[h * TOK : (h + 1) * TOK, :]
            r.out[0, h] = jnp.where(r.mask[0] > 0.5, block, MASKED)

    return call(
        "bias",
        kernel,
        LAYERS,
        me,
        [
            ("table", tables, pl.BlockSpec((1, HEADS, WIDE), lambda i, *_: (i, 0, 0))),
            ("shift", shifts, pl.BlockSpec((1, COLS, KEYS, KEYS), lambda i, *_: (i, 0, 0, 0))),
            ("mask", masks, pl.BlockSpec((1, TOK, KEYS), lambda i, *_: (i, 0, 0))),
        ],
        [
            (
                "out",
                (LAYERS, HEADS, TOK, KEYS),
                F32,
                pl.BlockSpec((1, HEADS, TOK, KEYS), lambda i, *_: (i, 0, 0, 0)),
            )
        ],
        [("flat", (HEADS * TOK, KEYS), F32), ("rows", (HEADS * GRID, KEYS), F32)],
        5,
    ).out


def table_grads(me, zero, one):
    shifts, _ = shift_arrays()

    def kernel(r):
        for layer, (grad, out) in enumerate(((r.grad0, r.out0), (r.grad1, r.out1))):
            total = None
            for x in range(GRID):
                part = grad[pl.ds(x, HEADS * GRID, stride=COLS), :]
                part = exact_dot(dot_nt, part, r.shift[layer, x])
                total = part if total is None else total + part
            r.rows[...] = total
            result = None
            for y, start in enumerate(static_maps(layer)[0]):
                part = pad_lanes(r.rows[pl.ds(y, HEADS, stride=GRID), :], WIDE)
                moved = pltpu.roll(part, int(COLS * start) % WIDE, 1)
                result = moved if result is None else result + moved
            out[...] = result

    out = call(
        "tables",
        kernel,
        1,
        me,
        [("grad0", zero, None), ("grad1", one, None), ("shift", shifts, None)],
        [("out0", (HEADS, WIDE), F32, None), ("out1", (HEADS, WIDE), F32, None)],
        [("rows", (HEADS * GRID, KEYS), F32)],
        6,
    )
    return out.out0, out.out1


def pieces_of(shards, group):
    narrow, wide = D // shards, FF // shards
    sizes = [("qkv", narrow, 3), ("proj", narrow, 1), ("up", narrow, 3), ("down", wide, 1)]
    if group == 0:
        sizes = [("conv", 9 * CIN // shards, 1)] + sizes
    else:
        sizes = sizes + [("head", narrow, 4)]
    out, at = {}, 0
    for name, rows, blocks in sizes:
        out[name] = (at, rows, blocks)
        at += rows * blocks
    return out, at


SHARDS = 8
COUNT_ROWS = 16
NAMES = ("conv", "qkv", "proj", "up", "down", "head")
WHOLE_NAMES = ("conv", "head")


def pack(parts):
    out = []
    for part in parts:
        if part.shape[1] == CLASSES:
            part = jnp.pad(part, ((0, 0), (0, CPAD - CLASSES)))
        out += [part[:, c : c + D] for c in range(0, part.shape[1], D)]
    return jnp.concatenate(out, axis=0)


def pack_weights(weights, counts):
    def kernel(r):
        for group, packed in ((0, r.packed0), (1, r.packed1)):
            for name, (at, rows, blocks) in pieces_of(SHARDS, group)[0].items():
                ref = getattr(r, name)
                for c in range(blocks):
                    width = min(D, ref.shape[-1] - c * D)
                    cols = slice(c * D, c * D + width)
                    value = ref[:, cols] if name in WHOLE_NAMES else ref[group, :, cols]
                    value = value.astype(BF16)
                    if width < D:
                        value = jnp.concatenate([value, jnp.zeros((rows, D - width), BF16)], axis=1)
                    packed[at + c * rows : at + (c + 1) * rows, :] = value
        end = pieces_of(SHARDS, 0)[1]
        r.packed0[end : end + COUNT_ROWS, :] = jnp.broadcast_to(r.count[...].astype(F32), (COUNT_ROWS, D)).astype(BF16)

    ends = [pieces_of(SHARDS, group)[1] for group in range(2)]
    out = call(
        "pack",
        kernel,
        1,
        jnp.zeros((1,), jnp.int32),
        [*[(n, w, None) for n, w in zip(NAMES, weights)], ("count", counts, None)],
        [("packed0", (ends[0] + COUNT_ROWS, D), BF16, None), ("packed1", (ends[1], D), BF16, None)],
        [],
        2,
    )
    return out.packed0, out.packed1


def unpack_weights(me, sources, targets, group):
    layout, _ = pieces_of(SHARDS, group)
    for ref, low, high, offsets in sources:
        for p, offset in enumerate(offsets):
            owner = me ^ offset
            for name, target in targets.items():
                at, rows, blocks = layout[name]
                if not low <= at < high:
                    continue
                place = pl.ds(pl.multiple_of(owner * rows, 16), rows)
                for c in range(blocks):
                    first = at - low + c * rows
                    target[place, c * D : (c + 1) * D] = ref[p, first : first + rows, :]


def units(layer, items):
    return [(n, n * TOK, group, hf) for n in range(items) for group in GROUPS[layer] for hf in range(2)]


def lanes_of(which, hf):
    return slice(which * D + hf * HALF, which * D + (hf + 1) * HALF)


def scores_of(hf):
    return slice(hf * 4 * KEYS, (hf + 1) * 4 * KEYS)


def attend(layer, items, joined_ref, bias_ref, probs_ref, mixed_ref):
    masks = head_masks()
    for item, base, (q0, nq, k0), hf in units(layer, items):
        query = joined_ref[base + q0 : base + q0 + nq, lanes_of(0, hf)]
        keys = spread_heads(joined_ref[base + k0 : base + k0 + KEYS, lanes_of(1, hf)], masks)
        probs_ref[item, q0 : q0 + nq, scores_of(hf)] = dot_nt(query, keys)
    for item in range(items):
        for q0, nq, k0 in GROUPS[layer]:
            for head in range(HEADS):
                place = (item, slice(q0, q0 + nq), slice(head * KEYS, (head + 1) * KEYS))
                s = probs_ref[place] * SCALE + bias_ref[0, head, q0 : q0 + nq, :]
                e = jnp.exp(s - jnp.max(s, axis=-1, keepdims=True))
                probs_ref[place] = e * (1.0 / jnp.sum(e, axis=-1, keepdims=True))
    for item, base, (q0, nq, k0), hf in units(layer, items):
        values = spread_heads(joined_ref[base + k0 : base + k0 + KEYS, lanes_of(2, hf)], masks)
        mixed = dot_nn(probs_ref[item, q0 : q0 + nq, scores_of(hf)].astype(BF16), values)
        mixed_ref[base + q0 : base + q0 + nq, lanes_of(0, hf)] = mixed.astype(BF16)


def layer_forward(layer, hidden, vec_ref, weights, bias_ref, outs, items):
    joined_ref, probs_ref, mixed_ref, after_ref, slope_ref, active_ref = outs
    vec = lambda i: vec_ref[LAYER_AT[layer] + i : LAYER_AT[layer] + i + 1, :]
    xhat, _ = norm_stats(hidden)
    normed = (xhat * vec(0) + vec(1)).astype(BF16)
    for c in range(3):
        part = dot_nn(normed, weights["qkv"][:, c * D : (c + 1) * D])
        if c != 1:
            part = part + vec(2 if c == 0 else 3)
        joined_ref[:, c * D : (c + 1) * D] = part.astype(BF16)
    attend(layer, items, joined_ref, bias_ref, probs_ref, mixed_ref)
    after = hidden + (dot_nn(mixed_ref[...], weights["proj"][...]) + vec(4))
    after_ref[...] = after
    xhat, _ = norm_stats(after)
    normed = (xhat * vec(5) + vec(6)).astype(BF16)
    total = None
    for c in range(3):
        pre = dot_nn(normed, weights["up"][:, c * D : (c + 1) * D]) + vec(8 + c)
        active, slope = gelu_parts(pre)
        active = active.astype(BF16)
        slope_ref[:, c * D : (c + 1) * D] = slope
        active_ref[:, c * D : (c + 1) * D] = active
        part = dot_nn(active, weights["down"][c * D : (c + 1) * D, :])
        total = part if total is None else total + part
    return after + (total + vec(7))


def conv_taps(patch_ref, item):
    odd = patch_ref[item, 1]
    up = jnp.concatenate([jnp.zeros((COLS, PARTS), BF16), odd[: TOK - COLS]], axis=0)
    return up, patch_ref[item, 0], odd


CACHE = (
    ("joined", 3 * D, BF16),
    ("probs", None, F32),
    ("mixed", D, BF16),
    ("after", D, F32),
    ("slope", FF, F32),
    ("active", FF, BF16),
)
MATRICES = (("qkv", (D, FF)), ("proj", (D, D)), ("up", (D, FF)), ("down", (FF, D)))
MATRIX_NAMES = [m[0] for m in MATRICES]


def token_spec(items, width=D):
    return pl.BlockSpec((items * TOK, width), lambda i, *_: (i, 0))


def cache_entries(slots, items):
    out = []
    for name, width, dtype in CACHE:
        if width is None:
            spec = pl.BlockSpec((items, TOK, HEADS * KEYS), lambda i, *_: (i, 0, 0))
            out.append((name, (slots, TOK, HEADS * KEYS), dtype, spec))
        else:
            out.append((name, (slots * TOK, width), dtype, token_spec(items, width)))
    return out


def caches_of(r):
    return tuple(getattr(r, entry[0]) for entry in CACHE)


def bias_spec(layer):
    return pl.BlockSpec((1, HEADS, TOK, KEYS), lambda i, *_: (layer, 0, 0, 0))


def patch_spec(items):
    return pl.BlockSpec((items, 2, TOK, PARTS), lambda i, *_: (i, 0, 0, 0))


def source_entries(sources):
    return [(f"source{i}", array, None) for i, (array, *_) in enumerate(sources)]


def sources_of(r, sources):
    return [(getattr(r, f"source{i}"), *entry[1:]) for i, entry in enumerate(sources)]


def count_of(sources):
    total = jnp.zeros((1, 1), F32)
    for ref, _, high, offsets in sources:
        if ref.shape[1] > high:
            for p in range(len(offsets)):
                total = total + ref[p, high : high + COUNT_ROWS, :].astype(F32)[0:1, 0:1]
    return total


CONV_AT, LAYER_AT, FINAL_AT, BIAS_AT = 0, (3, 14), 25, 27


def forward_zero(me, patches, sources, vecs, bias, items):
    slots = patches.shape[0]

    def kernel(r):
        names = ["conv_w", *MATRIX_NAMES]
        weights = {n: getattr(r, n) for n in names}

        @pl.when(pl.program_id(0) == 0)
        def _():
            targets = {n.removesuffix("_w"): ref for n, ref in weights.items()}
            unpack_weights(r.me[0], sources_of(r, sources), targets, 0)
            r.count[...] = jnp.broadcast_to(count_of(sources_of(r, sources)), r.count.shape)

        for item in range(items):
            taps = conv_taps(r.patch, item)
            total = None
            for a in range(3):
                part = dot_nn(taps[a], r.conv_w[a * PARTS : (a + 1) * PARTS, :])
                total = part if total is None else total + part
            r.conv[item * TOK : (item + 1) * TOK, :] = total + r.vecs[CONV_AT : CONV_AT + 1, :]
        xhat, _ = norm_stats(r.conv[...])
        hidden = xhat * r.vecs[CONV_AT + 1 : CONV_AT + 2, :] + r.vecs[CONV_AT + 2 : CONV_AT + 3, :]
        hidden = layer_forward(0, hidden, r.vecs, weights, r.bias, caches_of(r), items)
        for item in range(items):
            for place, row in enumerate(row_order(1)):
                r.hidden[item * TOK + place * COLS : item * TOK + (place + 1) * COLS, :] = hidden[
                    item * TOK + row * COLS : item * TOK + (row + 1) * COLS
                ]

    return call(
        "fwd0",
        kernel,
        slots // items,
        me,
        [
            ("patch", patches, patch_spec(items)),
            *source_entries(sources),
            ("vecs", vecs, None),
            ("bias", bias, bias_spec(0)),
        ],
        [
            ("hidden", (slots * TOK, D), F32, token_spec(items)),
            ("conv", (slots * TOK, D), F32, token_spec(items)),
            *cache_entries(slots, items),
            *[(n, shape, BF16, None) for n, shape in MATRICES],
            ("count", (8, 128), F32, None),
        ],
        [("conv_w", (9 * CIN, D), BF16)],
        54,
    )


def real_cells():
    place = lax.broadcasted_iota(jnp.int32, (TOK, 1), 0)
    return jnp.where(place % COLS < GRID, 1.0, 0.0)


def classify(r, slots, counts):
    rows = r.pooled.shape[0]
    place = lax.broadcasted_iota(jnp.int32, (rows, 1), 0)
    label = jnp.full((rows, 1), -1, jnp.int32)
    for i in range(slots):
        label = jnp.where(place == i, r.me[2 + i], label)
    live = jnp.where(place < r.me[1], 1.0, 0.0)
    count = sum([getattr(r, f"count{i}")[0:1, 0:1] for i in range(counts)])
    pooled = r.pooled[...].astype(BF16)
    head_bias = jnp.concatenate([r.vecs[BIAS_AT + c : BIAS_AT + c + 1, :] for c in range(CPAD // D)], axis=1)
    logits = dot_nn(pooled, r.head[...]) + head_bias
    peak = jnp.max(logits, axis=-1, keepdims=True)
    log_total = peak + jnp.log(jnp.sum(jnp.exp(logits - peak), axis=-1, keepdims=True))
    lane = lax.broadcasted_iota(jnp.int32, logits.shape, 1)
    onehot = jnp.where(label == lane, 1.0, 0.0)
    picked = jnp.sum(onehot * logits, axis=-1, keepdims=True)
    loss = col_sum(live * (log_total - picked))
    r.sums[0:8, :] = jnp.broadcast_to(loss, (8, 128))
    r.sums[8:16, :] = jnp.broadcast_to(count, (8, 128))
    d_logits = (jnp.exp(logits - log_total) - onehot) * ((1.0 / count) * live)
    d_logits = jnp.where(lane < CLASSES, d_logits, 0.0).astype(BF16)
    r.head_grad[...] = dot_tn(pooled, d_logits)
    r.hb_grad[...] = col_sum(d_logits.astype(F32))
    r.d_pooled[...] = dot_nt(d_logits, r.head[...]) * (1.0 / PIX)


def forward_one(me, hidden, sources, vecs, bias, items):
    slots = hidden.shape[0] // TOK
    rows = -(-slots // 16) * 16

    def kernel(r):
        weights = {n: getattr(r, n) for n in MATRIX_NAMES}
        step = pl.program_id(0)

        @pl.when(step == 0)
        def _():
            unpack_weights(r.me[0], sources_of(r, sources), weights | dict(head=r.head), 1)
            r.pooled[...] = jnp.zeros_like(r.pooled)

        out = layer_forward(1, r.hidden[...], r.vecs, weights, r.bias, caches_of(r), items)
        r.out[...] = out
        xhat, _ = norm_stats(out)
        normed = xhat * r.vecs[FINAL_AT : FINAL_AT + 1, :] + r.vecs[FINAL_AT + 1 : FINAL_AT + 2, :]
        real = real_cells()
        for item in range(items):
            mean = col_sum(normed[item * TOK : (item + 1) * TOK] * real) * (1.0 / PIX)
            r.pooled[pl.ds(step * items + item, 1), :] = mean

    return call(
        "fwd1",
        kernel,
        slots // items,
        me,
        [
            ("hidden", hidden, token_spec(items)),
            *source_entries(sources),
            ("vecs", vecs, None),
            ("bias", bias, bias_spec(1)),
        ],
        [
            ("out", (slots * TOK, D), F32, token_spec(items)),
            *cache_entries(slots, items),
            *[(n, shape, BF16, None) for n, shape in MATRICES],
            ("head", (D, CPAD), BF16, None),
            ("pooled", (rows, D), F32, None),
        ],
        [],
        42,
    )


def attend_back(layer, items, joined_ref, probs_ref, dmix_ref, djoin_ref, dkv_ref, dprob_ref, dscore_ref, bgrad_ref):
    masks = head_masks()
    for item, base, (q0, nq, k0), hf in units(layer, items):
        values = spread_heads(joined_ref[base + k0 : base + k0 + KEYS, lanes_of(2, hf)], masks)
        d_mix = dmix_ref[base + q0 : base + q0 + nq, lanes_of(0, hf)]
        dprob_ref[item, q0 : q0 + nq, scores_of(hf)] = dot_nt(d_mix, values)
    for q0, nq, k0 in GROUPS[layer]:
        for head in range(HEADS):
            total = None
            for item in range(items):
                place = (item, slice(q0, q0 + nq), slice(head * KEYS, (head + 1) * KEYS))
                p, dp = probs_ref[place], dprob_ref[place]
                ds = (p * (dp - jnp.sum(dp * p, axis=-1, keepdims=True))).astype(BF16)
                dscore_ref[place] = ds
                ds = ds.astype(F32)
                total = ds if total is None else total + ds
            bgrad_ref[head * TOK + q0 : head * TOK + q0 + nq, :] += total
    for item, base, (q0, nq, k0), hf in units(layer, items):
        keys = spread_heads(joined_ref[base + k0 : base + k0 + KEYS, lanes_of(1, hf)], masks)
        d_query = dot_nn(dscore_ref[item, q0 : q0 + nq, scores_of(hf)], keys) * SCALE
        djoin_ref[base + q0 : base + q0 + nq, lanes_of(0, hf)] = d_query.astype(BF16)
    dkv_ref[...] = jnp.zeros_like(dkv_ref)
    for item, base, (q0, nq, k0), hf in units(layer, items):
        qrows, krows = slice(base + q0, base + q0 + nq), slice(base + k0, base + k0 + KEYS)
        heads = [slice(h * KEYS, (h + 1) * KEYS) for h in range(hf * 4, hf * 4 + 4)]
        stacked = jnp.concatenate([dscore_ref[item, q0 : q0 + nq, h] for h in heads], axis=0)
        query = spread_heads(joined_ref[qrows, lanes_of(0, hf)], masks)
        dkv_ref[krows, lanes_of(0, hf)] += dot_tn(stacked, query)
        stacked = jnp.concatenate([probs_ref[item, q0 : q0 + nq, h].astype(BF16) for h in heads], axis=0)
        d_mix = spread_heads(dmix_ref[qrows, lanes_of(0, hf)], masks)
        dkv_ref[krows, lanes_of(1, hf)] += dot_tn(stacked, d_mix)
    djoin_ref[:, D : 2 * D] = (dkv_ref[:, 0:D] * SCALE).astype(BF16)
    djoin_ref[:, 2 * D : 3 * D] = dkv_ref[:, D : 2 * D].astype(BF16)


def layer_backward(layer, d_out, hidden, vec_ref, weights, caches, work, grads, vgrad_ref, bgrad_ref, items):
    joined_ref, probs_ref, mixed_ref, after_ref, slope_ref, active_ref = caches
    dmix_ref, djoin_ref, dkv_ref, dprob_ref, dscore_ref = work
    vec = lambda i: vec_ref[LAYER_AT[layer] + i : LAYER_AT[layer] + i + 1, :]

    def add(row, value):
        vgrad_ref[row : row + 1, :] += value

    d_branch = d_out.astype(BF16)
    add(7, col_sum(d_branch.astype(F32)))
    xhat, rstd = norm_stats(after_ref[...])
    normed = (xhat * vec(5) + vec(6)).astype(BF16)
    d_normed = None
    for c in range(3):
        cols = slice(c * D, (c + 1) * D)
        grads["down"][:, cols] += dot_tn(d_branch, active_ref[:, cols])
        d_active = dot_nt(d_branch, weights["down"][cols, :])
        d_pre = (d_active * slope_ref[:, cols]).astype(BF16)
        add(8 + c, col_sum(d_pre.astype(F32)))
        grads["up"][:, cols] += dot_tn(normed, d_pre)
        part = dot_nt(d_pre, weights["up"][:, cols])
        d_normed = part if d_normed is None else d_normed + part
    add(5, col_sum(d_normed * xhat))
    add(6, col_sum(d_normed))
    d_after = d_out + norm_back(d_normed, xhat, rstd, vec(5))
    d_proj = d_after.astype(BF16)
    add(4, col_sum(d_proj.astype(F32)))
    grads["proj"][...] += dot_tn(mixed_ref[...], d_proj)
    dmix_ref[...] = dot_nt(d_proj, weights["proj"][...]).astype(BF16)
    attend_back(layer, items, joined_ref, probs_ref, *work, bgrad_ref)
    add(2, col_sum(djoin_ref[:, 0:D].astype(F32)))
    add(3, col_sum(djoin_ref[:, 2 * D : 3 * D].astype(F32)))
    xhat, rstd = norm_stats(hidden)
    normed = (xhat * vec(0) + vec(1)).astype(BF16)
    d_normed = None
    for c in range(3):
        cols = slice(c * D, (c + 1) * D)
        grads["qkv"][:, cols] += dot_tn(normed, djoin_ref[:, cols])
        part = dot_nt(djoin_ref[:, cols], weights["qkv"][:, cols])
        d_normed = part if d_normed is None else d_normed + part
    add(0, col_sum(d_normed * xhat))
    add(1, col_sum(d_normed))
    return d_after + norm_back(d_normed, xhat, rstd, vec(0))


def split_two(x):
    high = x.astype(BF16)
    return high, (x - high.astype(F32)).astype(BF16)


def wide_dot(dot, rows, matrix):
    stacked = split_three(rows)
    high, low = split_two(matrix)
    out = dot(stacked, high) + dot(stacked, low)
    return out[0:RANK] + out[RANK : 2 * RANK] + out[2 * RANK : 3 * RANK]


def block_of(whole_ref, entry, c):
    at, rows, _ = entry
    return jnp.concatenate(
        [whole_ref[s, at + c * rows : at + (c + 1) * rows, :] for s in range(SHARDS)], axis=0
    )


def factor_of(r, group, name):
    ref = getattr(r, "fac_" + name)
    return ref[...] if name in WHOLE_NAMES else ref[group]


def finish_grads(r, group, grads):
    layout, _ = pieces_of(SHARDS, group)
    me = r.me[0]
    for name, (at, rows, blocks) in layout.items():
        matrix = grads[name]
        if name in ("down", "conv"):
            matrix = jnp.transpose(matrix[...])
        for s in range(SHARDS):
            for c in range(blocks):
                piece = matrix[s * rows : (s + 1) * rows, c * D : (c + 1) * D]
                r.whole[s, at + c * rows : at + (c + 1) * rows, :] = piece
    for name, (at, rows, blocks) in layout.items():
        err = getattr(r, "err_" + name)
        for c in range(blocks):
            width = min(D, err.shape[-1] - c * D)
            cols = slice(c * D, c * D + width)
            value = err[0, :, cols] if name in WHOLE_NAMES else err[0, group, :, cols]
            place = slice(at + c * rows, at + (c + 1) * rows)
            r.whole[me, place, 0:width] += value
    r.own[...] = r.whole[me]
    if group == 0:
        for i, chip in enumerate((0, 2, 4, 6)):
            r.far[i] = r.whole[me ^ chip ^ 1].astype(BF16)
            if chip:
                r.near[i - 1] = r.whole[me ^ chip].astype(BF16)
    else:
        r.sent1[...] = r.whole[me ^ 1].astype(BF16)
        for chip in (2, 4, 6):
            for core in range(2):
                getattr(r, f"sent{chip}")[core] = r.whole[me ^ chip ^ core].astype(BF16)
    at_lane, lefts = 0, []
    for name, entry in layout.items():
        total = None
        for c in range(entry[2]):
            fac = factor_of(r, group, name)
            width = min(D, fac.shape[-1] - c * D)
            block = block_of(r.whole, entry, c)
            part = wide_dot(dot_nt, fac[:, c * D : c * D + width], block[:, :width])
            total = part if total is None else total + part
        lefts.append(total)
    return jnp.concatenate(lefts, axis=1)


def left_lanes(group):
    return sum(rows * SHARDS for _, rows, _ in pieces_of(SHARDS, group)[0].values())


def right_lanes(group):
    return sum(blocks * D for _, _, blocks in pieces_of(SHARDS, group)[0].values())


SMALLS = 2 * 512 + 128 + 128
HALF_LEFT = (left_lanes(0) + left_lanes(1) + SMALLS) // 2
HALF_RIGHT = (right_lanes(0) + right_lanes(1) + 2 * WIDE) // 2


def pad_lanes(x, lanes):
    return jnp.concatenate([x, jnp.zeros((x.shape[0], lanes - x.shape[1]), x.dtype)], axis=1)


def put_halves(r, whole):
    n = whole.shape[1] // 2
    first, second = whole[:, :n], whole[:, n:]
    odd = (r.me[0] & 1) == 1
    r.mine[...] = jnp.where(odd, second, first)
    r.other[...] = jnp.where(odd, first, second)


def get_halves(r, mine, other):
    odd = (r.me[0] & 1) == 1
    mine, other = mine[...], other[...]
    return jnp.concatenate([jnp.where(odd, other, mine), jnp.where(odd, mine, other)], axis=1)


def backward_outs(group):
    rows = pieces_of(SHARDS, group)[1]
    return [
        ("vgrad", (16, D), F32, None),
        ("bgrad", (HEADS * TOK, KEYS), F32, None),
        ("whole", (SHARDS, rows, D), F32, None),
        ("own", (rows, D), F32, None),
    ]


def factor_inputs(group, errs, facs):
    out = []
    for name, err, fac in zip(NAMES, errs, facs):
        if name in pieces_of(SHARDS, group)[0]:
            out += [("err_" + name, err, None), ("fac_" + name, fac, None)]
    return out


def backward_scratch(items):
    return [
        ("d_mixed", (items * TOK, D), BF16),
        ("d_joined", (items * TOK, 3 * D), BF16),
        ("d_keys", (items * TOK, 2 * D), F32),
        ("d_probs", (items, TOK, HEADS * KEYS), F32),
        ("d_scores", (items, TOK, HEADS * KEYS), BF16),
        ("g_qkv", (D, FF), F32),
        ("g_proj", (D, D), F32),
        ("g_up", (D, FF), F32),
        ("g_down", (D, FF), F32),
    ]


def start_backward(r, grads):
    r.vgrad[...] = jnp.zeros_like(r.vgrad)
    r.bgrad[...] = jnp.zeros_like(r.bgrad)
    for ref in grads.values():
        ref[...] = jnp.zeros_like(ref)


def cache_inputs(caches, slots, items):
    return [(e[0], getattr(caches, e[0]), e[3]) for e in cache_entries(slots, items)]


def matrix_inputs(caches):
    return [(n, getattr(caches, n), None) for n in MATRIX_NAMES]


def backward_one(me, hidden, forward, vecs, count, errs, facs, items):
    slots = hidden.shape[0] // TOK

    def kernel(r):
        weights = {n: getattr(r, n) for n in MATRIX_NAMES}
        grads = {n: getattr(r, "g_" + n) for n in MATRIX_NAMES}
        step = pl.program_id(0)

        @pl.when(step == 0)
        def _():
            start_backward(r, grads)
            classify(r, slots, len(count))

        real = real_cells()
        d_final = jnp.concatenate(
            [real * r.d_pooled[pl.ds(step * items + item, 1), :] for item in range(items)], axis=0
        )
        xhat, rstd = norm_stats(r.out[...])
        r.vgrad[11:12, :] += col_sum(d_final * xhat)
        r.vgrad[12:13, :] += col_sum(d_final)
        d_out = norm_back(d_final, xhat, rstd, r.vecs[FINAL_AT : FINAL_AT + 1, :])
        work = (r.d_mixed, r.d_joined, r.d_keys, r.d_probs, r.d_scores)
        r.d_hidden[...] = layer_backward(
            1, d_out, r.hidden[...], r.vecs, weights, caches_of(r), work, grads, r.vgrad, r.bgrad, items
        )

        @pl.when(step == pl.num_programs(0) - 1)
        def _():
            r.left[...] = finish_grads(r, 1, grads | dict(head=r.head_grad))

    return call(
        "back1",
        kernel,
        slots // items,
        me,
        [
            ("out", forward.out, token_spec(items)),
            ("pooled", forward.pooled, None),
            *[(f"count{i}", c, None) for i, c in enumerate(count)],
            ("hidden", hidden, token_spec(items)),
            *matrix_inputs(forward),
            ("head", forward.head, None),
            ("vecs", vecs, None),
            *cache_inputs(forward, slots, items),
            *factor_inputs(1, errs, facs),
        ],
        [
            ("d_hidden", hidden.shape, F32, token_spec(items)),
            *backward_outs(1),
            ("left", (RANK, left_lanes(1)), F32, None),
            ("sums", (16, 128), F32, None),
            ("hb_grad", (1, CPAD), F32, None),
            *[(f"sent{chip}", (2, pieces_of(SHARDS, 1)[1], D), BF16, None) for chip in (2, 4, 6)],
            ("sent1", (pieces_of(SHARDS, 1)[1], D), BF16, None),
        ],
        [*backward_scratch(items), ("head_grad", (D, CPAD), F32), ("d_pooled", forward.pooled.shape, F32)],
        46,
    )


def backward_zero(me, back_one, forward, patches, vecs, errs, facs, items):
    slots = patches.shape[0]

    def kernel(r):
        weights = {n: getattr(r, n) for n in MATRIX_NAMES}
        grads = {n: getattr(r, "g_" + n) for n in [*MATRIX_NAMES, "conv"]}
        step = pl.program_id(0)

        @pl.when(step == 0)
        def _():
            start_backward(r, grads)

        order = row_order(1)
        rows = []
        for item in range(items):
            for row in range(GRID):
                first = item * TOK + order.index(row) * COLS
                rows.append(r.d_hidden[first : first + COLS, :])
        d_out = jnp.concatenate(rows, axis=0)
        conv_hat, conv_rstd = norm_stats(r.conv[...])
        gain = r.vecs[CONV_AT + 1 : CONV_AT + 2, :]
        hidden = conv_hat * gain + r.vecs[CONV_AT + 2 : CONV_AT + 3, :]
        work = (r.d_mixed, r.d_joined, r.d_keys, r.d_probs, r.d_scores)
        d_conv = layer_backward(
            0, d_out, hidden, r.vecs, weights, caches_of(r), work, grads, r.vgrad, r.bgrad, items
        )
        r.vgrad[12:13, :] += col_sum(d_conv * conv_hat)
        r.vgrad[13:14, :] += col_sum(d_conv)
        d_conv = norm_back(d_conv, conv_hat, conv_rstd, gain).astype(BF16)
        r.vgrad[11:12, :] += col_sum(d_conv.astype(F32))
        for item in range(items):
            taps = conv_taps(r.patch, item)
            part = d_conv[item * TOK : (item + 1) * TOK]
            for a in range(3):
                grads["conv"][:, a * PARTS : (a + 1) * PARTS] += dot_tn(part, taps[a])

        @pl.when(step == pl.num_programs(0) - 1)
        def _():
            parts = [finish_grads(r, 0, grads), r.left_one[...]]
            for ref in (r.vgrad, r.vgrad_one):
                parts += [ref[0:8, :], ref[8:16, :]]
            put_halves(r, jnp.concatenate([*parts, r.head_bias[...], r.sums[0:8, :]], axis=1))

    return call(
        "back0",
        kernel,
        slots // items,
        me,
        [
            ("d_hidden", back_one.d_hidden, token_spec(items)),
            ("conv", forward.conv, token_spec(items)),
            ("patch", patches, patch_spec(items)),
            *matrix_inputs(forward),
            ("vecs", vecs, None),
            *cache_inputs(forward, slots, items),
            ("left_one", back_one.left, None),
            ("vgrad_one", back_one.vgrad, None),
            ("head_bias", back_one.hb_grad.reshape(8, 128), None),
            ("sums", back_one.sums, None),
            *factor_inputs(0, errs, facs),
        ],
        [
            *backward_outs(0),
            ("far", (4, pieces_of(SHARDS, 0)[1], D), BF16, None),
            ("near", (3, pieces_of(SHARDS, 0)[1], D), BF16, None),
            ("mine", (RANK, HALF_LEFT), F32, None),
            ("other", (RANK, HALF_LEFT), F32, None),
        ],
        [*backward_scratch(items), ("g_conv", (D, 9 * CIN), F32)],
        63,
    )


def inverse_cholesky(gram):
    row = lax.broadcasted_iota(jnp.int32, (1, RANK, 2 * RANK), 1)
    lane = lax.broadcasted_iota(jnp.int32, (1, RANK, 2 * RANK), 2)
    eye = jnp.broadcast_to(jnp.where(lane == row + RANK, 1.0, 0.0), (gram.shape[0], RANK, 2 * RANK))
    work = jnp.concatenate([gram, jnp.zeros_like(gram)], axis=2) + eye
    for k in range(RANK):
        scale = 1.0 / jnp.sqrt(work[:, k : k + 1, k : k + 1])
        pivot = work[:, k : k + 1, :] * scale
        column = work[:, :, k : k + 1] * scale
        work = jnp.where(row > k, work - column * pivot, jnp.where(row == k, pivot, work))
    return work[:, :, RANK : 2 * RANK]


def basis_lanes(group):
    return sum(rows for _, rows, _ in pieces_of(SHARDS, group)[0].values())


def right_factors(me, left, whole_zero, whole_one, tables):
    def kernel(r):
        groups = (r.whole0, r.whole1)
        left = get_halves(r, r.left_mine, r.left_other)
        entries, at = [], 0
        for group in range(2):
            for entry in pieces_of(SHARDS, group)[0].values():
                entries.append((group, entry, left[:, at : at + entry[1] * SHARDS]))
                at += entry[1] * SHARDS
        grams = jnp.stack([dot_nt(x, x, precision=PRECISE) for _, _, x in entries])
        inverses = inverse_cholesky(grams)
        rows_of = [[], []]
        parts = []
        for i, (group, entry, x) in enumerate(entries):
            basis = dot_nn(inverses[i], x, precision=PRECISE)
            rows_of[group].append((basis, entry[1]))
            for c in range(entry[2]):
                parts.append(wide_dot(dot_nn, basis, block_of(groups[group], entry, c)))
        for group, out in ((0, r.basis0), (1, r.basis1)):
            for s in range(SHARDS):
                at = 0
                for basis, rows in rows_of[group]:
                    out[s, :, at : at + rows] = basis[:, s * rows : (s + 1) * rows]
                    at += rows
        put_halves(r, jnp.concatenate([*parts, r.table0[...], r.table1[...]], axis=1))

    return call(
        "right",
        kernel,
        1,
        me,
        [
            ("left_mine", left[0], None),
            ("left_other", left[1], None),
            ("whole0", whole_zero, None),
            ("whole1", whole_one, None),
            ("table0", tables[0], None),
            ("table1", tables[1], None),
        ],
        [
            ("mine", (RANK, HALF_RIGHT), F32, None),
            ("other", (RANK, HALF_RIGHT), F32, None),
            ("basis0", (SHARDS, RANK, basis_lanes(0)), F32, None),
            ("basis1", (SHARDS, RANK, basis_lanes(1)), F32, None),
        ],
        [],
        8,
    )


def six_products(x, other):
    high = x.astype(BF16).astype(F32)
    mid = (x - high).astype(BF16).astype(F32)
    low = x - high - mid
    terms = [high, mid, high, mid, low, high] if other else [high, high, mid, mid, high, low]
    return jnp.concatenate(terms, axis=0).astype(BF16)


def apply_update(me, weights, moms, facs, right, factors, own, received):
    def kernel(r):
        right_mine = get_halves(r, r.rep_mine, r.rep_other)
        right_all = get_halves(r, r.all_mine, r.all_other)
        at_col = 0
        for group in range(2):
            total = getattr(r, f"own{group}")[...] + getattr(r, f"sib{group}")[0].astype(F32)
            for chip in (2, 4, 6):
                total = total + getattr(r, f"got{group}_{chip}")[0].astype(F32)
            basis = getattr(r, f"basis{group}")
            at_row = 0
            for name, (at, rows, blocks) in pieces_of(SHARDS, group)[0].items():
                left = six_products(basis[0, :, at_row : at_row + rows], False)
                at_row += rows
                single = name in WHOLE_NAMES
                for c in range(blocks):
                    width = min(D, (CLASSES if name == "head" else blocks * D) - c * D)
                    cols = slice(c * D, c * D + width)
                    place = (slice(None), cols) if single else (group, slice(None), cols)
                    err_place = (0, slice(None), cols) if single else (0, group, slice(None), cols)
                    right = slice(at_col, at_col + D)
                    at_col += D
                    getattr(r, "new_fac_" + name)[place] = right_all[:, right][:, :width]
                    mine = dot_tn(left, six_products(right_mine[:, right], True))
                    every = dot_tn(left, six_products(right_all[:, right], True))
                    merged = total[at + c * rows : at + (c + 1) * rows]
                    getattr(r, "err_" + name)[err_place] = (merged - mine)[:, :width]
                    mom = MOMENTUM * getattr(r, "mom_" + name)[place] + every[:, :width]
                    getattr(r, "new_mom_" + name)[place] = mom
                    getattr(r, "new_" + name)[place] = getattr(r, "w_" + name)[place] - LEARN_RATE * mom
        r.small[...] = right_all[:, at_col:]

    mine_spec = lambda x: pl.BlockSpec((1,) + x.shape[1:], lambda i, m: (m[0], 0, 0))
    small = 2 * HALF_RIGHT - right_lanes(0) - right_lanes(1)
    return call(
        "update",
        kernel,
        1,
        me,
        [
            *[("w_" + n, w, None) for n, w in zip(NAMES, weights)],
            *[("mom_" + n, m, None) for n, m in zip(NAMES, moms)],
            *zip(("rep_mine", "rep_other", "all_mine", "all_other"), right, [None] * 4),
            ("basis0", factors[0], mine_spec(factors[0])),
            ("basis1", factors[1], mine_spec(factors[1])),
            ("own0", own[0], None),
            ("own1", own[1], None),
            *[(f"got{g}_{chip}", received[g][chip], None) for g in range(2) for chip in (2, 4, 6)],
            *[(f"sib{g}", received[g][1], None) for g in range(2)],
        ],
        [
            *[("new_" + n, w.shape, F32, None) for n, w in zip(NAMES, weights)],
            *[("new_mom_" + n, w.shape, F32, None) for n, w in zip(NAMES, weights)],
            *[("err_" + n, (1,) + w.shape, F32, None) for n, w in zip(NAMES, weights)],
            *[("new_fac_" + n, f.shape, F32, None) for n, f in zip(NAMES, facs)],
            ("small", (RANK, small), F32, None),
        ],
        [],
        5,
    )


def swap(x, offset):
    return lax.ppermute(x, FSDP, [(i, i ^ offset) for i in range(SHARDS)])


def swap_by_core(x, even, odd):
    return lax.ppermute(x, FSDP, [(i, i ^ (odd if i & 1 else even)) for i in range(SHARDS)])


def swap_rep(x, offset, reps):
    return lax.ppermute(x, REP, [(i, i ^ offset) for i in range(reps)])


def gather_chips(packed):
    return [packed, *[swap(packed, chip) for chip in (2, 4, 6)]]


def with_sibling(near, end):
    near = jnp.stack(near)
    return [(near, 0, end, (0, 2, 4, 6)), (swap(near, 1), 0, end, (1, 3, 5, 7))]


def gather_pair(packed):
    return jnp.stack([packed, swap(packed, 1)])


def spread_pair(pair, end):
    out = [(pair, 0, end, (0, 1))]
    return out + [(swap(pair, chip), 0, end, (chip, chip ^ 1)) for chip in (2, 4, 6)]


def sum_replica(mine, other):
    mine = mine + swap(other, 1)
    mine = mine + swap_by_core(mine, 2, 4)
    return mine + swap_by_core(mine, 4, 2)


def sum_replicas(x, reps):
    bit = 1
    while bit < reps:
        x = x + swap_rep(x, bit, reps)
        bit *= 2
    return x


def scatter_chips(back):
    return {chip: swap(getattr(back, f"sent{chip}"), chip) for chip in (2, 4, 6)}


def scatter_cores(back, received):
    total = back.sent1.astype(F32)
    for chip in (2, 4, 6):
        total = total + received[chip][1].astype(F32)
    return received | {1: swap(total.astype(BF16), 1)[None]}


def scatter_cores_first(far, near):
    got = swap(far, 1)
    sums = {}
    for i, chip in enumerate((2, 4, 6)):
        sums[chip] = (near[i].astype(F32) + got[i + 1].astype(F32)).astype(BF16)[None]
    return got, sums


def table_at(layer):
    return 3 * D + layer * (11 * D + HEADS * RB)


def small_blocks(small):
    parts, tables = [small[: 3 * D]], []
    for layer in range(LAYERS):
        at = table_at(layer)
        parts.append(small[at : at + 11 * D])
        tables.append(small[at + 11 * D : at + 11 * D + HEADS * RB])
    parts += [small[table_at(LAYERS) :], jnp.full((CPAD - CLASSES,), -1e30, F32)]
    vecs = jnp.concatenate(parts)
    tables = jnp.stack(tables).reshape(LAYERS, HEADS, 2 * KER - 1, 2 * KER - 1)
    tables = jnp.pad(tables, ((0, 0), (0, 0), (0, 3), (0, 3))).reshape(LAYERS, HEADS, WIDE)
    return vecs.reshape(-1, D), tables


def small_vector(vgrads, tables, head_bias):
    parts = [vgrads[0][11:14].reshape(-1)]
    for layer in range(LAYERS):
        table = tables[layer].reshape(HEADS, 16, 16)[:, : 2 * KER - 1, : 2 * KER - 1]
        parts += [vgrads[layer][:11].reshape(-1), table.reshape(-1)]
    return jnp.concatenate([*parts, vgrads[1][11:13].reshape(-1), head_bias[:CLASSES]])


def group_parts(group, conv, qkv, proj, up, down, head):
    layer = [m[group] for m in (qkv, proj, up, down)]
    return [conv] + layer if group == 0 else layer + [head]


def step(mesh, args):
    (
        features, labels, counts, tables, *rest
    ) = args
    weights, moms, errs, facs = rest[0:6], rest[6:12], rest[12:18], rest[18:24]
    small_params, small_mom = rest[24:]
    reps = mesh.shape[REP]
    quick = mesh.shape[FSDP] == SHARDS and reps & (reps - 1) == 0
    slots = features.shape[0]
    items = max(n for n in (1, 2, 3) if slots % n == 0)

    if quick:
        ends = [pieces_of(SHARDS, group)[1] for group in range(2)]
        packed, second = pack_weights(weights, counts)
        near = gather_chips(packed)
        near[0], second, features, labels, counts, small_params = lax.optimization_barrier(
            (packed, second, features, labels, counts, small_params)
        )
        me = lax.axis_index(FSDP).astype(jnp.int32)[None]
        me = jnp.concatenate([me, counts[0], labels])
        sources0 = with_sibling(near, ends[0])
        pair, *held = lax.optimization_barrier((gather_pair(second), *[a for a, *_ in sources0]))
        sources0 = [(a, *entry[1:]) for a, entry in zip(held, sources0)]
        sources1 = spread_pair(pair, ends[1])
    else:
        me = jnp.concatenate([jnp.zeros((1,), jnp.int32), counts[0], labels])
        sides = [lax.all_gather(w.astype(BF16), FSDP, axis=w.ndim - 2, tiled=True) for w in weights]
        sources = []
        for group in range(2):
            parts = group_parts(group, *sides)
            shards = [pack([p.reshape(SHARDS, -1, p.shape[1])[s] for p in parts]) for s in range(SHARDS)]
            sources.append([(jnp.stack(shards), 0, shards[0].shape[0], tuple(range(SHARDS)))])
        sources0, sources1 = sources

    vecs, bias_tables = small_blocks(small_params)
    bias = make_bias(me, bias_tables)
    patches = make_patches(features)
    zero = forward_zero(me, patches, sources0, vecs, bias, items)
    one = forward_one(me, zero.hidden, sources1, vecs, bias, items)
    if quick:
        count = [zero.count, *[swap_rep(zero.count, offset, reps) for offset in range(1, reps)]]
        count, *held = lax.optimization_barrier((count, *vars(one).values()))
        one = types.SimpleNamespace(**dict(zip(vars(one), held)))
    else:
        count = [jnp.broadcast_to(lax.psum(counts.astype(F32), (REP, FSDP)), (8, 128))]
    turned = [jnp.swapaxes(f, -1, -2) for f in facs]
    own_errs = errs
    if not quick:
        own_errs = [jnp.zeros((1,) + (w.shape[:-2] + (full // SHARDS, w.shape[-1])), F32) for w, full in zip(weights, FULL_ROWS)]
    back_one = backward_one(me, zero.hidden, one, vecs, count, own_errs, turned, items)
    item_count = back_one.sums[8, 0]
    if quick:
        received = [None, scatter_chips(back_one)]
    back_zero = backward_zero(me, back_one, zero, patches, vecs, own_errs, turned, items)
    if quick:
        received[1], *held = lax.optimization_barrier((received[1], *vars(back_zero).values()))
        back_zero = types.SimpleNamespace(**dict(zip(vars(back_zero), held)))
    tables_grad = table_grads(me, back_zero.bgrad, back_one.bgrad)
    if not quick:
        grads = [whole_matrices(group, b.whole) for group, b in ((0, back_zero), (1, back_one))]
        small = small_vector((back_zero.vgrad, back_one.vgrad), tables_grad, back_one.hb_grad[0])
        loss = lax.psum(back_one.sums[0, 0], (REP, FSDP))
        return (loss, item_count, *general_tail(grads, weights, moms, errs, facs, small, small_params, small_mom))

    got, sums = scatter_cores_first(back_zero.far, back_zero.near)
    mine = back_zero.mine + swap(back_zero.other, 1)
    left = mine + swap_by_core(mine, 2, 4)
    left, item_count, *tables_grad = lax.optimization_barrier((left, back_one.sums[8, 0], *tables_grad))
    left = left + swap_by_core(left, 4, 2)
    sums, left = lax.optimization_barrier((sums, left))
    received[0] = {chip: swap(x, chip) for chip, x in sums.items()} | {1: got}
    left = sum_replicas(left, reps)
    left_other = swap(left, 1)
    left, left_other, received[0] = lax.optimization_barrier((left, left_other, received[0]))
    factors = right_factors(me, (left, left_other), back_zero.whole, back_one.whole, tables_grad)
    received[1] = scatter_cores(back_one, received[1])
    mine = sum_replica(factors.mine, factors.other)
    every = sum_replicas(mine, reps)
    updated = apply_update(
        me,
        weights,
        moms,
        turned,
        (mine, swap(mine, 1), every, swap(every, 1)),
        (factors.basis0, factors.basis1),
        (back_zero.own, back_one.own),
        received,
    )
    odd = (me[0] & 1) == 1
    summed = jnp.where(odd, left, left_other)[:, HALF_LEFT - SMALLS :]
    vgrads = []
    for layer in range(LAYERS):
        first, second = summed[:, 512 * layer : 512 * layer + D], summed[:, 512 * layer + D : 512 * (layer + 1)]
        vgrads.append(jnp.concatenate([first, second], axis=0))
    head_bias_grad = summed[:, 1024 : 1024 + 128].reshape(-1)
    loss = summed[0, 1024 + 128]
    table_sums = [updated.small[:, WIDE * i : WIDE * (i + 1)] for i in range(2)]
    new_small_mom = MOMENTUM * small_mom + small_vector(vgrads, table_sums, head_bias_grad)
    return (
        loss,
        item_count,
        *[getattr(updated, "new_" + n) for n in NAMES],
        *[getattr(updated, "new_mom_" + n) for n in NAMES],
        *[getattr(updated, "err_" + n) for n in NAMES],
        *[jnp.swapaxes(getattr(updated, "new_fac_" + n), -1, -2) for n in NAMES],
        small_params - SMALL_RATE * new_small_mom,
        new_small_mom,
    )


FULL_ROWS = (9 * CIN, D, D, D, FF, D)


def whole_matrices(group, packed):
    out = {}
    for name, (at, rows, blocks) in pieces_of(SHARDS, group)[0].items():
        cols = [packed[:, at + c * rows : at + (c + 1) * rows, :].reshape(SHARDS * rows, D) for c in range(blocks)]
        out[name] = jnp.concatenate(cols, axis=1)
    return out


def orthonormal(product, gram_mat):
    lower_tri = jnp.linalg.cholesky(gram_mat)
    return jnp.swapaxes(
        jax.scipy.linalg.solve_triangular(lower_tri, jnp.swapaxes(product, 1, 2), lower=True), 1, 2
    )


def general_tail(grads, weights, moms, errs, facs, small, small_params, small_mom):
    layer = [jnp.stack([grads[g][n] for g in range(2)]) for n in MATRIX_NAMES]
    wholes = [grads[0]["conv"][None], *layer, grads[1]["head"][None, :, :CLASSES]]
    lift = lambda xs: [xs[0][None], *xs[1:5], xs[5][None]]
    weights, moms, facs = lift(weights), lift(moms), lift(facs)
    errors = [errs[0], *[e[0] for e in errs[1:5]], errs[5]]
    merged = [
        lax.psum_scatter(g, FSDP, scatter_dimension=1, tiled=True) + e for g, e in zip(wholes, errors)
    ]
    lefts = lax.psum(
        [jnp.einsum("bio,bok->bik", m, f, precision=PRECISE) for m, f in zip(merged, facs)], "rep"
    )
    grams = lax.psum([jnp.einsum("bik,bil->bkl", p, p, precision=PRECISE) for p in lefts], FSDP)
    bases = [orthonormal(p, g) for p, g in zip(lefts, grams)]
    local = [jnp.einsum("bio,bik->bok", m, b, precision=PRECISE) for m, b in zip(merged, bases)]
    mine = lax.psum([*local, small], FSDP)
    every = lax.psum(mine, REP)
    product = lambda b, q: jnp.einsum("bik,bok->bio", b, q, precision=PRECISE)
    new_errs = [m - product(b, q) for m, b, q in zip(merged, bases, mine)]
    new_moms = [MOMENTUM * m + product(b, q) for m, b, q in zip(moms, bases, every)]
    new_weights = [w - LEARN_RATE * m for w, m in zip(weights, new_moms)]
    drop = lambda xs: [xs[0][0], *xs[1:5], xs[5][0]]
    new_small_mom = MOMENTUM * small_mom + every[6]
    return (
        *drop(new_weights),
        *drop(new_moms),
        new_errs[0],
        *[e[None] for e in new_errs[1:5]],
        new_errs[5],
        *drop(every[:6]),
        small_params - SMALL_RATE * new_small_mom,
        new_small_mom,
    )


def solution(mesh):
    rows, mids = P(FSDP, None), P(None, FSDP, None)
    matrices = (rows, mids, mids, mids, mids, rows)
    errors = (
        P(REP, FSDP, None),
        *[P(REP, None, FSDP, None)] * 4,
        P(REP, FSDP, None),
    )
    return jax.shard_map(
        lambda *args: step(mesh, args),
        mesh=mesh,
        in_specs=(
            P((REP, FSDP), None, None, None),
            P((REP, FSDP)),
            P(REP, FSDP),
            P(),
            *matrices,
            *matrices,
            *errors,
            *[P()] * 8,
        ),
        out_specs=(P(), P(), *matrices, *matrices, *errors, *[P()] * 8),
        check_vma=False,
    )
```

```python
import functools
import types

import jax
import jax.numpy as jnp
import numpy as np
from jax import lax
from jax.experimental import pallas as pl
from jax.experimental.pallas import tpu as pltpu
from jax.sharding import PartitionSpec as P

D = 256
HEADS = 8
HEAD = 32
FF = 768
CLASSES = 1000
CPAD = 1024
CIN = 128
GRID = 14
KER = 7
LAYERS = 2
PIX = 196
RB = 169
RANK = 8

EPSILON = 1e-05
MASKED = -1000000000.0
MOMENTUM = 0.9
LEARN_RATE = 16.0
SMALL_RATE = 4.0
PRECISE = lax.Precision.HIGHEST
SCALE = HEAD ** (-0.5)

COLS = 16
TOK = GRID * COLS
KEYS = 128
HALF = 128
PARTS = 3 * CIN
FSDP, REP = "fsdp", "rep"
F32 = jnp.float32
BF16 = jnp.bfloat16
VMEM_LIMIT = 58 * 1024 * 1024
SMALL_LIMIT = 20 * 1024 * 1024

GROUPS = (
    ((0, 80, 0), (80, 32, 32), (112, 32, 64), (144, 80, 96)),
    ((0, 112, 0), (112, 112, 96)),
)


def row_order(layer):
    if layer % 2 == 0:
        return list(range(GRID))
    return [*range(0, GRID, 2), *range(1, GRID, 2)]


def window_start(cell, dil):
    residue, position = cell % dil, cell // dil
    length = (GRID - residue + dil - 1) // dil
    return min(max(position - KER // 2, 0), length - KER)


def in_window(query, key, dil):
    if query % dil != key % dil:
        return False
    first = window_start(query, dil)
    return first <= key // dil < first + KER


@functools.lru_cache(None)
def static_maps(layer):
    dil = 1 + layer % 2
    order = row_order(layer)
    starts = np.zeros(GRID, np.int64)
    mask = np.zeros((TOK, KEYS), np.float32)
    for q0, nq, k0 in GROUPS[layer % 2]:
        for place in range(q0 // COLS, (q0 + nq) // COLS):
            qy = order[place]
            for j in range(8):
                ky = order[k0 // COLS + j]
                if not in_window(qy, ky, dil):
                    continue
                starts[place] = ky // dil - qy // dil + KER - 1 - j
                for x in range(GRID):
                    for kx in range(GRID):
                        if in_window(x, kx, dil):
                            mask[place * COLS + x, j * COLS + kx] = 1.0
    shifts = np.zeros((COLS, KEYS, KEYS), np.float32)
    for x in range(GRID):
        for kx in range(GRID):
            if in_window(x, kx, dil):
                dx = kx // dil - x // dil + KER - 1
                for j in range(8):
                    shifts[x, j * COLS + dx, j * COLS + kx] = 1.0
    return starts, shifts, mask


def norm_stats(values):
    centred = values - jnp.mean(values, axis=-1, keepdims=True)
    rstd = lax.rsqrt(jnp.mean(centred * centred, axis=-1, keepdims=True) + EPSILON)
    return centred * rstd, rstd


def norm_back(grad, xhat, rstd, gain):
    scaled = grad * gain
    mean_one = jnp.mean(scaled, axis=-1, keepdims=True)
    mean_two = jnp.mean(scaled * xhat, axis=-1, keepdims=True)
    return rstd * (scaled - mean_one - xhat * mean_two)


def col_sum(values):
    return jnp.sum(values, axis=0, keepdims=True)


def dot_nn(a, b, **kw):
    return lax.dot_general(a, b, (((1,), (0,)), ((), ())), preferred_element_type=F32, **kw)


def dot_nt(a, b, **kw):
    return lax.dot_general(a, b, (((1,), (1,)), ((), ())), preferred_element_type=F32, **kw)


def dot_tn(a, b, **kw):
    return lax.dot_general(a, b, (((0,), (0,)), ((), ())), preferred_element_type=F32, **kw)


ERFC_T = 0.44
ERFC_POLY = (
    0.24822096599679971,
    0.24887097779118345,
    0.21731489562842682,
    0.21580753897325447,
    -0.020171305217729862,
    0.2966767736009737,
    -0.2779414931115683,
    0.07122182759012696,
)


def gelu_parts(x):
    bell = jnp.exp(-0.5 * x * x)
    t = 1.0 / (1.0 + (ERFC_T * 0.5**0.5) * jnp.abs(x))
    poly = jnp.full_like(t, 0.5 * ERFC_POLY[-1])
    for c in ERFC_POLY[-2::-1]:
        poly = poly * t + 0.5 * c
    tail = poly * t * bell
    cdf = jnp.where(x < 0, tail, 1.0 - tail)
    return x * cdf, cdf + x * bell * (1.0 / (2.0 * np.pi) ** 0.5)


def head_masks():
    lane = lax.broadcasted_iota(jnp.int32, (1, HALF), 1)
    return [jnp.where(lane // HEAD == h, 1.0, 0.0).astype(BF16) for h in range(4)]


def spread_heads(block, masks):
    return jnp.concatenate([block * m for m in masks], axis=0)


def whole(shape):
    return pl.BlockSpec(shape, lambda *_: (0,) * len(shape))


def params(limit=VMEM_LIMIT):
    return pltpu.CompilerParams(dimension_semantics=("arbitrary",), vmem_limit_bytes=limit)


def cost(micros):
    return pl.CostEstimate(flops=int(micros * 1.1e9), bytes_accessed=0, transcendentals=0)


def call(name, kernel, steps, me, ins, outs, scratch, micros, limit=VMEM_LIMIT):
    names = ["me", *[e[0] for e in ins], *[e[0] for e in outs], *[e[0] for e in scratch]]

    def body(*refs):
        kernel(types.SimpleNamespace(**dict(zip(names, refs, strict=True))))

    results = pl.pallas_call(
        body,
        grid_spec=pltpu.PrefetchScalarGridSpec(
            num_scalar_prefetch=1,
            grid=(steps,),
            in_specs=[e[2] or whole(e[1].shape) for e in ins],
            out_specs=[e[3] or whole(e[1]) for e in outs],
            scratch_shapes=[pltpu.VMEM(e[1], e[2]) for e in scratch],
        ),
        out_shape=[jax.ShapeDtypeStruct(e[1], e[2]) for e in outs],
        compiler_params=params(limit),
        cost_estimate=cost(micros),
        name=name,
    )(me, *[e[1] for e in ins])
    return types.SimpleNamespace(**dict(zip([e[0] for e in outs], results, strict=True)))


def patch_kernel(feat_ref, out_ref, wide_ref, patch_ref):
    @pl.when(pl.program_id(0) == 0)
    def _():
        patch_ref[...] = jnp.zeros_like(patch_ref)

    for item in range(feat_ref.shape[0]):
        wide_ref[item, :, 0 : 2 * GRID, :] = feat_ref[item].astype(F32)
        even = wide_ref[item, :, pl.ds(0, GRID, stride=2), :]
        odd = wide_ref[item, :, pl.ds(1, GRID, stride=2), :]
        patch_ref[item, :, 1 : GRID + 1, 0:CIN] = odd
        patch_ref[item, :, 0:GRID, CIN : 2 * CIN] = even
        patch_ref[item, :, 0:GRID, 2 * CIN : 3 * CIN] = odd
        both = patch_ref[item].astype(BF16).reshape(GRID, 2, COLS, PARTS)
        for par in range(2):
            out_ref[item, par] = both[:, par].reshape(TOK, PARTS)


def make_patches(features):
    slots = features.shape[0]
    items = max(n for n in (1, 2, 3, 4) if slots % n == 0)
    return pl.pallas_call(
        patch_kernel,
        grid=(slots // items,),
        in_specs=[pl.BlockSpec((items, 2 * GRID, 2 * GRID, CIN), lambda i: (i, 0, 0, 0))],
        out_specs=pl.BlockSpec((items, 2, TOK, PARTS), lambda i: (i, 0, 0, 0)),
        out_shape=jax.ShapeDtypeStruct((slots, 2, TOK, PARTS), BF16),
        scratch_shapes=[
            pltpu.VMEM((items, 2 * GRID, 32, CIN), F32),
            pltpu.VMEM((items, 2 * GRID, COLS, PARTS), F32),
        ],
        compiler_params=params(),
        cost_estimate=cost(7),
        name="patches",
    )(features)


WIDE = 16 * COLS


def split_three(x):
    high = x.astype(BF16).astype(F32)
    mid = (x - high).astype(BF16).astype(F32)
    return jnp.concatenate([high, mid, x - high - mid], axis=0).astype(BF16)


def exact_dot(dot, x, hot):
    n = x.shape[0]
    out = dot(split_three(x), hot)
    return out[0:n] + out[n : 2 * n] + out[2 * n : 3 * n]


def shift_arrays():
    maps = [static_maps(layer) for layer in range(LAYERS)]
    return jnp.asarray(np.stack([m[1] for m in maps]), BF16), jnp.asarray(np.stack([m[2] for m in maps]))


def make_bias(me, tables):
    shifts, masks = shift_arrays()

    def kernel(r):
        for layer in range(LAYERS):

            @pl.when(pl.program_id(0) == layer)
            def _():
                for y, start in enumerate(static_maps(layer)[0]):
                    moved = pltpu.roll(r.table[0], int(-COLS * start) % WIDE, 1)
                    r.rows[pl.ds(y, HEADS, stride=GRID), :] = moved[:, :KEYS]

        rows = r.rows[...]
        for x in range(GRID):
            r.flat[pl.ds(x, HEADS * GRID, stride=COLS), :] = exact_dot(dot_nn, rows, r.shift[0, x])
        for x in range(GRID, COLS):
            r.flat[pl.ds(x, HEADS * GRID, stride=COLS), :] = jnp.zeros((HEADS * GRID, KEYS), F32)
        for h in range(HEADS):
            block = r.flat[h * TOK : (h + 1) * TOK, :]
            r.out[0, h] = jnp.where(r.mask[0] > 0.5, block, MASKED)

    return call(
        "bias",
        kernel,
        LAYERS,
        me,
        [
            ("table", tables, pl.BlockSpec((1, HEADS, WIDE), lambda i, *_: (i, 0, 0))),
            ("shift", shifts, pl.BlockSpec((1, COLS, KEYS, KEYS), lambda i, *_: (i, 0, 0, 0))),
            ("mask", masks, pl.BlockSpec((1, TOK, KEYS), lambda i, *_: (i, 0, 0))),
        ],
        [
            (
                "out",
                (LAYERS, HEADS, TOK, KEYS),
                F32,
                pl.BlockSpec((1, HEADS, TOK, KEYS), lambda i, *_: (i, 0, 0, 0)),
            )
        ],
        [("flat", (HEADS * TOK, KEYS), F32), ("rows", (HEADS * GRID, KEYS), F32)],
        5,
    ).out


def table_grad(me, grad, layer):
    shifts, _ = shift_arrays()

    def kernel(r):
        total = None
        for x in range(GRID):
            part = r.grad[pl.ds(x, HEADS * GRID, stride=COLS), :]
            part = exact_dot(dot_nt, part, r.shift[0, x])
            total = part if total is None else total + part
        r.rows[...] = total
        result = None
        for y, start in enumerate(static_maps(layer)[0]):
            part = pad_lanes(r.rows[pl.ds(y, HEADS, stride=GRID), :], WIDE)
            moved = pltpu.roll(part, int(COLS * start) % WIDE, 1)
            result = moved if result is None else result + moved
        r.out[...] = result

    return call(
        "table",
        kernel,
        1,
        me,
        [
            ("grad", grad, None),
            ("shift", shifts, pl.BlockSpec((1, COLS, KEYS, KEYS), lambda *_: (layer, 0, 0, 0))),
        ],
        [("out", (HEADS, WIDE), F32, None)],
        [("rows", (HEADS * GRID, KEYS), F32)],
        3,
    ).out


def pieces_of(shards, group):
    narrow, wide = D // shards, FF // shards
    sizes = [("qkv", narrow, 3), ("proj", narrow, 1), ("up", narrow, 3), ("down", wide, 1)]
    if group == 0:
        sizes = [("conv", 9 * CIN // shards, 1)] + sizes
    else:
        sizes = sizes + [("head", narrow, 4)]
    out, at = {}, 0
    for name, rows, blocks in sizes:
        out[name] = (at, rows, blocks)
        at += rows * blocks
    return out, at


SHARDS = 8
COUNT_ROWS = 16
NAMES = ("conv", "qkv", "proj", "up", "down", "head")
WHOLE_NAMES = ("conv", "head")


def pack(parts):
    out = []
    for part in parts:
        if part.shape[1] == CLASSES:
            part = jnp.pad(part, ((0, 0), (0, CPAD - CLASSES)))
        out += [part[:, c : c + D] for c in range(0, part.shape[1], D)]
    return jnp.concatenate(out, axis=0)


def pack_weights(weights, counts):
    def kernel(r):
        for group, packed in ((0, r.packed0), (1, r.packed1)):
            for name, (at, rows, blocks) in pieces_of(SHARDS, group)[0].items():
                ref = getattr(r, name)
                for c in range(blocks):
                    width = min(D, ref.shape[-1] - c * D)
                    cols = slice(c * D, c * D + width)
                    value = ref[:, cols] if name in WHOLE_NAMES else ref[group, :, cols]
                    value = value.astype(BF16)
                    if width < D:
                        value = jnp.concatenate([value, jnp.zeros((rows, D - width), BF16)], axis=1)
                    packed[at + c * rows : at + (c + 1) * rows, :] = value
        end = pieces_of(SHARDS, 0)[1]
        r.packed0[end : end + COUNT_ROWS, :] = jnp.broadcast_to(r.count[...].astype(F32), (COUNT_ROWS, D)).astype(BF16)

    ends = [pieces_of(SHARDS, group)[1] for group in range(2)]
    out = call(
        "pack",
        kernel,
        1,
        jnp.zeros((1,), jnp.int32),
        [*[(n, w, None) for n, w in zip(NAMES, weights)], ("count", counts, None)],
        [("packed0", (ends[0] + COUNT_ROWS, D), BF16, None), ("packed1", (ends[1], D), BF16, None)],
        [],
        2,
    )
    return out.packed0, out.packed1


def unpack_weights(me, sources, targets, group):
    layout, _ = pieces_of(SHARDS, group)
    for ref, low, high, offsets in sources:
        for p, offset in enumerate(offsets):
            owner = me ^ offset
            for name, target in targets.items():
                at, rows, blocks = layout[name]
                if not low <= at < high:
                    continue
                place = pl.ds(pl.multiple_of(owner * rows, 16), rows)
                for c in range(blocks):
                    first = at - low + c * rows
                    target[place, c * D : (c + 1) * D] = ref[p, first : first + rows, :]


def units(layer, items):
    return [(n, n * TOK, group, hf) for n in range(items) for group in GROUPS[layer] for hf in range(2)]


def lanes_of(which, hf):
    return slice(which * D + hf * HALF, which * D + (hf + 1) * HALF)


def scores_of(hf):
    return slice(hf * 4 * KEYS, (hf + 1) * 4 * KEYS)


def attend(layer, items, joined_ref, bias_ref, score_ref, probs_ref, mixed_ref):
    masks = head_masks()
    for item, base, (q0, nq, k0), hf in units(layer, items):
        query = joined_ref[base + q0 : base + q0 + nq, lanes_of(0, hf)]
        keys = spread_heads(joined_ref[base + k0 : base + k0 + KEYS, lanes_of(1, hf)], masks)
        score_ref[item, q0 : q0 + nq, scores_of(hf)] = dot_nt(query, keys)
    for item in range(items):
        for q0, nq, k0 in GROUPS[layer]:
            for head in range(HEADS):
                place = (item, slice(q0, q0 + nq), slice(head * KEYS, (head + 1) * KEYS))
                s = score_ref[place] * SCALE + bias_ref[0, head, q0 : q0 + nq, :]
                e = jnp.exp(s - jnp.max(s, axis=-1, keepdims=True))
                probs_ref[place] = (e * (1.0 / jnp.sum(e, axis=-1, keepdims=True))).astype(BF16)
    for item, base, (q0, nq, k0), hf in units(layer, items):
        values = spread_heads(joined_ref[base + k0 : base + k0 + KEYS, lanes_of(2, hf)], masks)
        mixed = dot_nn(probs_ref[item, q0 : q0 + nq, scores_of(hf)], values)
        mixed_ref[base + q0 : base + q0 + nq, lanes_of(0, hf)] = mixed.astype(BF16)


def layer_forward(layer, hidden, vec_ref, weights, bias_ref, outs, work, items):
    joined_ref, probs_ref, mixed_ref, after_ref, slope_ref, active_ref = outs
    score_ref, pre_ref = work
    vec = lambda i: vec_ref[LAYER_AT[layer] + i : LAYER_AT[layer] + i + 1, :]
    xhat, _ = norm_stats(hidden)
    normed = (xhat * vec(0) + vec(1)).astype(BF16)
    for c in range(3):
        part = dot_nn(normed, weights["qkv"][:, c * D : (c + 1) * D])
        if c != 1:
            part = part + vec(2 if c == 0 else 3)
        joined_ref[:, c * D : (c + 1) * D] = part.astype(BF16)
    attend(layer, items, joined_ref, bias_ref, score_ref, probs_ref, mixed_ref)
    after = hidden + (dot_nn(mixed_ref[...], weights["proj"][...]) + vec(4))
    after_ref[...] = after
    xhat, _ = norm_stats(after)
    normed = (xhat * vec(5) + vec(6)).astype(BF16)
    for c in range(3):
        cols = slice(c * D, (c + 1) * D)
        pre_ref[:, cols] = dot_nn(normed, weights["up"][:, cols])
    for c in range(3):
        cols = slice(c * D, (c + 1) * D)
        active, slope = gelu_parts(pre_ref[:, cols] + vec(8 + c))
        slope_ref[:, cols] = slope.astype(BF16)
        active_ref[:, cols] = active.astype(BF16)
    return after_ref[...] + (dot_nn(active_ref[...], weights["down"][...]) + vec(7))


def conv_taps(patch_ref, item):
    odd = patch_ref[item, 1]
    up = jnp.concatenate([jnp.zeros((COLS, PARTS), BF16), odd[: TOK - COLS]], axis=0)
    return up, patch_ref[item, 0], odd


CACHE = (
    ("joined", 3 * D, BF16),
    ("probs", None, BF16),
    ("mixed", D, BF16),
    ("after", D, F32),
    ("slope", FF, BF16),
    ("active", FF, BF16),
)
MATRICES = (("qkv", (D, FF)), ("proj", (D, D)), ("up", (D, FF)), ("down", (FF, D)))
MATRIX_NAMES = [m[0] for m in MATRICES]


def token_spec(items, width=D):
    return pl.BlockSpec((items * TOK, width), lambda i, *_: (i, 0))


def cache_entries(slots, items):
    out = []
    for name, width, dtype in CACHE:
        if width is None:
            spec = pl.BlockSpec((items, TOK, HEADS * KEYS), lambda i, *_: (i, 0, 0))
            out.append((name, (slots, TOK, HEADS * KEYS), dtype, spec))
        else:
            out.append((name, (slots * TOK, width), dtype, token_spec(items, width)))
    return out


def forward_scratch(items):
    return [("scores", (items, TOK, HEADS * KEYS), F32), ("pre", (items * TOK, FF), F32)]


def caches_of(r):
    return tuple(getattr(r, entry[0]) for entry in CACHE)


def bias_spec(layer):
    return pl.BlockSpec((1, HEADS, TOK, KEYS), lambda i, *_: (layer, 0, 0, 0))


def patch_spec(items):
    return pl.BlockSpec((items, 2, TOK, PARTS), lambda i, *_: (i, 0, 0, 0))


def source_entries(sources):
    return [(f"source{i}", array, None) for i, (array, *_) in enumerate(sources)]


def sources_of(r, sources):
    return [(getattr(r, f"source{i}"), *entry[1:]) for i, entry in enumerate(sources)]


def count_of(sources):
    total = jnp.zeros((1, 1), F32)
    for ref, _, high, offsets in sources:
        if ref.shape[1] > high:
            for p in range(len(offsets)):
                total = total + ref[p, high : high + COUNT_ROWS, :].astype(F32)[0:1, 0:1]
    return total


CONV_AT, LAYER_AT, FINAL_AT, BIAS_AT = 0, (3, 14), 25, 27


def forward_zero(me, patches, sources, vecs, bias, items):
    slots = patches.shape[0]

    def kernel(r):
        names = ["conv_w", *MATRIX_NAMES]
        weights = {n: getattr(r, n) for n in names}

        @pl.when(pl.program_id(0) == 0)
        def _():
            targets = {n.removesuffix("_w"): ref for n, ref in weights.items()}
            unpack_weights(r.me[0], sources_of(r, sources), targets, 0)
            r.count[...] = jnp.broadcast_to(count_of(sources_of(r, sources)), r.count.shape)

        for item in range(items):
            taps = conv_taps(r.patch, item)
            total = None
            for a in range(3):
                part = dot_nn(taps[a], r.conv_w[a * PARTS : (a + 1) * PARTS, :])
                total = part if total is None else total + part
            r.conv[item * TOK : (item + 1) * TOK, :] = total + r.vecs[CONV_AT : CONV_AT + 1, :]
        xhat, _ = norm_stats(r.conv[...])
        hidden = xhat * r.vecs[CONV_AT + 1 : CONV_AT + 2, :] + r.vecs[CONV_AT + 2 : CONV_AT + 3, :]
        hidden = layer_forward(0, hidden, r.vecs, weights, r.bias, caches_of(r), (r.scores, r.pre), items)
        for item in range(items):
            for place, row in enumerate(row_order(1)):
                r.hidden[item * TOK + place * COLS : item * TOK + (place + 1) * COLS, :] = hidden[
                    item * TOK + row * COLS : item * TOK + (row + 1) * COLS
                ]

    return call(
        "fwd0",
        kernel,
        slots // items,
        me,
        [
            ("patch", patches, patch_spec(items)),
            *source_entries(sources),
            ("vecs", vecs, None),
            ("bias", bias, bias_spec(0)),
        ],
        [
            ("hidden", (slots * TOK, D), F32, token_spec(items)),
            ("conv", (slots * TOK, D), F32, token_spec(items)),
            *cache_entries(slots, items),
            *[(n, shape, BF16, None) for n, shape in MATRICES],
            ("count", (8, 128), F32, None),
        ],
        [("conv_w", (9 * CIN, D), BF16), *forward_scratch(items)],
        30,
    )


def real_cells():
    place = lax.broadcasted_iota(jnp.int32, (TOK, 1), 0)
    return jnp.where(place % COLS < GRID, 1.0, 0.0)


def classify(r, slots, counts):
    rows = r.pooled.shape[0]
    place = lax.broadcasted_iota(jnp.int32, (rows, 1), 0)
    label = jnp.full((rows, 1), -1, jnp.int32)
    for i in range(slots):
        label = jnp.where(place == i, r.me[2 + i], label)
    live = jnp.where(place < r.me[1], 1.0, 0.0)
    count = sum([getattr(r, f"count{i}")[0:1, 0:1] for i in range(counts)])
    pooled = r.pooled[...].astype(BF16)
    head_bias = jnp.concatenate([r.vecs[BIAS_AT + c : BIAS_AT + c + 1, :] for c in range(CPAD // D)], axis=1)
    logits = dot_nn(pooled, r.head[...]) + head_bias
    peak = jnp.max(logits, axis=-1, keepdims=True)
    log_total = peak + jnp.log(jnp.sum(jnp.exp(logits - peak), axis=-1, keepdims=True))
    lane = lax.broadcasted_iota(jnp.int32, logits.shape, 1)
    onehot = jnp.where(label == lane, 1.0, 0.0)
    picked = jnp.sum(onehot * logits, axis=-1, keepdims=True)
    loss = col_sum(live * (log_total - picked))
    r.sums[0:8, :] = jnp.broadcast_to(loss, (8, 128))
    r.sums[8:16, :] = jnp.broadcast_to(count, (8, 128))
    d_logits = (jnp.exp(logits - log_total) - onehot) * ((1.0 / count) * live)
    d_logits = jnp.where(lane < CLASSES, d_logits, 0.0).astype(BF16)
    r.head_grad[...] = dot_tn(pooled, d_logits)
    r.hb_grad[...] = col_sum(d_logits.astype(F32))
    r.d_pooled[...] = dot_nt(d_logits, r.head[...]) * (1.0 / PIX)


def forward_one(me, hidden, sources, vecs, bias, items):
    slots = hidden.shape[0] // TOK
    rows = -(-slots // 16) * 16

    def kernel(r):
        weights = {n: getattr(r, n) for n in MATRIX_NAMES}
        step = pl.program_id(0)

        @pl.when(step == 0)
        def _():
            unpack_weights(r.me[0], sources_of(r, sources), weights | dict(head=r.head), 1)
            r.pooled[...] = jnp.zeros_like(r.pooled)

        out = layer_forward(1, r.hidden[...], r.vecs, weights, r.bias, caches_of(r), (r.scores, r.pre), items)
        r.out[...] = out
        xhat, _ = norm_stats(out)
        normed = xhat * r.vecs[FINAL_AT : FINAL_AT + 1, :] + r.vecs[FINAL_AT + 1 : FINAL_AT + 2, :]
        real = real_cells()
        for item in range(items):
            mean = col_sum(normed[item * TOK : (item + 1) * TOK] * real) * (1.0 / PIX)
            r.pooled[pl.ds(step * items + item, 1), :] = mean

    return call(
        "fwd1",
        kernel,
        slots // items,
        me,
        [
            ("hidden", hidden, token_spec(items)),
            *source_entries(sources),
            ("vecs", vecs, None),
            ("bias", bias, bias_spec(1)),
        ],
        [
            ("out", (slots * TOK, D), F32, token_spec(items)),
            *cache_entries(slots, items),
            *[(n, shape, BF16, None) for n, shape in MATRICES],
            ("head", (D, CPAD), BF16, None),
            ("pooled", (rows, D), F32, None),
        ],
        forward_scratch(items),
        28,
    )


def attend_back(layer, items, joined_ref, probs_ref, dmix_ref, djoin_ref, dkv_ref, dprob_ref, dscore_ref, bgrad_ref):
    masks = head_masks()
    for item, base, (q0, nq, k0), hf in units(layer, items):
        values = spread_heads(joined_ref[base + k0 : base + k0 + KEYS, lanes_of(2, hf)], masks)
        d_mix = dmix_ref[base + q0 : base + q0 + nq, lanes_of(0, hf)]
        dprob_ref[item, q0 : q0 + nq, scores_of(hf)] = dot_nt(d_mix, values)
    for q0, nq, k0 in GROUPS[layer]:
        for head in range(HEADS):
            total = None
            for item in range(items):
                place = (item, slice(q0, q0 + nq), slice(head * KEYS, (head + 1) * KEYS))
                p, dp = probs_ref[place].astype(F32), dprob_ref[place]
                ds = (p * (dp - jnp.sum(dp * p, axis=-1, keepdims=True))).astype(BF16)
                dscore_ref[place] = ds
                ds = ds.astype(F32)
                total = ds if total is None else total + ds
            bgrad_ref[head * TOK + q0 : head * TOK + q0 + nq, :] += total
    for item, base, (q0, nq, k0), hf in units(layer, items):
        keys = spread_heads(joined_ref[base + k0 : base + k0 + KEYS, lanes_of(1, hf)], masks)
        d_query = dot_nn(dscore_ref[item, q0 : q0 + nq, scores_of(hf)], keys) * SCALE
        djoin_ref[base + q0 : base + q0 + nq, lanes_of(0, hf)] = d_query.astype(BF16)
    dkv_ref[...] = jnp.zeros_like(dkv_ref)
    for item, base, (q0, nq, k0), hf in units(layer, items):
        qrows, krows = slice(base + q0, base + q0 + nq), slice(base + k0, base + k0 + KEYS)
        heads = [slice(h * KEYS, (h + 1) * KEYS) for h in range(hf * 4, hf * 4 + 4)]
        stacked = jnp.concatenate([dscore_ref[item, q0 : q0 + nq, h] for h in heads], axis=0)
        query = spread_heads(joined_ref[qrows, lanes_of(0, hf)], masks)
        dkv_ref[krows, lanes_of(0, hf)] += dot_tn(stacked, query)
        stacked = jnp.concatenate([probs_ref[item, q0 : q0 + nq, h] for h in heads], axis=0)
        d_mix = spread_heads(dmix_ref[qrows, lanes_of(0, hf)], masks)
        dkv_ref[krows, lanes_of(1, hf)] += dot_tn(stacked, d_mix)
    djoin_ref[:, D : 2 * D] = (dkv_ref[:, 0:D] * SCALE).astype(BF16)
    djoin_ref[:, 2 * D : 3 * D] = dkv_ref[:, D : 2 * D].astype(BF16)


def layer_backward(layer, d_out, hidden, vec_ref, weights, caches, work, grads, vgrad_ref, bgrad_ref, items):
    joined_ref, probs_ref, mixed_ref, after_ref, slope_ref, active_ref = caches
    dpre_ref, *work = work
    dmix_ref, djoin_ref = work[:2]
    vec = lambda i: vec_ref[LAYER_AT[layer] + i : LAYER_AT[layer] + i + 1, :]

    def add(row, value):
        vgrad_ref[row : row + 1, :] += value

    d_branch = d_out.astype(BF16)
    add(7, col_sum(d_branch.astype(F32)))
    for c in range(3):
        cols = slice(c * D, (c + 1) * D)
        dpre_ref[:, cols] = dot_nt(d_branch, weights["down"][cols, :])
    grads["down"][...] += dot_tn(d_branch, active_ref[...])
    for c in range(3):
        cols = slice(c * D, (c + 1) * D)
        d_pre = (dpre_ref[:, cols] * slope_ref[:, cols].astype(F32)).astype(BF16)
        djoin_ref[:, cols] = d_pre
        add(8 + c, col_sum(d_pre.astype(F32)))
    xhat, rstd = norm_stats(after_ref[...])
    normed = (xhat * vec(5) + vec(6)).astype(BF16)
    grads["up"][...] += dot_tn(normed, djoin_ref[...])
    d_normed = dot_nt(djoin_ref[...], weights["up"][...])
    add(5, col_sum(d_normed * xhat))
    add(6, col_sum(d_normed))
    d_after = d_out + norm_back(d_normed, xhat, rstd, vec(5))
    d_proj = d_after.astype(BF16)
    add(4, col_sum(d_proj.astype(F32)))
    grads["proj"][...] += dot_tn(mixed_ref[...], d_proj)
    dmix_ref[...] = dot_nt(d_proj, weights["proj"][...]).astype(BF16)
    attend_back(layer, items, joined_ref, probs_ref, *work, bgrad_ref)
    add(2, col_sum(djoin_ref[:, 0:D].astype(F32)))
    add(3, col_sum(djoin_ref[:, 2 * D : 3 * D].astype(F32)))
    xhat, rstd = norm_stats(hidden)
    normed = (xhat * vec(0) + vec(1)).astype(BF16)
    grads["qkv"][...] += dot_tn(normed, djoin_ref[...])
    d_normed = dot_nt(djoin_ref[...], weights["qkv"][...])
    add(0, col_sum(d_normed * xhat))
    add(1, col_sum(d_normed))
    return d_after + norm_back(d_normed, xhat, rstd, vec(0))


def split_two(x):
    high = x.astype(BF16)
    return high, (x - high.astype(F32)).astype(BF16)


def wide_dot(dot, rows, matrix):
    stacked = split_three(rows)
    high, low = split_two(matrix)
    out = dot(stacked, high) + dot(stacked, low)
    return out[0:RANK] + out[RANK : 2 * RANK] + out[2 * RANK : 3 * RANK]


def block_of(whole_ref, entry, c):
    at, rows, _ = entry
    return jnp.concatenate(
        [whole_ref[s, at + c * rows : at + (c + 1) * rows, :] for s in range(SHARDS)], axis=0
    )


def factor_of(r, group, name):
    ref = getattr(r, "fac_" + name)
    return ref[...] if name in WHOLE_NAMES else ref[group]


def finish_grads(r, group, grads):
    layout, _ = pieces_of(SHARDS, group)
    me = r.me[0]
    for name, (at, rows, blocks) in layout.items():
        matrix = grads[name]
        if name in ("down", "conv"):
            matrix = jnp.transpose(matrix[...])
        for s in range(SHARDS):
            for c in range(blocks):
                piece = matrix[s * rows : (s + 1) * rows, c * D : (c + 1) * D]
                r.sums_of[s, at + c * rows : at + (c + 1) * rows, :] = piece
    for name, (at, rows, blocks) in layout.items():
        err = getattr(r, "err_" + name)
        for c in range(blocks):
            width = min(D, err.shape[-1] - c * D)
            cols = slice(c * D, c * D + width)
            value = err[0, :, cols] if name in WHOLE_NAMES else err[0, group, :, cols]
            place = slice(at + c * rows, at + (c + 1) * rows)
            r.sums_of[me, place, 0:width] += value
    r.own[...] = r.sums_of[me]
    r.whole[...] = r.sums_of[...].astype(r.whole.dtype)
    if group == 0:
        for i, chip in enumerate((0, 2, 4, 6)):
            r.far[i] = r.sums_of[me ^ chip ^ 1].astype(BF16)
            if chip:
                r.near[i - 1] = r.sums_of[me ^ chip].astype(BF16)
    else:
        r.sent1[...] = r.sums_of[me ^ 1].astype(BF16)
        for chip in (2, 4, 6):
            for core in range(2):
                getattr(r, f"sent{chip}")[core] = r.sums_of[me ^ chip ^ core].astype(BF16)
    at_lane, lefts = 0, []
    for name, entry in layout.items():
        total = None
        for c in range(entry[2]):
            fac = factor_of(r, group, name)
            width = min(D, fac.shape[-1] - c * D)
            block = block_of(r.sums_of, entry, c)
            part = wide_dot(dot_nt, fac[:, c * D : c * D + width], block[:, :width])
            total = part if total is None else total + part
        lefts.append(total)
    return jnp.concatenate(lefts, axis=1)


def left_lanes(group):
    return sum(rows * SHARDS for _, rows, _ in pieces_of(SHARDS, group)[0].values())


def right_lanes(group):
    return sum(blocks * D for _, _, blocks in pieces_of(SHARDS, group)[0].values())


SMALLS = 2 * 512 + 128 + 128
HALF_LEFT = (left_lanes(0) + left_lanes(1) + SMALLS) // 2
HALF_RIGHT = (right_lanes(0) + right_lanes(1) + 2 * WIDE) // 2


def pad_lanes(x, lanes):
    return jnp.concatenate([x, jnp.zeros((x.shape[0], lanes - x.shape[1]), x.dtype)], axis=1)


def put_halves(r, whole):
    n = whole.shape[1] // 2
    first, second = whole[:, :n], whole[:, n:]
    odd = (r.me[0] & 1) == 1
    r.mine[...] = jnp.where(odd, second, first)
    r.other[...] = jnp.where(odd, first, second)


def get_halves(r, mine, other):
    odd = (r.me[0] & 1) == 1
    mine, other = mine[...], other[...]
    return jnp.concatenate([jnp.where(odd, other, mine), jnp.where(odd, mine, other)], axis=1)


def backward_outs(group, dtype):
    rows = pieces_of(SHARDS, group)[1]
    return [
        ("vgrad", (16, D), F32, None),
        ("bgrad", (HEADS * TOK, KEYS), F32, None),
        ("whole", (SHARDS, rows, D), dtype, None),
        ("own", (rows, D), F32, None),
    ]


def factor_inputs(group, errs, facs):
    out = []
    for name, err, fac in zip(NAMES, errs, facs):
        if name in pieces_of(SHARDS, group)[0]:
            out += [("err_" + name, err, None), ("fac_" + name, fac, None)]
    return out


def backward_scratch(items, group):
    return [
        ("sums_of", (SHARDS, pieces_of(SHARDS, group)[1], D), F32),
        ("d_pre", (items * TOK, FF), F32),
        ("d_mixed", (items * TOK, D), BF16),
        ("d_joined", (items * TOK, 3 * D), BF16),
        ("d_keys", (items * TOK, 2 * D), F32),
        ("d_probs", (items, TOK, HEADS * KEYS), F32),
        ("d_scores", (items, TOK, HEADS * KEYS), BF16),
        ("g_qkv", (D, FF), F32),
        ("g_proj", (D, D), F32),
        ("g_up", (D, FF), F32),
        ("g_down", (D, FF), F32),
    ]


def start_backward(r, grads):
    r.vgrad[...] = jnp.zeros_like(r.vgrad)
    r.bgrad[...] = jnp.zeros_like(r.bgrad)
    for ref in grads.values():
        ref[...] = jnp.zeros_like(ref)


def cache_inputs(caches, slots, items):
    return [(e[0], getattr(caches, e[0]), e[3]) for e in cache_entries(slots, items)]


def matrix_inputs(caches):
    return [(n, getattr(caches, n), None) for n in MATRIX_NAMES]


def backward_one(me, hidden, forward, vecs, count, errs, facs, items, dtype):
    slots = hidden.shape[0] // TOK

    def kernel(r):
        weights = {n: getattr(r, n) for n in MATRIX_NAMES}
        grads = {n: getattr(r, "g_" + n) for n in MATRIX_NAMES}
        step = pl.program_id(0)

        @pl.when(step == 0)
        def _():
            start_backward(r, grads)
            classify(r, slots, len(count))

        real = real_cells()
        d_final = jnp.concatenate(
            [real * r.d_pooled[pl.ds(step * items + item, 1), :] for item in range(items)], axis=0
        )
        xhat, rstd = norm_stats(r.out[...])
        r.vgrad[11:12, :] += col_sum(d_final * xhat)
        r.vgrad[12:13, :] += col_sum(d_final)
        d_out = norm_back(d_final, xhat, rstd, r.vecs[FINAL_AT : FINAL_AT + 1, :])
        work = (r.d_pre, r.d_mixed, r.d_joined, r.d_keys, r.d_probs, r.d_scores)
        r.d_hidden[...] = layer_backward(
            1, d_out, r.hidden[...], r.vecs, weights, caches_of(r), work, grads, r.vgrad, r.bgrad, items
        )

        @pl.when(step == pl.num_programs(0) - 1)
        def _():
            r.left[...] = finish_grads(r, 1, grads | dict(head=r.head_grad))

    return call(
        "back1",
        kernel,
        slots // items,
        me,
        [
            ("out", forward.out, token_spec(items)),
            ("pooled", forward.pooled, None),
            *[(f"count{i}", c, None) for i, c in enumerate(count)],
            ("hidden", hidden, token_spec(items)),
            *matrix_inputs(forward),
            ("head", forward.head, None),
            ("vecs", vecs, None),
            *cache_inputs(forward, slots, items),
            *factor_inputs(1, errs, facs),
        ],
        [
            ("d_hidden", hidden.shape, F32, token_spec(items)),
            *backward_outs(1, dtype),
            ("left", (RANK, left_lanes(1)), F32, None),
            ("sums", (16, 128), F32, None),
            ("hb_grad", (1, CPAD), F32, None),
            *[(f"sent{chip}", (2, pieces_of(SHARDS, 1)[1], D), BF16, None) for chip in (2, 4, 6)],
            ("sent1", (pieces_of(SHARDS, 1)[1], D), BF16, None),
        ],
        [*backward_scratch(items, 1), ("head_grad", (D, CPAD), F32), ("d_pooled", forward.pooled.shape, F32)],
        46,
    )


def backward_zero(me, back_one, forward, patches, vecs, errs, facs, items, dtype):
    slots = patches.shape[0]

    def kernel(r):
        weights = {n: getattr(r, n) for n in MATRIX_NAMES}
        grads = {n: getattr(r, "g_" + n) for n in [*MATRIX_NAMES, "conv"]}
        step = pl.program_id(0)

        @pl.when(step == 0)
        def _():
            start_backward(r, grads)

        order = row_order(1)
        rows = []
        for item in range(items):
            for row in range(GRID):
                first = item * TOK + order.index(row) * COLS
                rows.append(r.d_hidden[first : first + COLS, :])
        d_out = jnp.concatenate(rows, axis=0)
        conv_hat, conv_rstd = norm_stats(r.conv[...])
        gain = r.vecs[CONV_AT + 1 : CONV_AT + 2, :]
        hidden = conv_hat * gain + r.vecs[CONV_AT + 2 : CONV_AT + 3, :]
        work = (r.d_pre, r.d_mixed, r.d_joined, r.d_keys, r.d_probs, r.d_scores)
        d_conv = layer_backward(
            0, d_out, hidden, r.vecs, weights, caches_of(r), work, grads, r.vgrad, r.bgrad, items
        )
        r.vgrad[12:13, :] += col_sum(d_conv * conv_hat)
        r.vgrad[13:14, :] += col_sum(d_conv)
        d_conv = norm_back(d_conv, conv_hat, conv_rstd, gain).astype(BF16)
        r.vgrad[11:12, :] += col_sum(d_conv.astype(F32))
        for item in range(items):
            taps = conv_taps(r.patch, item)
            part = jnp.transpose(d_conv[item * TOK : (item + 1) * TOK])
            for a in range(3):
                grads["conv"][:, a * PARTS : (a + 1) * PARTS] += dot_nn(part, taps[a])

        @pl.when(step == pl.num_programs(0) - 1)
        def _():
            parts = [finish_grads(r, 0, grads), r.left_one[...]]
            for ref in (r.vgrad, r.vgrad_one):
                parts += [ref[0:8, :], ref[8:16, :]]
            put_halves(r, jnp.concatenate([*parts, r.head_bias[...], r.sums[0:8, :]], axis=1))

    return call(
        "back0",
        kernel,
        slots // items,
        me,
        [
            ("d_hidden", back_one.d_hidden, token_spec(items)),
            ("conv", forward.conv, token_spec(items)),
            ("patch", patches, patch_spec(items)),
            *matrix_inputs(forward),
            ("vecs", vecs, None),
            *cache_inputs(forward, slots, items),
            ("left_one", back_one.left, None),
            ("vgrad_one", back_one.vgrad, None),
            ("head_bias", back_one.hb_grad.reshape(8, 128), None),
            ("sums", back_one.sums, None),
            *factor_inputs(0, errs, facs),
        ],
        [
            *backward_outs(0, dtype),
            ("far", (4, pieces_of(SHARDS, 0)[1], D), BF16, None),
            ("near", (3, pieces_of(SHARDS, 0)[1], D), BF16, None),
            ("mine", (RANK, HALF_LEFT), F32, None),
            ("other", (RANK, HALF_LEFT), F32, None),
        ],
        [*backward_scratch(items, 0), ("g_conv", (D, 9 * CIN), F32)],
        63,
    )


def inverse_cholesky(gram):
    row = lax.broadcasted_iota(jnp.int32, (1, RANK, 2 * RANK), 1)
    lane = lax.broadcasted_iota(jnp.int32, (1, RANK, 2 * RANK), 2)
    eye = jnp.broadcast_to(jnp.where(lane == row + RANK, 1.0, 0.0), (gram.shape[0], RANK, 2 * RANK))
    work = jnp.concatenate([gram, jnp.zeros_like(gram)], axis=2) + eye
    for k in range(RANK):
        scale = 1.0 / jnp.sqrt(work[:, k : k + 1, k : k + 1])
        pivot = work[:, k : k + 1, :] * scale
        column = work[:, :, k : k + 1] * scale
        work = jnp.where(row > k, work - column * pivot, jnp.where(row == k, pivot, work))
    return work[:, :, RANK : 2 * RANK]


def basis_lanes(group):
    return sum(rows for _, rows, _ in pieces_of(SHARDS, group)[0].values())


def right_factors(me, left, whole_zero, whole_one, tables):
    def kernel(r):
        groups = (r.whole0, r.whole1)
        left = get_halves(r, r.left_mine, r.left_other)
        entries, at = [], 0
        for group in range(2):
            for entry in pieces_of(SHARDS, group)[0].values():
                entries.append((group, entry, left[:, at : at + entry[1] * SHARDS]))
                at += entry[1] * SHARDS
        grams = jnp.stack([dot_nt(x, x, precision=PRECISE) for _, _, x in entries])
        inverses = inverse_cholesky(grams)
        rows_of = [[], []]
        parts = []
        for i, (group, entry, x) in enumerate(entries):
            basis = dot_nn(inverses[i], x, precision=PRECISE)
            rows_of[group].append((basis, entry[1]))
            for c in range(entry[2]):
                parts.append(exact_dot(dot_nn, basis, block_of(groups[group], entry, c)))
        for group, out in ((0, r.basis0), (1, r.basis1)):
            for s in range(SHARDS):
                at = 0
                for basis, rows in rows_of[group]:
                    out[s, :, at : at + rows] = basis[:, s * rows : (s + 1) * rows]
                    at += rows
        put_halves(r, jnp.concatenate([*parts, r.table0[...], r.table1[...]], axis=1))

    return call(
        "right",
        kernel,
        1,
        me,
        [
            ("left_mine", left[0], None),
            ("left_other", left[1], None),
            ("whole0", whole_zero, None),
            ("whole1", whole_one, None),
            ("table0", tables[0], None),
            ("table1", tables[1], None),
        ],
        [
            ("mine", (RANK, HALF_RIGHT), F32, None),
            ("other", (RANK, HALF_RIGHT), F32, None),
            ("basis0", (SHARDS, RANK, basis_lanes(0)), F32, None),
            ("basis1", (SHARDS, RANK, basis_lanes(1)), F32, None),
        ],
        [],
        6,
        SMALL_LIMIT,
    )


def six_products(x, other):
    high = x.astype(BF16).astype(F32)
    mid = (x - high).astype(BF16).astype(F32)
    low = x - high - mid
    terms = [high, mid, high, mid, low, high] if other else [high, high, mid, mid, high, low]
    return jnp.concatenate(terms, axis=0).astype(BF16)


def apply_update(me, weights, moms, facs, right, factors, own, received):
    def kernel(r):
        right_mine = get_halves(r, r.rep_mine, r.rep_other)
        right_all = get_halves(r, r.all_mine, r.all_other)
        at_col = 0
        for group in range(2):
            total = getattr(r, f"own{group}")[...] + getattr(r, f"sib{group}")[0].astype(F32)
            for chip in (2, 4, 6):
                total = total + getattr(r, f"got{group}_{chip}")[0].astype(F32)
            basis = getattr(r, f"basis{group}")
            at_row = 0
            for name, (at, rows, blocks) in pieces_of(SHARDS, group)[0].items():
                left = six_products(basis[0, :, at_row : at_row + rows], False)
                at_row += rows
                single = name in WHOLE_NAMES
                for c in range(blocks):
                    width = min(D, (CLASSES if name == "head" else blocks * D) - c * D)
                    cols = slice(c * D, c * D + width)
                    place = (slice(None), cols) if single else (group, slice(None), cols)
                    err_place = (0, slice(None), cols) if single else (0, group, slice(None), cols)
                    right = slice(at_col, at_col + D)
                    at_col += D
                    getattr(r, "new_fac_" + name)[place] = right_all[:, right][:, :width]
                    mine = dot_tn(left, six_products(right_mine[:, right], True))
                    every = dot_tn(left, six_products(right_all[:, right], True))
                    merged = total[at + c * rows : at + (c + 1) * rows]
                    getattr(r, "err_" + name)[err_place] = (merged - mine)[:, :width]
                    mom = MOMENTUM * getattr(r, "mom_" + name)[place] + every[:, :width]
                    getattr(r, "new_mom_" + name)[place] = mom
                    getattr(r, "new_" + name)[place] = getattr(r, "w_" + name)[place] - LEARN_RATE * mom
        r.small[...] = right_all[:, at_col:]

    first = lambda x: pl.BlockSpec((1,) + x.shape[1:], lambda *_: (0, 0, 0))
    mine_spec = lambda x: pl.BlockSpec((1,) + x.shape[1:], lambda i, m: (m[0], 0, 0))
    small = 2 * HALF_RIGHT - right_lanes(0) - right_lanes(1)
    return call(
        "update",
        kernel,
        1,
        me,
        [
            *[("w_" + n, w, None) for n, w in zip(NAMES, weights)],
            *[("mom_" + n, m, None) for n, m in zip(NAMES, moms)],
            *zip(("rep_mine", "rep_other", "all_mine", "all_other"), right, [None] * 4),
            ("basis0", factors[0], mine_spec(factors[0])),
            ("basis1", factors[1], mine_spec(factors[1])),
            ("own0", own[0], None),
            ("own1", own[1], None),
            *[(f"got{g}_{c}", received[g][c], first(received[g][c])) for g in range(2) for c in (2, 4, 6)],
            *[(f"sib{g}", received[g][1], first(received[g][1])) for g in range(2)],
        ],
        [
            *[("new_" + n, w.shape, F32, None) for n, w in zip(NAMES, weights)],
            *[("new_mom_" + n, w.shape, F32, None) for n, w in zip(NAMES, weights)],
            *[("err_" + n, (1,) + w.shape, F32, None) for n, w in zip(NAMES, weights)],
            *[("new_fac_" + n, f.shape, F32, None) for n, f in zip(NAMES, facs)],
            ("small", (RANK, small), F32, None),
        ],
        [],
        5,
    )


def swap(x, offset):
    return lax.ppermute(x, FSDP, [(i, i ^ offset) for i in range(SHARDS)])


def swap_by_core(x, even, odd):
    return lax.ppermute(x, FSDP, [(i, i ^ (odd if i & 1 else even)) for i in range(SHARDS)])


def swap_rep(x, offset, reps):
    return lax.ppermute(x, REP, [(i, i ^ offset) for i in range(reps)])


def gather_chips(packed):
    return [packed, *[swap(packed, chip) for chip in (2, 4, 6)]]


def with_sibling(near, end):
    near = jnp.stack(near)
    return [(near, 0, end, (0, 2, 4, 6)), (swap(near, 1), 0, end, (1, 3, 5, 7))]


def gather_pair(packed):
    return jnp.stack([packed, swap(packed, 1)])


def spread_pair(pair, end):
    out = [(pair, 0, end, (0, 1))]
    return out + [(swap(pair, chip), 0, end, (chip, chip ^ 1)) for chip in (2, 4, 6)]


def sum_replica(mine, other):
    mine = mine + swap(other, 1)
    mine = mine + swap_by_core(mine, 2, 4)
    return mine + swap_by_core(mine, 4, 2)


def sum_replicas(x, reps):
    bit = 1
    while bit < reps:
        x = x + swap_rep(x, bit, reps)
        bit *= 2
    return x


def scatter_chips(back):
    return {chip: swap(getattr(back, f"sent{chip}"), chip) for chip in (2, 4, 6)}


def scatter_cores(back, received):
    total = back.sent1.astype(F32)
    for chip in (2, 4, 6):
        total = total + received[chip][1].astype(F32)
    return received | {1: swap(total.astype(BF16), 1)[None]}


def scatter_chip_sums(got, near):
    received = {1: got}
    for i, chip in enumerate((2, 4, 6)):
        total = near[i].astype(F32) + got[i + 1].astype(F32)
        received[chip] = swap(total.astype(BF16)[None], chip)
    return received


def table_at(layer):
    return 3 * D + layer * (11 * D + HEADS * RB)


def small_blocks(small):
    parts, tables = [small[: 3 * D]], []
    for layer in range(LAYERS):
        at = table_at(layer)
        parts.append(small[at : at + 11 * D])
        tables.append(small[at + 11 * D : at + 11 * D + HEADS * RB])
    parts += [small[table_at(LAYERS) :], jnp.full((CPAD - CLASSES,), -1e30, F32)]
    vecs = jnp.concatenate(parts)
    tables = jnp.stack(tables).reshape(LAYERS, HEADS, 2 * KER - 1, 2 * KER - 1)
    tables = jnp.pad(tables, ((0, 0), (0, 0), (0, 3), (0, 3))).reshape(LAYERS, HEADS, WIDE)
    return vecs.reshape(-1, D), tables


def small_vector(vgrads, tables, head_bias):
    parts = [vgrads[0][11:14].reshape(-1)]
    for layer in range(LAYERS):
        table = tables[layer].reshape(HEADS, 16, 16)[:, : 2 * KER - 1, : 2 * KER - 1]
        parts += [vgrads[layer][:11].reshape(-1), table.reshape(-1)]
    return jnp.concatenate([*parts, vgrads[1][11:13].reshape(-1), head_bias[:CLASSES]])


def group_parts(group, conv, qkv, proj, up, down, head):
    layer = [m[group] for m in (qkv, proj, up, down)]
    return [conv] + layer if group == 0 else layer + [head]


def step(mesh, args):
    (
        features, labels, counts, tables, *rest
    ) = args
    weights, moms, errs, facs = rest[0:6], rest[6:12], rest[12:18], rest[18:24]
    small_params, small_mom = rest[24:]
    reps = mesh.shape[REP]
    quick = mesh.shape[FSDP] == SHARDS and reps & (reps - 1) == 0
    slots = features.shape[0]
    items = max(n for n in (1, 2, 3) if slots % n == 0)

    if quick:
        ends = [pieces_of(SHARDS, group)[1] for group in range(2)]
        packed, second = pack_weights(weights, counts)
        near = gather_chips(packed)
        near[0], second, features, labels, counts, small_params = lax.optimization_barrier(
            (packed, second, features, labels, counts, small_params)
        )
        me = lax.axis_index(FSDP).astype(jnp.int32)[None]
        me = jnp.concatenate([me, counts[0], labels])
        vecs, bias_tables = small_blocks(small_params)
        patches = make_patches(features)
        bias = make_bias(me, bias_tables)
        pair, patches, bias, vecs, *near = lax.optimization_barrier((gather_pair(second), patches, bias, vecs, *near))
        sources0 = with_sibling(near, ends[0])
        sources1 = spread_pair(pair, ends[1])
    else:
        me = jnp.concatenate([jnp.zeros((1,), jnp.int32), counts[0], labels])
        sides = [lax.all_gather(w.astype(BF16), FSDP, axis=w.ndim - 2, tiled=True) for w in weights]
        sources = []
        for group in range(2):
            parts = group_parts(group, *sides)
            shards = [pack([p.reshape(SHARDS, -1, p.shape[1])[s] for p in parts]) for s in range(SHARDS)]
            sources.append([(jnp.stack(shards), 0, shards[0].shape[0], tuple(range(SHARDS)))])
        sources0, sources1 = sources

    if not quick:
        vecs, bias_tables = small_blocks(small_params)
        bias = make_bias(me, bias_tables)
        patches = make_patches(features)
    zero = forward_zero(me, patches, sources0, vecs, bias, items)
    one = forward_one(me, zero.hidden, sources1, vecs, bias, items)
    if quick:
        count = [zero.count, *[swap_rep(zero.count, offset, reps) for offset in range(1, reps)]]
        count, *held = lax.optimization_barrier((count, *vars(one).values()))
        one = types.SimpleNamespace(**dict(zip(vars(one), held)))
    else:
        count = [jnp.broadcast_to(lax.psum(counts.astype(F32), (REP, FSDP)), (8, 128))]
    turned = [jnp.swapaxes(f, -1, -2) for f in facs]
    sum_type = BF16 if quick else F32
    own_errs = errs
    if not quick:
        own_errs = [jnp.zeros((1,) + (w.shape[:-2] + (full // SHARDS, w.shape[-1])), F32) for w, full in zip(weights, FULL_ROWS)]
    back_one = backward_one(me, zero.hidden, one, vecs, count, own_errs, turned, items, sum_type)
    item_count = back_one.sums[8, 0]
    if quick:
        received = [None, scatter_chips(back_one)]
    back_zero = backward_zero(me, back_one, zero, patches, vecs, own_errs, turned, items, sum_type)
    if quick:
        received[1], *held = lax.optimization_barrier((received[1], *vars(back_zero).values()))
        back_zero = types.SimpleNamespace(**dict(zip(vars(back_zero), held)))
    tables_grad = [table_grad(me, b.bgrad, layer) for layer, b in enumerate((back_zero, back_one))]
    if not quick:
        grads = [whole_matrices(group, b.whole) for group, b in ((0, back_zero), (1, back_one))]
        small = small_vector((back_zero.vgrad, back_one.vgrad), tables_grad, back_one.hb_grad[0])
        loss = lax.psum(back_one.sums[0, 0], (REP, FSDP))
        return (loss, item_count, *general_tail(grads, weights, moms, errs, facs, small, small_params, small_mom))

    far = swap(back_zero.far, 1)
    left = back_zero.mine + swap(back_zero.other, 1)
    left = left + swap_by_core(left, 2, 4)
    left, tables_grad[1], item_count = lax.optimization_barrier((left, tables_grad[1], back_one.sums[8, 0]))
    left = left + swap_by_core(left, 4, 2)
    left, tables_grad[0] = lax.optimization_barrier((left, tables_grad[0]))
    far, _ = lax.optimization_barrier((far, left))
    received[0] = scatter_chip_sums(far, back_zero.near)
    left = sum_replicas(left, reps)
    left_other = swap(left, 1)
    left, left_other, received[0] = lax.optimization_barrier((left, left_other, received[0]))
    factors = right_factors(me, (left, left_other), back_zero.whole, back_one.whole, tables_grad)
    received[1] = scatter_cores(back_one, received[1])
    mine = sum_replica(factors.mine, factors.other)
    every = sum_replicas(mine, reps)
    updated = apply_update(
        me,
        weights,
        moms,
        turned,
        (mine, swap(mine, 1), every, swap(every, 1)),
        (factors.basis0, factors.basis1),
        (back_zero.own, back_one.own),
        received,
    )
    odd = (me[0] & 1) == 1
    summed = jnp.where(odd, left, left_other)[:, HALF_LEFT - SMALLS :]
    vgrads = []
    for layer in range(LAYERS):
        first, second = summed[:, 512 * layer : 512 * layer + D], summed[:, 512 * layer + D : 512 * (layer + 1)]
        vgrads.append(jnp.concatenate([first, second], axis=0))
    head_bias_grad = summed[:, 1024 : 1024 + 128].reshape(-1)
    loss = summed[0, 1024 + 128]
    table_sums = [updated.small[:, WIDE * i : WIDE * (i + 1)] for i in range(2)]
    new_small_mom = MOMENTUM * small_mom + small_vector(vgrads, table_sums, head_bias_grad)
    return (
        loss,
        item_count,
        *[getattr(updated, "new_" + n) for n in NAMES],
        *[getattr(updated, "new_mom_" + n) for n in NAMES],
        *[getattr(updated, "err_" + n) for n in NAMES],
        *[jnp.swapaxes(getattr(updated, "new_fac_" + n), -1, -2) for n in NAMES],
        small_params - SMALL_RATE * new_small_mom,
        new_small_mom,
    )


FULL_ROWS = (9 * CIN, D, D, D, FF, D)


def whole_matrices(group, packed):
    out = {}
    for name, (at, rows, blocks) in pieces_of(SHARDS, group)[0].items():
        cols = [packed[:, at + c * rows : at + (c + 1) * rows, :].reshape(SHARDS * rows, D) for c in range(blocks)]
        out[name] = jnp.concatenate(cols, axis=1)
    return out


def orthonormal(product, gram_mat):
    lower_tri = jnp.linalg.cholesky(gram_mat)
    return jnp.swapaxes(
        jax.scipy.linalg.solve_triangular(lower_tri, jnp.swapaxes(product, 1, 2), lower=True), 1, 2
    )


def general_tail(grads, weights, moms, errs, facs, small, small_params, small_mom):
    layer = [jnp.stack([grads[g][n] for g in range(2)]) for n in MATRIX_NAMES]
    wholes = [grads[0]["conv"][None], *layer, grads[1]["head"][None, :, :CLASSES]]
    lift = lambda xs: [xs[0][None], *xs[1:5], xs[5][None]]
    weights, moms, facs = lift(weights), lift(moms), lift(facs)
    errors = [errs[0], *[e[0] for e in errs[1:5]], errs[5]]
    merged = [
        lax.psum_scatter(g, FSDP, scatter_dimension=1, tiled=True) + e for g, e in zip(wholes, errors)
    ]
    lefts = lax.psum(
        [jnp.einsum("bio,bok->bik", m, f, precision=PRECISE) for m, f in zip(merged, facs)], "rep"
    )
    grams = lax.psum([jnp.einsum("bik,bil->bkl", p, p, precision=PRECISE) for p in lefts], FSDP)
    bases = [orthonormal(p, g) for p, g in zip(lefts, grams)]
    local = [jnp.einsum("bio,bik->bok", m, b, precision=PRECISE) for m, b in zip(merged, bases)]
    mine = lax.psum([*local, small], FSDP)
    every = lax.psum(mine, REP)
    product = lambda b, q: jnp.einsum("bik,bok->bio", b, q, precision=PRECISE)
    new_errs = [m - product(b, q) for m, b, q in zip(merged, bases, mine)]
    new_moms = [MOMENTUM * m + product(b, q) for m, b, q in zip(moms, bases, every)]
    new_weights = [w - LEARN_RATE * m for w, m in zip(weights, new_moms)]
    drop = lambda xs: [xs[0][0], *xs[1:5], xs[5][0]]
    new_small_mom = MOMENTUM * small_mom + every[6]
    return (
        *drop(new_weights),
        *drop(new_moms),
        new_errs[0],
        *[e[None] for e in new_errs[1:5]],
        new_errs[5],
        *drop(every[:6]),
        small_params - SMALL_RATE * new_small_mom,
        new_small_mom,
    )


def solution(mesh):
    rows, mids = P(FSDP, None), P(None, FSDP, None)
    matrices = (rows, mids, mids, mids, mids, rows)
    errors = (
        P(REP, FSDP, None),
        *[P(REP, None, FSDP, None)] * 4,
        P(REP, FSDP, None),
    )
    return jax.shard_map(
        lambda *args: step(mesh, args),
        mesh=mesh,
        in_specs=(
            P((REP, FSDP), None, None, None),
            P((REP, FSDP)),
            P(REP, FSDP),
            P(),
            *matrices,
            *matrices,
            *errors,
            *[P()] * 8,
        ),
        out_specs=(P(), P(), *matrices, *matrices, *errors, *[P()] * 8),
        check_vma=False,
    )
```

```python
import functools
import types

import jax
import jax.numpy as jnp
import numpy as np
from jax import lax
from jax.experimental import pallas as pl
from jax.experimental.pallas import tpu as pltpu
from jax.sharding import PartitionSpec as P

D = 256
HEADS = 8
HEAD = 32
FF = 768
CLASSES = 1000
CPAD = 1024
CIN = 128
GRID = 14
KER = 7
LAYERS = 2
PIX = 196
RB = 169
RANK = 8

EPSILON = 1e-05
MASKED = -1000000000.0
MOMENTUM = 0.9
LEARN_RATE = 16.0
SMALL_RATE = 4.0
PRECISE = lax.Precision.HIGHEST
SCALE = HEAD ** (-0.5)
LOG2E = 1.4426950408889634

COLS = 16
TOK = GRID * COLS
KEYS = 128
HALF = 128
PARTS = 3 * CIN
FSDP, REP = "fsdp", "rep"
F32 = jnp.float32
BF16 = jnp.bfloat16
VMEM_LIMIT = 58 * 1024 * 1024
SMALL_LIMIT = 20 * 1024 * 1024

GROUPS = (
    ((0, 80, 0), (80, 32, 32), (112, 32, 64), (144, 80, 96)),
    ((0, 112, 0), (112, 112, 96)),
)


def row_order(layer):
    if layer % 2 == 0:
        return list(range(GRID))
    return [*range(0, GRID, 2), *range(1, GRID, 2)]


def window_start(cell, dil):
    residue, position = cell % dil, cell // dil
    length = (GRID - residue + dil - 1) // dil
    return min(max(position - KER // 2, 0), length - KER)


def in_window(query, key, dil):
    if query % dil != key % dil:
        return False
    first = window_start(query, dil)
    return first <= key // dil < first + KER


@functools.lru_cache(None)
def static_maps(layer):
    dil = 1 + layer % 2
    order = row_order(layer)
    starts = np.zeros(GRID, np.int64)
    mask = np.zeros((TOK, KEYS), np.float32)
    for q0, nq, k0 in GROUPS[layer % 2]:
        for place in range(q0 // COLS, (q0 + nq) // COLS):
            qy = order[place]
            for j in range(8):
                ky = order[k0 // COLS + j]
                if not in_window(qy, ky, dil):
                    continue
                starts[place] = ky // dil - qy // dil + KER - 1 - j
                for x in range(GRID):
                    for kx in range(GRID):
                        if in_window(x, kx, dil):
                            mask[place * COLS + x, j * COLS + kx] = 1.0
    shifts = np.zeros((COLS, KEYS, KEYS), np.float32)
    for x in range(GRID):
        for kx in range(GRID):
            if in_window(x, kx, dil):
                dx = kx // dil - x // dil + KER - 1
                for j in range(8):
                    shifts[x, j * COLS + dx, j * COLS + kx] = 1.0
    return starts, shifts, mask


def norm_stats(values):
    centred = values - jnp.mean(values, axis=-1, keepdims=True)
    rstd = lax.rsqrt(jnp.mean(centred * centred, axis=-1, keepdims=True) + EPSILON)
    return centred * rstd, rstd


def norm_back(grad, xhat, rstd, gain):
    scaled = grad * gain
    mean_one = jnp.mean(scaled, axis=-1, keepdims=True)
    mean_two = jnp.mean(scaled * xhat, axis=-1, keepdims=True)
    return rstd * (scaled - mean_one - xhat * mean_two)


def col_sum(values):
    return jnp.sum(values, axis=0, keepdims=True)


def dot_nn(a, b, **kw):
    return lax.dot_general(a, b, (((1,), (0,)), ((), ())), preferred_element_type=F32, **kw)


def dot_nt(a, b, **kw):
    return lax.dot_general(a, b, (((1,), (1,)), ((), ())), preferred_element_type=F32, **kw)


def dot_tn(a, b, **kw):
    return lax.dot_general(a, b, (((0,), (0,)), ((), ())), preferred_element_type=F32, **kw)


ERFC_T = 0.44
ERFC_POLY = (
    0.24822096599679971,
    0.24887097779118345,
    0.21731489562842682,
    0.21580753897325447,
    -0.020171305217729862,
    0.2966767736009737,
    -0.2779414931115683,
    0.07122182759012696,
)


def gelu_parts(x):
    bell = jnp.exp2(x * x * (-0.5 * LOG2E))
    t = 1.0 / (1.0 + (ERFC_T * 0.5**0.5) * jnp.abs(x))
    poly = jnp.full_like(t, 0.5 * ERFC_POLY[-1])
    for c in ERFC_POLY[-2::-1]:
        poly = poly * t + 0.5 * c
    tail = poly * t * bell
    cdf = jnp.where(x < 0, tail, 1.0 - tail)
    return x * cdf, cdf + x * bell * (1.0 / (2.0 * np.pi) ** 0.5)


def head_masks():
    lane = lax.broadcasted_iota(jnp.int32, (1, HALF), 1)
    return [jnp.where(lane // HEAD == h, 1.0, 0.0).astype(BF16) for h in range(4)]


def spread_heads(block, masks):
    return jnp.concatenate([block * m for m in masks], axis=0)


def whole(shape):
    return pl.BlockSpec(shape, lambda *_: (0,) * len(shape))


def params(limit=VMEM_LIMIT):
    return pltpu.CompilerParams(dimension_semantics=("arbitrary",), vmem_limit_bytes=limit)


def cost(micros):
    return pl.CostEstimate(flops=int(micros * 1.1e9), bytes_accessed=0, transcendentals=0)


def call(name, kernel, steps, me, ins, outs, scratch, micros, limit=VMEM_LIMIT):
    names = ["me", *[e[0] for e in ins], *[e[0] for e in outs], *[e[0] for e in scratch]]

    def body(*refs):
        kernel(types.SimpleNamespace(**dict(zip(names, refs, strict=True))))

    results = pl.pallas_call(
        body,
        grid_spec=pltpu.PrefetchScalarGridSpec(
            num_scalar_prefetch=1,
            grid=(steps,),
            in_specs=[e[2] or whole(e[1].shape) for e in ins],
            out_specs=[e[3] or whole(e[1]) for e in outs],
            scratch_shapes=[pltpu.VMEM(e[1], e[2]) for e in scratch],
        ),
        out_shape=[jax.ShapeDtypeStruct(e[1], e[2]) for e in outs],
        compiler_params=params(limit),
        cost_estimate=cost(micros),
        name=name,
    )(me, *[e[1] for e in ins])
    return types.SimpleNamespace(**dict(zip([e[0] for e in outs], results, strict=True)))


def patch_kernel(feat_ref, out_ref, wide_ref, patch_ref):
    @pl.when(pl.program_id(0) == 0)
    def _():
        patch_ref[...] = jnp.zeros_like(patch_ref)

    for item in range(feat_ref.shape[0]):
        wide_ref[item, :, 0 : 2 * GRID, :] = feat_ref[item].astype(F32)
        even = wide_ref[item, :, pl.ds(0, GRID, stride=2), :]
        odd = wide_ref[item, :, pl.ds(1, GRID, stride=2), :]
        patch_ref[item, :, 1 : GRID + 1, 0:CIN] = odd
        patch_ref[item, :, 0:GRID, CIN : 2 * CIN] = even
        patch_ref[item, :, 0:GRID, 2 * CIN : 3 * CIN] = odd
        both = patch_ref[item].astype(BF16).reshape(GRID, 2, COLS, PARTS)
        for par in range(2):
            out_ref[item, par] = both[:, par].reshape(TOK, PARTS)


def make_patches(features):
    slots = features.shape[0]
    items = max(n for n in (1, 2, 3, 4) if slots % n == 0)
    return pl.pallas_call(
        patch_kernel,
        grid=(slots // items,),
        in_specs=[pl.BlockSpec((items, 2 * GRID, 2 * GRID, CIN), lambda i: (i, 0, 0, 0))],
        out_specs=pl.BlockSpec((items, 2, TOK, PARTS), lambda i: (i, 0, 0, 0)),
        out_shape=jax.ShapeDtypeStruct((slots, 2, TOK, PARTS), BF16),
        scratch_shapes=[
            pltpu.VMEM((items, 2 * GRID, 32, CIN), F32),
            pltpu.VMEM((items, 2 * GRID, COLS, PARTS), F32),
        ],
        compiler_params=params(),
        cost_estimate=cost(7),
        name="patches",
    )(features)


WIDE = 16 * COLS


def split_three(x):
    high = x.astype(BF16).astype(F32)
    mid = (x - high).astype(BF16).astype(F32)
    return jnp.concatenate([high, mid, x - high - mid], axis=0).astype(BF16)


def exact_dot(dot, x, hot):
    n = x.shape[0]
    out = dot(split_three(x), hot)
    return out[0:n] + out[n : 2 * n] + out[2 * n : 3 * n]


def shift_arrays():
    return np.stack([static_maps(layer)[1] for layer in range(LAYERS)])


def make_bias(me, tables):
    shifts = jnp.asarray(shift_arrays(), BF16)
    masks = jnp.asarray(np.stack([static_maps(layer)[2] for layer in range(LAYERS)]))

    def kernel(r):
        for layer in range(LAYERS):

            @pl.when(pl.program_id(0) == layer)
            def _():
                for y, start in enumerate(static_maps(layer)[0]):
                    moved = pltpu.roll(r.table[0], int(-COLS * start) % WIDE, 1)
                    r.rows[pl.ds(y, HEADS, stride=GRID), :] = moved[:, :KEYS]

        rows = r.rows[...]
        for x in range(GRID):
            r.flat[pl.ds(x, HEADS * GRID, stride=COLS), :] = exact_dot(dot_nn, rows, r.shift[0, x])
        for x in range(GRID, COLS):
            r.flat[pl.ds(x, HEADS * GRID, stride=COLS), :] = jnp.zeros((HEADS * GRID, KEYS), F32)
        for h in range(HEADS):
            block = r.flat[h * TOK : (h + 1) * TOK, :]
            r.out[0, h] = jnp.where(r.mask[0] > 0.5, block * LOG2E, MASKED)

    return call(
        "bias",
        kernel,
        LAYERS,
        me,
        [
            ("table", tables, pl.BlockSpec((1, HEADS, WIDE), lambda i, *_: (i, 0, 0))),
            ("shift", shifts, pl.BlockSpec((1, COLS, KEYS, KEYS), lambda i, *_: (i, 0, 0, 0))),
            ("mask", masks, pl.BlockSpec((1, TOK, KEYS), lambda i, *_: (i, 0, 0))),
        ],
        [
            (
                "out",
                (LAYERS, HEADS, TOK, KEYS),
                F32,
                pl.BlockSpec((1, HEADS, TOK, KEYS), lambda i, *_: (i, 0, 0, 0)),
            )
        ],
        [("flat", (HEADS * TOK, KEYS), F32), ("rows", (HEADS * GRID, KEYS), F32)],
        5,
    ).out


def table_grads(me, zero, one):
    back = jnp.asarray(np.swapaxes(shift_arrays(), -1, -2), BF16)

    def kernel(r):
        for layer, grad in enumerate((r.grad0, r.grad1)):
            total = None
            for x in range(GRID):
                part = grad[pl.ds(x, HEADS * GRID, stride=COLS), :]
                part = exact_dot(dot_nn, part, r.back[layer, x])
                total = part if total is None else total + part
            r.rows[layer] = total
        for layer, out in enumerate((r.out0, r.out1)):
            result = None
            for y, start in enumerate(static_maps(layer)[0]):
                part = pad_lanes(r.rows[layer, pl.ds(y, HEADS, stride=GRID), :], WIDE)
                moved = pltpu.roll(part, int(COLS * start) % WIDE, 1)
                result = moved if result is None else result + moved
            out[...] = result

    out = call(
        "tables",
        kernel,
        1,
        me,
        [("grad0", zero, None), ("grad1", one, None), ("back", back, None)],
        [("out0", (HEADS, WIDE), F32, None), ("out1", (HEADS, WIDE), F32, None)],
        [("rows", (LAYERS, HEADS * GRID, KEYS), F32)],
        5,
    )
    return [out.out0, out.out1]


def pieces_of(shards, group):
    narrow, wide = D // shards, FF // shards
    sizes = [("qkv", narrow, 3), ("proj", narrow, 1), ("up", narrow, 3), ("down", wide, 1)]
    if group == 0:
        sizes = [("conv", 9 * CIN // shards, 1)] + sizes
    else:
        sizes = sizes + [("head", narrow, 4)]
    out, at = {}, 0
    for name, rows, blocks in sizes:
        out[name] = (at, rows, blocks)
        at += rows * blocks
    return out, at


SHARDS = 8
COUNT_ROWS = 16
NAMES = ("conv", "qkv", "proj", "up", "down", "head")
WHOLE_NAMES = ("conv", "head")


def pack(parts):
    out = []
    for part in parts:
        if part.shape[1] == CLASSES:
            part = jnp.pad(part, ((0, 0), (0, CPAD - CLASSES)))
        out += [part[:, c : c + D] for c in range(0, part.shape[1], D)]
    return jnp.concatenate(out, axis=0)


def pack_weights(weights, counts):
    def kernel(r):
        for group, packed in ((0, r.packed0), (1, r.packed1)):
            for name, (at, rows, blocks) in pieces_of(SHARDS, group)[0].items():
                ref = getattr(r, name)
                for c in range(blocks):
                    width = min(D, ref.shape[-1] - c * D)
                    cols = slice(c * D, c * D + width)
                    value = ref[:, cols] if name in WHOLE_NAMES else ref[group, :, cols]
                    value = value.astype(BF16)
                    if width < D:
                        value = jnp.concatenate([value, jnp.zeros((rows, D - width), BF16)], axis=1)
                    packed[at + c * rows : at + (c + 1) * rows, :] = value
        end = pieces_of(SHARDS, 0)[1]
        r.packed0[end : end + COUNT_ROWS, :] = jnp.broadcast_to(r.count[...].astype(F32), (COUNT_ROWS, D)).astype(BF16)

    ends = [pieces_of(SHARDS, group)[1] for group in range(2)]
    out = call(
        "pack",
        kernel,
        1,
        jnp.zeros((1,), jnp.int32),
        [*[(n, w, None) for n, w in zip(NAMES, weights)], ("count", counts, None)],
        [("packed0", (ends[0] + COUNT_ROWS, D), BF16, None), ("packed1", (ends[1], D), BF16, None)],
        [],
        2,
    )
    return out.packed0, out.packed1


def unpack_weights(me, sources, targets, group):
    layout, _ = pieces_of(SHARDS, group)
    for ref, low, high, offsets in sources:
        for p, offset in enumerate(offsets):
            owner = me ^ offset
            for name, target in targets.items():
                at, rows, blocks = layout[name]
                if not low <= at < high:
                    continue
                place = pl.ds(pl.multiple_of(owner * rows, 16), rows)
                for c in range(blocks):
                    first = at - low + c * rows
                    target[place, c * D : (c + 1) * D] = ref[p, first : first + rows, :]


def units(layer, items):
    return [(n, n * TOK, group, hf) for n in range(items) for group in GROUPS[layer] for hf in range(2)]


def lanes_of(which, hf):
    return slice(which * D + hf * HALF, which * D + (hf + 1) * HALF)


def scores_of(hf):
    return slice(hf * 4 * KEYS, (hf + 1) * 4 * KEYS)


def attend(layer, items, joined_ref, bias_ref, score_ref, probs_ref, mixed_ref):
    masks = head_masks()
    for item, base, (q0, nq, k0), hf in units(layer, items):
        query = joined_ref[base + q0 : base + q0 + nq, lanes_of(0, hf)]
        keys = spread_heads(joined_ref[base + k0 : base + k0 + KEYS, lanes_of(1, hf)], masks)
        score_ref[item, q0 : q0 + nq, scores_of(hf)] = dot_nt(query, keys)
    for item in range(items):
        for q0, nq, k0 in GROUPS[layer]:
            for head in range(HEADS):
                place = (item, slice(q0, q0 + nq), slice(head * KEYS, (head + 1) * KEYS))
                s = score_ref[place] * (SCALE * LOG2E) + bias_ref[0, head, q0 : q0 + nq, :]
                e = jnp.exp2(s - jnp.max(s, axis=-1, keepdims=True))
                probs_ref[place] = (e * (1.0 / jnp.sum(e, axis=-1, keepdims=True))).astype(BF16)
    for item, base, (q0, nq, k0), hf in units(layer, items):
        values = spread_heads(joined_ref[base + k0 : base + k0 + KEYS, lanes_of(2, hf)], masks)
        mixed = dot_nn(probs_ref[item, q0 : q0 + nq, scores_of(hf)], values)
        mixed_ref[base + q0 : base + q0 + nq, lanes_of(0, hf)] = mixed.astype(BF16)


def layer_forward(layer, hidden, vec_ref, weights, bias_ref, outs, work, items):
    joined_ref, probs_ref, mixed_ref, after_ref, slope_ref, active_ref = outs
    score_ref, pre_ref = work
    vec = lambda i: vec_ref[LAYER_AT[layer] + i : LAYER_AT[layer] + i + 1, :]
    xhat, _ = norm_stats(hidden)
    normed = (xhat * vec(0) + vec(1)).astype(BF16)
    for c in range(3):
        part = dot_nn(normed, weights["qkv"][:, c * D : (c + 1) * D])
        if c != 1:
            part = part + vec(2 if c == 0 else 3)
        joined_ref[:, c * D : (c + 1) * D] = part.astype(BF16)
    attend(layer, items, joined_ref, bias_ref, score_ref, probs_ref, mixed_ref)
    after = hidden + (dot_nn(mixed_ref[...], weights["proj"][...]) + vec(4))
    after_ref[...] = after
    xhat, _ = norm_stats(after)
    normed = (xhat * vec(5) + vec(6)).astype(BF16)
    for c in range(3):
        cols = slice(c * D, (c + 1) * D)
        pre_ref[:, cols] = dot_nn(normed, weights["up"][:, cols])
    for c in range(3):
        cols = slice(c * D, (c + 1) * D)
        active, slope = gelu_parts(pre_ref[:, cols] + vec(8 + c))
        slope_ref[:, cols] = slope.astype(BF16)
        active_ref[:, cols] = active.astype(BF16)
    return after_ref[...] + (dot_nn(active_ref[...], weights["down"][...]) + vec(7))


def conv_taps(patch_ref, item):
    odd = patch_ref[item, 1]
    up = jnp.concatenate([jnp.zeros((COLS, PARTS), BF16), odd[: TOK - COLS]], axis=0)
    return up, patch_ref[item, 0], odd


CACHE = (
    ("joined", 3 * D, BF16),
    ("probs", None, BF16),
    ("mixed", D, BF16),
    ("after", D, F32),
    ("slope", FF, BF16),
    ("active", FF, BF16),
)
MATRICES = (("qkv", (D, FF)), ("proj", (D, D)), ("up", (D, FF)), ("down", (FF, D)))
MATRIX_NAMES = [m[0] for m in MATRICES]


def token_spec(items, width=D):
    return pl.BlockSpec((items * TOK, width), lambda i, *_: (i, 0))


def cache_entries(slots, items):
    out = []
    for name, width, dtype in CACHE:
        if width is None:
            spec = pl.BlockSpec((items, TOK, HEADS * KEYS), lambda i, *_: (i, 0, 0))
            out.append((name, (slots, TOK, HEADS * KEYS), dtype, spec))
        else:
            out.append((name, (slots * TOK, width), dtype, token_spec(items, width)))
    return out


def forward_scratch(items):
    return [("scores", (items, TOK, HEADS * KEYS), F32), ("pre", (items * TOK, FF), F32)]


def caches_of(r):
    return tuple(getattr(r, entry[0]) for entry in CACHE)


def bias_spec(layer):
    return pl.BlockSpec((1, HEADS, TOK, KEYS), lambda i, *_: (layer, 0, 0, 0))


def patch_spec(items):
    return pl.BlockSpec((items, 2, TOK, PARTS), lambda i, *_: (i, 0, 0, 0))


def source_entries(sources):
    return [(f"source{i}", array, None) for i, (array, *_) in enumerate(sources)]


def sources_of(r, sources):
    return [(getattr(r, f"source{i}"), *entry[1:]) for i, entry in enumerate(sources)]


def count_of(sources):
    total = jnp.zeros((1, 1), F32)
    for ref, _, high, offsets in sources:
        if ref.shape[1] > high:
            for p in range(len(offsets)):
                total = total + ref[p, high : high + COUNT_ROWS, :].astype(F32)[0:1, 0:1]
    return total


CONV_AT, LAYER_AT, FINAL_AT, BIAS_AT = 0, (3, 14), 25, 27


def forward_zero(me, patches, sources, vecs, bias, items):
    slots = patches.shape[0]

    def kernel(r):
        names = ["conv_w", *MATRIX_NAMES]
        weights = {n: getattr(r, n) for n in names}

        @pl.when(pl.program_id(0) == 0)
        def _():
            targets = {n.removesuffix("_w"): ref for n, ref in weights.items()}
            unpack_weights(r.me[0], sources_of(r, sources), targets, 0)
            r.count[...] = jnp.broadcast_to(count_of(sources_of(r, sources)), r.count.shape)

        for item in range(items):
            taps = conv_taps(r.patch, item)
            total = None
            for a in range(3):
                part = dot_nn(taps[a], r.conv_w[a * PARTS : (a + 1) * PARTS, :])
                total = part if total is None else total + part
            r.conv[item * TOK : (item + 1) * TOK, :] = total + r.vecs[CONV_AT : CONV_AT + 1, :]
        xhat, _ = norm_stats(r.conv[...])
        hidden = xhat * r.vecs[CONV_AT + 1 : CONV_AT + 2, :] + r.vecs[CONV_AT + 2 : CONV_AT + 3, :]
        hidden = layer_forward(0, hidden, r.vecs, weights, r.bias, caches_of(r), (r.scores, r.pre), items)
        for item in range(items):
            for place, row in enumerate(row_order(1)):
                r.hidden[item * TOK + place * COLS : item * TOK + (place + 1) * COLS, :] = hidden[
                    item * TOK + row * COLS : item * TOK + (row + 1) * COLS
                ]

    return call(
        "fwd0",
        kernel,
        slots // items,
        me,
        [
            ("patch", patches, patch_spec(items)),
            *source_entries(sources),
            ("vecs", vecs, None),
            ("bias", bias, bias_spec(0)),
        ],
        [
            ("hidden", (slots * TOK, D), F32, token_spec(items)),
            ("conv", (slots * TOK, D), F32, token_spec(items)),
            *cache_entries(slots, items),
            *[(n, shape, BF16, None) for n, shape in MATRICES],
            ("count", (8, 128), F32, None),
        ],
        [("conv_w", (9 * CIN, D), BF16), *forward_scratch(items)],
        30,
    )


def real_cells():
    place = lax.broadcasted_iota(jnp.int32, (TOK, 1), 0)
    return jnp.where(place % COLS < GRID, 1.0, 0.0)


def classify(r, slots, counts):
    rows = r.pooled.shape[0]
    place = lax.broadcasted_iota(jnp.int32, (rows, 1), 0)
    label = jnp.full((rows, 1), -1, jnp.int32)
    for i in range(slots):
        label = jnp.where(place == i, r.me[2 + i], label)
    live = jnp.where(place < r.me[1], 1.0, 0.0)
    count = sum([getattr(r, f"count{i}")[0:1, 0:1] for i in range(counts)])
    pooled = r.pooled[...].astype(BF16)
    head_bias = jnp.concatenate([r.vecs[BIAS_AT + c : BIAS_AT + c + 1, :] for c in range(CPAD // D)], axis=1)
    logits = dot_nn(pooled, r.head[...]) + head_bias
    peak = jnp.max(logits, axis=-1, keepdims=True)
    log_total = peak + jnp.log(jnp.sum(jnp.exp(logits - peak), axis=-1, keepdims=True))
    lane = lax.broadcasted_iota(jnp.int32, logits.shape, 1)
    onehot = jnp.where(label == lane, 1.0, 0.0)
    picked = jnp.sum(onehot * logits, axis=-1, keepdims=True)
    loss = col_sum(live * (log_total - picked))
    row = lax.broadcasted_iota(jnp.int32, (8, 128), 0)
    r.sums[...] = jnp.where(row == 0, loss, jnp.where(row == 1, col_sum(live), count))
    d_logits = (jnp.exp(logits - log_total) - onehot) * ((1.0 / count) * live)
    d_logits = jnp.where(lane < CLASSES, d_logits, 0.0).astype(BF16)
    r.head_grad[...] = dot_tn(pooled, d_logits)
    r.hb_grad[...] = col_sum(d_logits.astype(F32))
    r.d_pooled[...] = dot_nt(d_logits, r.head[...]) * (1.0 / PIX)


def forward_one(me, hidden, sources, vecs, bias, items):
    slots = hidden.shape[0] // TOK
    rows = -(-slots // 16) * 16

    def kernel(r):
        weights = {n: getattr(r, n) for n in MATRIX_NAMES}
        step = pl.program_id(0)

        @pl.when(step == 0)
        def _():
            unpack_weights(r.me[0], sources_of(r, sources), weights | dict(head=r.head), 1)
            r.pooled[...] = jnp.zeros_like(r.pooled)

        out = layer_forward(1, r.hidden[...], r.vecs, weights, r.bias, caches_of(r), (r.scores, r.pre), items)
        r.out[...] = out
        xhat, _ = norm_stats(out)
        normed = xhat * r.vecs[FINAL_AT : FINAL_AT + 1, :] + r.vecs[FINAL_AT + 1 : FINAL_AT + 2, :]
        real = real_cells()
        for item in range(items):
            mean = col_sum(normed[item * TOK : (item + 1) * TOK] * real) * (1.0 / PIX)
            r.pooled[pl.ds(step * items + item, 1), :] = mean

    return call(
        "fwd1",
        kernel,
        slots // items,
        me,
        [
            ("hidden", hidden, token_spec(items)),
            *source_entries(sources),
            ("vecs", vecs, None),
            ("bias", bias, bias_spec(1)),
        ],
        [
            ("out", (slots * TOK, D), F32, token_spec(items)),
            *cache_entries(slots, items),
            *[(n, shape, BF16, None) for n, shape in MATRICES],
            ("head", (D, CPAD), BF16, None),
            ("pooled", (rows, D), F32, None),
        ],
        forward_scratch(items),
        28,
    )


def attend_back(layer, items, joined_ref, probs_ref, dmix_ref, djoin_ref, dkv_ref, dprob_ref, dscore_ref, bgrad_ref):
    masks = head_masks()
    for item, base, (q0, nq, k0), hf in units(layer, items):
        values = spread_heads(joined_ref[base + k0 : base + k0 + KEYS, lanes_of(2, hf)], masks)
        d_mix = dmix_ref[base + q0 : base + q0 + nq, lanes_of(0, hf)]
        dprob_ref[item, q0 : q0 + nq, scores_of(hf)] = dot_nt(d_mix, values)
    for q0, nq, k0 in GROUPS[layer]:
        for head in range(HEADS):
            total = None
            for item in range(items):
                place = (item, slice(q0, q0 + nq), slice(head * KEYS, (head + 1) * KEYS))
                p, dp = probs_ref[place].astype(F32), dprob_ref[place]
                ds = (p * (dp - jnp.sum(dp * p, axis=-1, keepdims=True))).astype(BF16)
                dscore_ref[place] = ds
                ds = ds.astype(F32)
                total = ds if total is None else total + ds
            bgrad_ref[head * TOK + q0 : head * TOK + q0 + nq, :] += total
    for item, base, (q0, nq, k0), hf in units(layer, items):
        keys = spread_heads(joined_ref[base + k0 : base + k0 + KEYS, lanes_of(1, hf)], masks)
        d_query = dot_nn(dscore_ref[item, q0 : q0 + nq, scores_of(hf)], keys) * SCALE
        djoin_ref[base + q0 : base + q0 + nq, lanes_of(0, hf)] = d_query.astype(BF16)
    dkv_ref[...] = jnp.zeros_like(dkv_ref)
    for item, base, (q0, nq, k0), hf in units(layer, items):
        qrows, krows = slice(base + q0, base + q0 + nq), slice(base + k0, base + k0 + KEYS)
        heads = [slice(h * KEYS, (h + 1) * KEYS) for h in range(hf * 4, hf * 4 + 4)]
        for which, left, right in ((0, joined_ref, dscore_ref), (1, dmix_ref, probs_ref)):
            turned = jnp.transpose(left[qrows, lanes_of(0, hf)])
            parts = []
            for h in range(4):
                parts.append(dot_nn(turned[h * HEAD : (h + 1) * HEAD], right[item, q0 : q0 + nq, heads[h]]))
            dkv_ref[krows, lanes_of(which, hf)] += jnp.transpose(jnp.concatenate(parts, axis=0))
    djoin_ref[:, D : 2 * D] = (dkv_ref[:, 0:D] * SCALE).astype(BF16)
    djoin_ref[:, 2 * D : 3 * D] = dkv_ref[:, D : 2 * D].astype(BF16)


def layer_backward(layer, d_out, hidden, vec_ref, weights, caches, work, grads, vgrad_ref, bgrad_ref, items):
    joined_ref, probs_ref, mixed_ref, after_ref, slope_ref, active_ref = caches
    dpre_ref, *work = work
    dmix_ref, djoin_ref = work[:2]
    vec = lambda i: vec_ref[LAYER_AT[layer] + i : LAYER_AT[layer] + i + 1, :]

    def add(row, value):
        vgrad_ref[row : row + 1, :] += value

    d_branch = d_out.astype(BF16)
    add(7, col_sum(d_branch.astype(F32)))
    for c in range(3):
        cols = slice(c * D, (c + 1) * D)
        dpre_ref[:, cols] = dot_nt(d_branch, weights["down"][cols, :])
    grads["down"][...] += dot_tn(d_branch, active_ref[...])
    for c in range(3):
        cols = slice(c * D, (c + 1) * D)
        d_pre = (dpre_ref[:, cols] * slope_ref[:, cols].astype(F32)).astype(BF16)
        djoin_ref[:, cols] = d_pre
        add(8 + c, col_sum(d_pre.astype(F32)))
    xhat, rstd = norm_stats(after_ref[...])
    normed = (xhat * vec(5) + vec(6)).astype(BF16)
    grads["up"][...] += dot_tn(normed, djoin_ref[...])
    d_normed = dot_nt(djoin_ref[...], weights["up"][...])
    add(5, col_sum(d_normed * xhat))
    add(6, col_sum(d_normed))
    d_after = d_out + norm_back(d_normed, xhat, rstd, vec(5))
    d_proj = d_after.astype(BF16)
    add(4, col_sum(d_proj.astype(F32)))
    grads["proj"][...] += dot_tn(mixed_ref[...], d_proj)
    dmix_ref[...] = dot_nt(d_proj, weights["proj"][...]).astype(BF16)
    attend_back(layer, items, joined_ref, probs_ref, *work, bgrad_ref)
    add(2, col_sum(djoin_ref[:, 0:D].astype(F32)))
    add(3, col_sum(djoin_ref[:, 2 * D : 3 * D].astype(F32)))
    xhat, rstd = norm_stats(hidden)
    normed = (xhat * vec(0) + vec(1)).astype(BF16)
    grads["qkv"][...] += dot_tn(normed, djoin_ref[...])
    d_normed = dot_nt(djoin_ref[...], weights["qkv"][...])
    add(0, col_sum(d_normed * xhat))
    add(1, col_sum(d_normed))
    return d_after + norm_back(d_normed, xhat, rstd, vec(0))


def split_two(x):
    high = x.astype(BF16)
    return high, (x - high.astype(F32)).astype(BF16)


def wide_dot(dot, rows, matrix):
    stacked = split_three(rows)
    high, low = split_two(matrix)
    out = dot(stacked, high) + dot(stacked, low)
    return out[0:RANK] + out[RANK : 2 * RANK] + out[2 * RANK : 3 * RANK]


def block_of(whole_ref, entry, c):
    at, rows, _ = entry
    return jnp.concatenate(
        [whole_ref[s, at + c * rows : at + (c + 1) * rows, :] for s in range(SHARDS)], axis=0
    )


def factor_of(r, group, name):
    ref = getattr(r, "fac_" + name)
    return ref[...] if name in WHOLE_NAMES else ref[group]


def finish_grads(r, group, grads):
    layout, _ = pieces_of(SHARDS, group)
    me = r.me[0]
    for name, (at, rows, blocks) in layout.items():
        matrix = grads[name]
        if name in ("down", "conv"):
            matrix = jnp.transpose(matrix[...])
        for s in range(SHARDS):
            for c in range(blocks):
                piece = matrix[s * rows : (s + 1) * rows, c * D : (c + 1) * D]
                r.sums_of[s, at + c * rows : at + (c + 1) * rows, :] = piece
    for name, (at, rows, blocks) in layout.items():
        err = getattr(r, "err_" + name)
        for c in range(blocks):
            width = min(D, err.shape[-1] - c * D)
            cols = slice(c * D, c * D + width)
            value = err[0, :, cols] if name in WHOLE_NAMES else err[0, group, :, cols]
            place = slice(at + c * rows, at + (c + 1) * rows)
            r.sums_of[me, place, 0:width] += value
    r.own[...] = r.sums_of[me]
    r.whole[...] = r.sums_of[...].astype(r.whole.dtype)
    if group == 0:
        for i, chip in enumerate((0, 2, 4, 6)):
            r.far[i] = r.sums_of[me ^ chip ^ 1].astype(BF16)
            if chip:
                r.near[i - 1] = r.sums_of[me ^ chip].astype(BF16)
    else:
        r.sent1[...] = r.sums_of[me ^ 1].astype(BF16)
        for chip in (2, 4, 6):
            for core in range(2):
                getattr(r, f"sent{chip}")[core] = r.sums_of[me ^ chip ^ core].astype(BF16)
    at_lane, lefts = 0, []
    for name, entry in layout.items():
        total = None
        for c in range(entry[2]):
            fac = factor_of(r, group, name)
            width = min(D, fac.shape[-1] - c * D)
            block = block_of(r.sums_of, entry, c)
            part = wide_dot(dot_nt, fac[:, c * D : c * D + width], block[:, :width])
            total = part if total is None else total + part
        lefts.append(total)
    return jnp.concatenate(lefts, axis=1)


def left_lanes(group):
    return sum(rows * SHARDS for _, rows, _ in pieces_of(SHARDS, group)[0].values())


def right_lanes(group):
    return sum(blocks * D for _, _, blocks in pieces_of(SHARDS, group)[0].values())


SMALLS = 2 * 512 + 128 + 128
HALF_LEFT = (left_lanes(0) + left_lanes(1) + SMALLS) // 2
HALF_RIGHT = (right_lanes(0) + right_lanes(1) + 2 * WIDE) // 2


def pad_lanes(x, lanes):
    return jnp.concatenate([x, jnp.zeros((x.shape[0], lanes - x.shape[1]), x.dtype)], axis=1)


def put_halves(r, whole):
    n = whole.shape[1] // 2
    first, second = whole[:, :n], whole[:, n:]
    odd = (r.me[0] & 1) == 1
    r.mine[...] = jnp.where(odd, second, first)
    r.other[...] = jnp.where(odd, first, second)


def get_halves(r, mine, other):
    odd = (r.me[0] & 1) == 1
    mine, other = mine[...], other[...]
    return jnp.concatenate([jnp.where(odd, other, mine), jnp.where(odd, mine, other)], axis=1)


def backward_outs(group, dtype):
    rows = pieces_of(SHARDS, group)[1]
    return [
        ("vgrad", (16, D), F32, None),
        ("bgrad", (HEADS * TOK, KEYS), F32, None),
        ("whole", (SHARDS, rows, D), dtype, None),
        ("own", (rows, D), F32, None),
    ]


def factor_inputs(group, errs, facs):
    out = []
    for name, err, fac in zip(NAMES, errs, facs):
        if name in pieces_of(SHARDS, group)[0]:
            out += [("err_" + name, err, None), ("fac_" + name, fac, None)]
    return out


def backward_scratch(items, group):
    return [
        ("sums_of", (SHARDS, pieces_of(SHARDS, group)[1], D), F32),
        ("d_pre", (items * TOK, FF), F32),
        ("d_mixed", (items * TOK, D), BF16),
        ("d_joined", (items * TOK, 3 * D), BF16),
        ("d_keys", (items * TOK, 2 * D), F32),
        ("d_probs", (items, TOK, HEADS * KEYS), F32),
        ("d_scores", (items, TOK, HEADS * KEYS), BF16),
        ("g_qkv", (D, FF), F32),
        ("g_proj", (D, D), F32),
        ("g_up", (D, FF), F32),
        ("g_down", (D, FF), F32),
    ]


def start_backward(r, grads):
    r.vgrad[...] = jnp.zeros_like(r.vgrad)
    r.bgrad[...] = jnp.zeros_like(r.bgrad)
    for ref in grads.values():
        ref[...] = jnp.zeros_like(ref)


def cache_inputs(caches, slots, items):
    return [(e[0], getattr(caches, e[0]), e[3]) for e in cache_entries(slots, items)]


def matrix_inputs(caches):
    return [(n, getattr(caches, n), None) for n in MATRIX_NAMES]


def backward_one(me, hidden, forward, vecs, count, errs, facs, items, dtype):
    slots = hidden.shape[0] // TOK

    def kernel(r):
        weights = {n: getattr(r, n) for n in MATRIX_NAMES}
        grads = {n: getattr(r, "g_" + n) for n in MATRIX_NAMES}
        step = pl.program_id(0)

        @pl.when(step == 0)
        def _():
            start_backward(r, grads)
            classify(r, slots, len(count))

        real = real_cells()
        d_final = jnp.concatenate(
            [real * r.d_pooled[pl.ds(step * items + item, 1), :] for item in range(items)], axis=0
        )
        xhat, rstd = norm_stats(r.out[...])
        r.vgrad[11:12, :] += col_sum(d_final * xhat)
        r.vgrad[12:13, :] += col_sum(d_final)
        d_out = norm_back(d_final, xhat, rstd, r.vecs[FINAL_AT : FINAL_AT + 1, :])
        work = (r.d_pre, r.d_mixed, r.d_joined, r.d_keys, r.d_probs, r.d_scores)
        r.d_hidden[...] = layer_backward(
            1, d_out, r.hidden[...], r.vecs, weights, caches_of(r), work, grads, r.vgrad, r.bgrad, items
        )

        @pl.when(step == pl.num_programs(0) - 1)
        def _():
            r.left[...] = finish_grads(r, 1, grads | dict(head=r.head_grad))

    return call(
        "back1",
        kernel,
        slots // items,
        me,
        [
            ("out", forward.out, token_spec(items)),
            ("pooled", forward.pooled, None),
            *[(f"count{i}", c, None) for i, c in enumerate(count)],
            ("hidden", hidden, token_spec(items)),
            *matrix_inputs(forward),
            ("head", forward.head, None),
            ("vecs", vecs, None),
            *cache_inputs(forward, slots, items),
            *factor_inputs(1, errs, facs),
        ],
        [
            ("d_hidden", hidden.shape, F32, token_spec(items)),
            *backward_outs(1, dtype),
            ("left", (RANK, left_lanes(1)), F32, None),
            ("sums", (8, 128), F32, None),
            ("hb_grad", (1, CPAD), F32, None),
            *[(f"sent{chip}", (2, pieces_of(SHARDS, 1)[1], D), BF16, None) for chip in (2, 4, 6)],
            ("sent1", (pieces_of(SHARDS, 1)[1], D), BF16, None),
        ],
        [*backward_scratch(items, 1), ("head_grad", (D, CPAD), F32), ("d_pooled", forward.pooled.shape, F32)],
        46,
    )


def backward_zero(me, back_one, forward, patches, vecs, errs, facs, items, dtype):
    slots = patches.shape[0]

    def kernel(r):
        weights = {n: getattr(r, n) for n in MATRIX_NAMES}
        grads = {n: getattr(r, "g_" + n) for n in [*MATRIX_NAMES, "conv"]}
        step = pl.program_id(0)

        @pl.when(step == 0)
        def _():
            start_backward(r, grads)

        order = row_order(1)
        rows = []
        for item in range(items):
            for row in range(GRID):
                first = item * TOK + order.index(row) * COLS
                rows.append(r.d_hidden[first : first + COLS, :])
        d_out = jnp.concatenate(rows, axis=0)
        conv_hat, conv_rstd = norm_stats(r.conv[...])
        gain = r.vecs[CONV_AT + 1 : CONV_AT + 2, :]
        hidden = conv_hat * gain + r.vecs[CONV_AT + 2 : CONV_AT + 3, :]
        work = (r.d_pre, r.d_mixed, r.d_joined, r.d_keys, r.d_probs, r.d_scores)
        d_conv = layer_backward(
            0, d_out, hidden, r.vecs, weights, caches_of(r), work, grads, r.vgrad, r.bgrad, items
        )
        r.vgrad[12:13, :] += col_sum(d_conv * conv_hat)
        r.vgrad[13:14, :] += col_sum(d_conv)
        d_conv = norm_back(d_conv, conv_hat, conv_rstd, gain).astype(BF16)
        r.vgrad[11:12, :] += col_sum(d_conv.astype(F32))
        for item in range(items):
            taps = conv_taps(r.patch, item)
            part = jnp.transpose(d_conv[item * TOK : (item + 1) * TOK])
            for a in range(3):
                grads["conv"][:, a * PARTS : (a + 1) * PARTS] += dot_nn(part, taps[a])

        @pl.when(step == pl.num_programs(0) - 1)
        def _():
            parts = [finish_grads(r, 0, grads), r.left_one[...]]
            for ref in (r.vgrad, r.vgrad_one):
                parts += [ref[0:8, :], ref[8:16, :]]
            put_halves(r, jnp.concatenate([*parts, r.head_bias[...], r.sums[...]], axis=1))

    return call(
        "back0",
        kernel,
        slots // items,
        me,
        [
            ("d_hidden", back_one.d_hidden, token_spec(items)),
            ("conv", forward.conv, token_spec(items)),
            ("patch", patches, patch_spec(items)),
            *matrix_inputs(forward),
            ("vecs", vecs, None),
            *cache_inputs(forward, slots, items),
            ("left_one", back_one.left, None),
            ("vgrad_one", back_one.vgrad, None),
            ("head_bias", back_one.hb_grad.reshape(8, 128), None),
            ("sums", back_one.sums, None),
            *factor_inputs(0, errs, facs),
        ],
        [
            *backward_outs(0, dtype),
            ("far", (4, pieces_of(SHARDS, 0)[1], D), BF16, None),
            ("near", (3, pieces_of(SHARDS, 0)[1], D), BF16, None),
            ("mine", (RANK, HALF_LEFT), F32, None),
            ("other", (RANK, HALF_LEFT), F32, None),
        ],
        [*backward_scratch(items, 0), ("g_conv", (D, 9 * CIN), F32)],
        63,
    )


def inverse_cholesky(gram):
    row = lax.broadcasted_iota(jnp.int32, (1, RANK, 2 * RANK), 1)
    lane = lax.broadcasted_iota(jnp.int32, (1, RANK, 2 * RANK), 2)
    eye = jnp.broadcast_to(jnp.where(lane == row + RANK, 1.0, 0.0), (gram.shape[0], RANK, 2 * RANK))
    work = jnp.concatenate([gram, jnp.zeros_like(gram)], axis=2) + eye
    for k in range(RANK):
        scale = 1.0 / jnp.sqrt(work[:, k : k + 1, k : k + 1])
        pivot = work[:, k : k + 1, :] * scale
        column = work[:, :, k : k + 1] * scale
        work = jnp.where(row > k, work - column * pivot, jnp.where(row == k, pivot, work))
    return work[:, :, RANK : 2 * RANK]


def basis_lanes(group):
    return sum(rows for _, rows, _ in pieces_of(SHARDS, group)[0].values())


def right_factors(me, left, whole_zero, whole_one, tables):
    def kernel(r):
        groups = (r.whole0, r.whole1)
        left = get_halves(r, r.left_mine, r.left_other)
        entries, at = [], 0
        for group in range(2):
            for entry in pieces_of(SHARDS, group)[0].values():
                entries.append((group, entry, left[:, at : at + entry[1] * SHARDS]))
                at += entry[1] * SHARDS
        grams = jnp.stack([dot_nt(x, x, precision=PRECISE) for _, _, x in entries])
        inverses = inverse_cholesky(grams)
        rows_of = [[], []]
        parts = []
        for i, (group, entry, x) in enumerate(entries):
            basis = dot_nn(inverses[i], x, precision=PRECISE)
            rows_of[group].append((basis, entry[1]))
            for c in range(entry[2]):
                parts.append(exact_dot(dot_nn, basis, block_of(groups[group], entry, c)))
        for group, out in ((0, r.basis0), (1, r.basis1)):
            for s in range(SHARDS):
                at = 0
                for basis, rows in rows_of[group]:
                    out[s, :, at : at + rows] = basis[:, s * rows : (s + 1) * rows]
                    at += rows
        put_halves(r, jnp.concatenate([*parts, r.table0[...], r.table1[...]], axis=1))

    return call(
        "right",
        kernel,
        1,
        me,
        [
            ("left_mine", left[0], None),
            ("left_other", left[1], None),
            ("whole0", whole_zero, None),
            ("whole1", whole_one, None),
            ("table0", tables[0], None),
            ("table1", tables[1], None),
        ],
        [
            ("mine", (RANK, HALF_RIGHT), F32, None),
            ("other", (RANK, HALF_RIGHT), F32, None),
            ("basis0", (SHARDS, RANK, basis_lanes(0)), F32, None),
            ("basis1", (SHARDS, RANK, basis_lanes(1)), F32, None),
        ],
        [],
        6,
        SMALL_LIMIT,
    )


def six_products(x, other):
    high = x.astype(BF16).astype(F32)
    mid = (x - high).astype(BF16).astype(F32)
    low = x - high - mid
    terms = [high, mid, high, mid, low, high] if other else [high, high, mid, mid, high, low]
    return jnp.concatenate(terms, axis=0).astype(BF16)


def apply_update(me, weights, moms, facs, right, factors, own, received):
    def kernel(r):
        right_mine = get_halves(r, r.rep_mine, r.rep_other)
        right_all = get_halves(r, r.all_mine, r.all_other)
        at_col = 0
        for group in range(2):
            total = getattr(r, f"own{group}")[...] + getattr(r, f"sib{group}")[0].astype(F32)
            for chip in (2, 4, 6):
                total = total + getattr(r, f"got{group}_{chip}")[0].astype(F32)
            basis = getattr(r, f"basis{group}")
            at_row = 0
            for name, (at, rows, blocks) in pieces_of(SHARDS, group)[0].items():
                left = six_products(basis[0, :, at_row : at_row + rows], False)
                at_row += rows
                single = name in WHOLE_NAMES
                for c in range(blocks):
                    width = min(D, (CLASSES if name == "head" else blocks * D) - c * D)
                    cols = slice(c * D, c * D + width)
                    place = (slice(None), cols) if single else (group, slice(None), cols)
                    err_place = (0, slice(None), cols) if single else (0, group, slice(None), cols)
                    right = slice(at_col, at_col + D)
                    at_col += D
                    getattr(r, "new_fac_" + name)[place] = right_all[:, right][:, :width]
                    mine = dot_tn(left, six_products(right_mine[:, right], True))
                    every = dot_tn(left, six_products(right_all[:, right], True))
                    merged = total[at + c * rows : at + (c + 1) * rows]
                    getattr(r, "err_" + name)[err_place] = (merged - mine)[:, :width]
                    mom = MOMENTUM * getattr(r, "mom_" + name)[place] + every[:, :width]
                    getattr(r, "new_mom_" + name)[place] = mom
                    getattr(r, "new_" + name)[place] = getattr(r, "w_" + name)[place] - LEARN_RATE * mom
        r.small[...] = right_all[:, at_col:]

    first = lambda x: pl.BlockSpec((1,) + x.shape[1:], lambda *_: (0, 0, 0))
    mine_spec = lambda x: pl.BlockSpec((1,) + x.shape[1:], lambda i, m: (m[0], 0, 0))
    small = 2 * HALF_RIGHT - right_lanes(0) - right_lanes(1)
    return call(
        "update",
        kernel,
        1,
        me,
        [
            *[("w_" + n, w, None) for n, w in zip(NAMES, weights)],
            *[("mom_" + n, m, None) for n, m in zip(NAMES, moms)],
            *zip(("rep_mine", "rep_other", "all_mine", "all_other"), right, [None] * 4),
            ("basis0", factors[0], mine_spec(factors[0])),
            ("basis1", factors[1], mine_spec(factors[1])),
            ("own0", own[0], None),
            ("own1", own[1], None),
            *[(f"got{g}_{c}", received[g][c], first(received[g][c])) for g in range(2) for c in (2, 4, 6)],
            *[(f"sib{g}", received[g][1], first(received[g][1])) for g in range(2)],
        ],
        [
            *[("new_" + n, w.shape, F32, None) for n, w in zip(NAMES, weights)],
            *[("new_mom_" + n, w.shape, F32, None) for n, w in zip(NAMES, weights)],
            *[("err_" + n, (1,) + w.shape, F32, None) for n, w in zip(NAMES, weights)],
            *[("new_fac_" + n, f.shape, F32, None) for n, f in zip(NAMES, facs)],
            ("small", (RANK, small), F32, None),
        ],
        [],
        5,
    )


def swap(x, offset):
    return lax.ppermute(x, FSDP, [(i, i ^ offset) for i in range(SHARDS)])


def swap_rep(x, offset, reps):
    return lax.ppermute(x, REP, [(i, i ^ offset) for i in range(reps)])


def gather_chips(packed):
    return [packed, *[swap(packed, chip) for chip in (2, 4, 6)]]


def with_sibling(near, end):
    near = jnp.stack(near)
    return [(near, 0, end, (0, 2, 4, 6)), (swap(near, 1), 0, end, (1, 3, 5, 7))]


def gather_pair(packed):
    return jnp.stack([packed, swap(packed, 1)])


def spread_pair(pair, end):
    out = [(pair, 0, end, (0, 1))]
    return out + [(swap(pair, chip), 0, end, (chip, chip ^ 1)) for chip in (2, 4, 6)]


def sum_chips(x):
    return (x + swap(x, 2)) + (swap(x, 4) + swap(x, 6))


def sum_replica(mine, other):
    return sum_chips(mine + swap(other, 1))


def sum_replicas(x, reps):
    bit = 1
    while bit < reps:
        x = x + swap_rep(x, bit, reps)
        bit *= 2
    return x


def scatter_chips(back):
    return {chip: swap(getattr(back, f"sent{chip}"), chip) for chip in (2, 4, 6)}


def scatter_cores(back, received):
    total = back.sent1.astype(F32)
    for chip in (2, 4, 6):
        total = total + received[chip][1].astype(F32)
    return received | {1: swap(total.astype(BF16), 1)[None]}


def scatter_chip_sums(got, near):
    received = {1: got}
    for i, chip in enumerate((2, 4, 6)):
        total = near[i].astype(F32) + got[i + 1].astype(F32)
        received[chip] = swap(total.astype(BF16)[None], chip)
    return received


def table_at(layer):
    return 3 * D + layer * (11 * D + HEADS * RB)


def small_blocks(small):
    parts, tables = [small[: 3 * D]], []
    for layer in range(LAYERS):
        at = table_at(layer)
        parts.append(small[at : at + 11 * D])
        tables.append(small[at + 11 * D : at + 11 * D + HEADS * RB])
    parts += [small[table_at(LAYERS) :], jnp.full((CPAD - CLASSES,), -1e30, F32)]
    vecs = jnp.concatenate(parts)
    tables = jnp.stack(tables).reshape(LAYERS, HEADS, 2 * KER - 1, 2 * KER - 1)
    tables = jnp.pad(tables, ((0, 0), (0, 0), (0, 3), (0, 3))).reshape(LAYERS, HEADS, WIDE)
    return vecs.reshape(-1, D), tables


def small_vector(vgrads, tables, head_bias):
    parts = [vgrads[0][11:14].reshape(-1)]
    for layer in range(LAYERS):
        table = tables[layer].reshape(HEADS, 16, 16)[:, : 2 * KER - 1, : 2 * KER - 1]
        parts += [vgrads[layer][:11].reshape(-1), table.reshape(-1)]
    return jnp.concatenate([*parts, vgrads[1][11:13].reshape(-1), head_bias[:CLASSES]])


def group_parts(group, conv, qkv, proj, up, down, head):
    layer = [m[group] for m in (qkv, proj, up, down)]
    return [conv] + layer if group == 0 else layer + [head]


def step(mesh, args):
    (
        features, labels, counts, tables, *rest
    ) = args
    weights, moms, errs, facs = rest[0:6], rest[6:12], rest[12:18], rest[18:24]
    small_params, small_mom = rest[24:]
    reps = mesh.shape[REP]
    quick = mesh.shape[FSDP] == SHARDS and reps & (reps - 1) == 0
    slots = features.shape[0]
    ahead = max(n for n in (1, 2, 3, 4) if slots % n == 0)
    items = max(n for n in (1, 2, 3) if slots % n == 0)

    if quick:
        ends = [pieces_of(SHARDS, group)[1] for group in range(2)]
        packed, second = pack_weights(weights, counts)
        near = gather_chips(packed)
        near[0], second, features, labels, counts, small_params = lax.optimization_barrier(
            (packed, second, features, labels, counts, small_params)
        )
        me = lax.axis_index(FSDP).astype(jnp.int32)[None]
        me = jnp.concatenate([me, counts[0], labels])
        vecs, bias_tables = small_blocks(small_params)
        patches = make_patches(features)
        bias = make_bias(me, bias_tables)
        pair, patches, bias, vecs, *near = lax.optimization_barrier((gather_pair(second), patches, bias, vecs, *near))
        sources0 = with_sibling(near, ends[0])
        sources1 = spread_pair(pair, ends[1])
    else:
        me = jnp.concatenate([jnp.zeros((1,), jnp.int32), counts[0], labels])
        sides = [lax.all_gather(w.astype(BF16), FSDP, axis=w.ndim - 2, tiled=True) for w in weights]
        sources = []
        for group in range(2):
            parts = group_parts(group, *sides)
            shards = [pack([p.reshape(SHARDS, -1, p.shape[1])[s] for p in parts]) for s in range(SHARDS)]
            sources.append([(jnp.stack(shards), 0, shards[0].shape[0], tuple(range(SHARDS)))])
        sources0, sources1 = sources

    if not quick:
        vecs, bias_tables = small_blocks(small_params)
        bias = make_bias(me, bias_tables)
        patches = make_patches(features)
    zero = forward_zero(me, patches, sources0, vecs, bias, ahead)
    one = forward_one(me, zero.hidden, sources1, vecs, bias, ahead)
    if quick:
        count = [zero.count, *[swap_rep(zero.count, offset, reps) for offset in range(1, reps)]]
        count, *held = lax.optimization_barrier((count, *vars(one).values()))
        one = types.SimpleNamespace(**dict(zip(vars(one), held)))
    else:
        count = [jnp.broadcast_to(lax.psum(counts.astype(F32), (REP, FSDP)), (8, 128))]
    turned = [jnp.swapaxes(f, -1, -2) for f in facs]
    sum_type = BF16 if quick else F32
    own_errs = errs
    if not quick:
        own_errs = [jnp.zeros((1,) + (w.shape[:-2] + (full // SHARDS, w.shape[-1])), F32) for w, full in zip(weights, FULL_ROWS)]
    back_one = backward_one(me, zero.hidden, one, vecs, count, own_errs, turned, items, sum_type)
    if quick:
        received = [None, scatter_chips(back_one)]
    back_zero = backward_zero(me, back_one, zero, patches, vecs, own_errs, turned, items, sum_type)
    if quick:
        received[1], *held = lax.optimization_barrier((received[1], *vars(back_zero).values()))
        back_zero = types.SimpleNamespace(**dict(zip(vars(back_zero), held)))
    tables_grad = table_grads(me, back_zero.bgrad, back_one.bgrad)
    if not quick:
        grads = [whole_matrices(group, b.whole) for group, b in ((0, back_zero), (1, back_one))]
        small = small_vector((back_zero.vgrad, back_one.vgrad), tables_grad, back_one.hb_grad[0])
        loss, item_count = lax.psum(back_one.sums[0, 0], (REP, FSDP)), back_one.sums[2, 0]
        return (loss, item_count, *general_tail(grads, weights, moms, errs, facs, small, small_params, small_mom))

    far = swap(back_zero.far, 1)
    left = back_zero.mine + swap(back_zero.other, 1)
    left = sum_chips(left)
    left, *tables_grad = lax.optimization_barrier((left, *tables_grad))
    far, _ = lax.optimization_barrier((far, left))
    received[0] = scatter_chip_sums(far, back_zero.near)
    bit, early = 1, iter((2, 4))
    while bit < reps:
        left = left + swap_rep(left, bit, reps)
        chip = next(early, 6)
        left, received[0][chip] = lax.optimization_barrier((left, received[0][chip]))
        bit *= 2
    left_other = swap(left, 1)
    left, left_other, received[0] = lax.optimization_barrier((left, left_other, received[0]))
    factors = right_factors(me, (left, left_other), back_zero.whole, back_one.whole, tables_grad)
    received[1] = scatter_cores(back_one, received[1])
    mine = sum_replica(factors.mine, factors.other)
    every = sum_replicas(mine, reps)
    updated = apply_update(
        me,
        weights,
        moms,
        turned,
        (mine, swap(mine, 1), every, swap(every, 1)),
        (factors.basis0, factors.basis1),
        (back_zero.own, back_one.own),
        received,
    )
    odd = (me[0] & 1) == 1
    summed = jnp.where(odd, left, left_other)[:, HALF_LEFT - SMALLS :]
    vgrads = []
    for layer in range(LAYERS):
        first, second = summed[:, 512 * layer : 512 * layer + D], summed[:, 512 * layer + D : 512 * (layer + 1)]
        vgrads.append(jnp.concatenate([first, second], axis=0))
    head_bias_grad = summed[:, 1024 : 1024 + 128].reshape(-1)
    loss, item_count = summed[0, 1024 + 128], summed[1, 1024 + 128]
    table_sums = [updated.small[:, WIDE * i : WIDE * (i + 1)] for i in range(2)]
    new_small_mom = MOMENTUM * small_mom + small_vector(vgrads, table_sums, head_bias_grad)
    return (
        loss,
        item_count,
        *[getattr(updated, "new_" + n) for n in NAMES],
        *[getattr(updated, "new_mom_" + n) for n in NAMES],
        *[getattr(updated, "err_" + n) for n in NAMES],
        *[jnp.swapaxes(getattr(updated, "new_fac_" + n), -1, -2) for n in NAMES],
        small_params - SMALL_RATE * new_small_mom,
        new_small_mom,
    )


FULL_ROWS = (9 * CIN, D, D, D, FF, D)


def whole_matrices(group, packed):
    out = {}
    for name, (at, rows, blocks) in pieces_of(SHARDS, group)[0].items():
        cols = [packed[:, at + c * rows : at + (c + 1) * rows, :].reshape(SHARDS * rows, D) for c in range(blocks)]
        out[name] = jnp.concatenate(cols, axis=1)
    return out


def orthonormal(product, gram_mat):
    lower_tri = jnp.linalg.cholesky(gram_mat)
    return jnp.swapaxes(
        jax.scipy.linalg.solve_triangular(lower_tri, jnp.swapaxes(product, 1, 2), lower=True), 1, 2
    )


def general_tail(grads, weights, moms, errs, facs, small, small_params, small_mom):
    layer = [jnp.stack([grads[g][n] for g in range(2)]) for n in MATRIX_NAMES]
    wholes = [grads[0]["conv"][None], *layer, grads[1]["head"][None, :, :CLASSES]]
    lift = lambda xs: [xs[0][None], *xs[1:5], xs[5][None]]
    weights, moms, facs = lift(weights), lift(moms), lift(facs)
    errors = [errs[0], *[e[0] for e in errs[1:5]], errs[5]]
    merged = [
        lax.psum_scatter(g, FSDP, scatter_dimension=1, tiled=True) + e for g, e in zip(wholes, errors)
    ]
    lefts = lax.psum(
        [jnp.einsum("bio,bok->bik", m, f, precision=PRECISE) for m, f in zip(merged, facs)], "rep"
    )
    grams = lax.psum([jnp.einsum("bik,bil->bkl", p, p, precision=PRECISE) for p in lefts], FSDP)
    bases = [orthonormal(p, g) for p, g in zip(lefts, grams)]
    local = [jnp.einsum("bio,bik->bok", m, b, precision=PRECISE) for m, b in zip(merged, bases)]
    mine = lax.psum([*local, small], FSDP)
    every = lax.psum(mine, REP)
    product = lambda b, q: jnp.einsum("bik,bok->bio", b, q, precision=PRECISE)
    new_errs = [m - product(b, q) for m, b, q in zip(merged, bases, mine)]
    new_moms = [MOMENTUM * m + product(b, q) for m, b, q in zip(moms, bases, every)]
    new_weights = [w - LEARN_RATE * m for w, m in zip(weights, new_moms)]
    drop = lambda xs: [xs[0][0], *xs[1:5], xs[5][0]]
    new_small_mom = MOMENTUM * small_mom + every[6]
    return (
        *drop(new_weights),
        *drop(new_moms),
        new_errs[0],
        *[e[None] for e in new_errs[1:5]],
        new_errs[5],
        *drop(every[:6]),
        small_params - SMALL_RATE * new_small_mom,
        new_small_mom,
    )


def solution(mesh):
    rows, mids = P(FSDP, None), P(None, FSDP, None)
    matrices = (rows, mids, mids, mids, mids, rows)
    errors = (
        P(REP, FSDP, None),
        *[P(REP, None, FSDP, None)] * 4,
        P(REP, FSDP, None),
    )
    return jax.shard_map(
        lambda *args: step(mesh, args),
        mesh=mesh,
        in_specs=(
            P((REP, FSDP), None, None, None),
            P((REP, FSDP)),
            P(REP, FSDP),
            P(),
            *matrices,
            *matrices,
            *errors,
            *[P()] * 8,
        ),
        out_specs=(P(), P(), *matrices, *matrices, *errors, *[P()] * 8),
        check_vma=False,
    )
```

```python
import functools
import types

import jax
import jax.numpy as jnp
import numpy as np
from jax import lax
from jax.experimental import pallas as pl
from jax.experimental.pallas import tpu as pltpu
from jax.sharding import PartitionSpec as P

D = 256
HEADS = 8
HEAD = 32
FF = 768
CLASSES = 1000
CPAD = 1024
CIN = 128
GRID = 14
KER = 7
LAYERS = 2
PIX = 196
RB = 169
RANK = 8

EPSILON = 1e-05
MASKED = -1000000000.0
MOMENTUM = 0.9
LEARN_RATE = 16.0
SMALL_RATE = 4.0
PRECISE = lax.Precision.HIGHEST
SCALE = HEAD ** (-0.5)
LOG2E = 1.4426950408889634

COLS = 16
TOK = GRID * COLS
KEYS = 128
HALF = 128
PARTS = 3 * CIN
FSDP, REP = "fsdp", "rep"
F32 = jnp.float32
BF16 = jnp.bfloat16
VMEM_LIMIT = 58 * 1024 * 1024
SMALL_LIMIT = 20 * 1024 * 1024

GROUPS = (
    ((0, 80, 0), (80, 32, 32), (112, 32, 64), (144, 80, 96)),
    ((0, 112, 0), (112, 112, 96)),
)


def row_order(layer):
    if layer % 2 == 0:
        return list(range(GRID))
    return [*range(0, GRID, 2), *range(1, GRID, 2)]


def window_start(cell, dil):
    residue, position = cell % dil, cell // dil
    length = (GRID - residue + dil - 1) // dil
    return min(max(position - KER // 2, 0), length - KER)


def in_window(query, key, dil):
    if query % dil != key % dil:
        return False
    first = window_start(query, dil)
    return first <= key // dil < first + KER


@functools.lru_cache(None)
def static_maps(layer):
    dil = 1 + layer % 2
    order = row_order(layer)
    starts = np.zeros(GRID, np.int64)
    mask = np.zeros((TOK, KEYS), np.float32)
    for q0, nq, k0 in GROUPS[layer % 2]:
        for place in range(q0 // COLS, (q0 + nq) // COLS):
            qy = order[place]
            for j in range(8):
                ky = order[k0 // COLS + j]
                if not in_window(qy, ky, dil):
                    continue
                starts[place] = ky // dil - qy // dil + KER - 1 - j
                for x in range(GRID):
                    for kx in range(GRID):
                        if in_window(x, kx, dil):
                            mask[place * COLS + x, j * COLS + kx] = 1.0
    shifts = np.zeros((COLS, KEYS, KEYS), np.float32)
    for x in range(GRID):
        for kx in range(GRID):
            if in_window(x, kx, dil):
                dx = kx // dil - x // dil + KER - 1
                for j in range(8):
                    shifts[x, j * COLS + dx, j * COLS + kx] = 1.0
    return starts, shifts, mask


def norm_stats(values):
    centred = values - jnp.mean(values, axis=-1, keepdims=True)
    rstd = lax.rsqrt(jnp.mean(centred * centred, axis=-1, keepdims=True) + EPSILON)
    return centred * rstd, rstd


def norm_back(grad, xhat, rstd, gain):
    scaled = grad * gain
    mean_one = jnp.mean(scaled, axis=-1, keepdims=True)
    mean_two = jnp.mean(scaled * xhat, axis=-1, keepdims=True)
    return rstd * (scaled - mean_one - xhat * mean_two)


def col_sum(values):
    return jnp.sum(values, axis=0, keepdims=True)


def dot_nn(a, b, **kw):
    return lax.dot_general(a, b, (((1,), (0,)), ((), ())), preferred_element_type=F32, **kw)


def dot_nt(a, b, **kw):
    return lax.dot_general(a, b, (((1,), (1,)), ((), ())), preferred_element_type=F32, **kw)


def dot_tn(a, b, **kw):
    return lax.dot_general(a, b, (((0,), (0,)), ((), ())), preferred_element_type=F32, **kw)


ERFC_T = 0.44
ERFC_POLY = (
    0.24822096599679971,
    0.24887097779118345,
    0.21731489562842682,
    0.21580753897325447,
    -0.020171305217729862,
    0.2966767736009737,
    -0.2779414931115683,
    0.07122182759012696,
)


def gelu_parts(x):
    bell = jnp.exp2(x * x * (-0.5 * LOG2E))
    t = 1.0 / (1.0 + (ERFC_T * 0.5**0.5) * jnp.abs(x))
    poly = jnp.full_like(t, 0.5 * ERFC_POLY[-1])
    for c in ERFC_POLY[-2::-1]:
        poly = poly * t + 0.5 * c
    tail = poly * t * bell
    cdf = jnp.where(x < 0, tail, 1.0 - tail)
    return x * cdf, cdf + x * bell * (1.0 / (2.0 * np.pi) ** 0.5)


def head_masks():
    lane = lax.broadcasted_iota(jnp.int32, (1, HALF), 1)
    return [jnp.where(lane // HEAD == h, 1.0, 0.0).astype(BF16) for h in range(4)]


def spread_heads(block, masks):
    return jnp.concatenate([block * m for m in masks], axis=0)


def whole(shape):
    return pl.BlockSpec(shape, lambda *_: (0,) * len(shape))


def params(limit=VMEM_LIMIT):
    return pltpu.CompilerParams(dimension_semantics=("arbitrary",), vmem_limit_bytes=limit)


def cost(micros):
    return pl.CostEstimate(flops=int(micros * 1.1e9), bytes_accessed=0, transcendentals=0)


def call(name, kernel, steps, me, ins, outs, scratch, micros, limit=VMEM_LIMIT):
    names = ["me", *[e[0] for e in ins], *[e[0] for e in outs], *[e[0] for e in scratch]]

    def body(*refs):
        kernel(types.SimpleNamespace(**dict(zip(names, refs, strict=True))))

    results = pl.pallas_call(
        body,
        grid_spec=pltpu.PrefetchScalarGridSpec(
            num_scalar_prefetch=1,
            grid=(steps,),
            in_specs=[e[2] or whole(e[1].shape) for e in ins],
            out_specs=[e[3] or whole(e[1]) for e in outs],
            scratch_shapes=[pltpu.VMEM(e[1], e[2]) for e in scratch],
        ),
        out_shape=[jax.ShapeDtypeStruct(e[1], e[2]) for e in outs],
        compiler_params=params(limit),
        cost_estimate=cost(micros),
        name=name,
    )(me, *[e[1] for e in ins])
    return types.SimpleNamespace(**dict(zip([e[0] for e in outs], results, strict=True)))


def patch_kernel(feat_ref, out_ref, wide_ref, patch_ref):
    @pl.when(pl.program_id(0) == 0)
    def _():
        patch_ref[...] = jnp.zeros_like(patch_ref)

    for item in range(feat_ref.shape[0]):
        wide_ref[item, :, 0 : 2 * GRID, :] = feat_ref[item].astype(F32)
        even = wide_ref[item, :, pl.ds(0, GRID, stride=2), :]
        odd = wide_ref[item, :, pl.ds(1, GRID, stride=2), :]
        patch_ref[item, :, 1 : GRID + 1, 0:CIN] = odd
        patch_ref[item, :, 0:GRID, CIN : 2 * CIN] = even
        patch_ref[item, :, 0:GRID, 2 * CIN : 3 * CIN] = odd
        both = patch_ref[item].astype(BF16).reshape(GRID, 2, COLS, PARTS)
        for par in range(2):
            out_ref[item, par] = both[:, par].reshape(TOK, PARTS)


def make_patches(features):
    slots = features.shape[0]
    items = max(n for n in (1, 2, 3, 4) if slots % n == 0)
    return pl.pallas_call(
        patch_kernel,
        grid=(slots // items,),
        in_specs=[pl.BlockSpec((items, 2 * GRID, 2 * GRID, CIN), lambda i: (i, 0, 0, 0))],
        out_specs=pl.BlockSpec((items, 2, TOK, PARTS), lambda i: (i, 0, 0, 0)),
        out_shape=jax.ShapeDtypeStruct((slots, 2, TOK, PARTS), BF16),
        scratch_shapes=[
            pltpu.VMEM((items, 2 * GRID, 32, CIN), F32),
            pltpu.VMEM((items, 2 * GRID, COLS, PARTS), F32),
        ],
        compiler_params=params(),
        cost_estimate=cost(7),
        name="patches",
    )(features)


WIDE = 16 * COLS


def split_three(x):
    high = x.astype(BF16).astype(F32)
    mid = (x - high).astype(BF16).astype(F32)
    return jnp.concatenate([high, mid, x - high - mid], axis=0).astype(BF16)


def exact_dot(dot, x, hot):
    n = x.shape[0]
    out = dot(split_three(x), hot)
    return out[0:n] + out[n : 2 * n] + out[2 * n : 3 * n]


def shift_arrays():
    return np.stack([static_maps(layer)[1] for layer in range(LAYERS)])


def make_bias(me, tables):
    shifts = np.swapaxes(shift_arrays()[:, :GRID], 1, 2).reshape(LAYERS, KEYS, GRID * KEYS)
    shifts = jnp.asarray(shifts, BF16)
    masks = jnp.asarray(np.stack([static_maps(layer)[2] for layer in range(LAYERS)]))

    def kernel(r):
        for layer in range(LAYERS):

            @pl.when(pl.program_id(0) == layer)
            def _():
                for y, start in enumerate(static_maps(layer)[0]):
                    moved = pltpu.roll(r.table[0], int(-COLS * start) % WIDE, 1)
                    r.rows[pl.ds(y, HEADS, stride=GRID), :] = moved[:, :KEYS]

        rows = r.rows[...]
        moved = exact_dot(dot_nn, rows, r.shift[0])
        for x in range(GRID):
            r.flat[pl.ds(x, HEADS * GRID, stride=COLS), :] = moved[:, x * KEYS : (x + 1) * KEYS]
        for x in range(GRID, COLS):
            r.flat[pl.ds(x, HEADS * GRID, stride=COLS), :] = jnp.zeros((HEADS * GRID, KEYS), F32)
        for h in range(HEADS):
            block = r.flat[h * TOK : (h + 1) * TOK, :]
            r.out[0, h] = jnp.where(r.mask[0] > 0.5, block * LOG2E, MASKED)

    return call(
        "bias",
        kernel,
        LAYERS,
        me,
        [
            ("table", tables, pl.BlockSpec((1, HEADS, WIDE), lambda i, *_: (i, 0, 0))),
            ("shift", shifts, pl.BlockSpec((1, KEYS, GRID * KEYS), lambda i, *_: (i, 0, 0))),
            ("mask", masks, pl.BlockSpec((1, TOK, KEYS), lambda i, *_: (i, 0, 0))),
        ],
        [
            (
                "out",
                (LAYERS, HEADS, TOK, KEYS),
                F32,
                pl.BlockSpec((1, HEADS, TOK, KEYS), lambda i, *_: (i, 0, 0, 0)),
            )
        ],
        [("flat", (HEADS * TOK, KEYS), F32), ("rows", (HEADS * GRID, KEYS), F32)],
        5,
    ).out


def table_grads(me, zero, one):
    back = np.swapaxes(shift_arrays()[:, :GRID], -1, -2).reshape(LAYERS, GRID * KEYS, KEYS)
    back = jnp.asarray(back, BF16)

    def kernel(r):
        for layer, grad in enumerate((r.grad0, r.grad1)):
            parts = [grad[pl.ds(x, HEADS * GRID, stride=COLS), :] for x in range(GRID)]
            r.rows[layer] = exact_dot(dot_nn, jnp.concatenate(parts, axis=1), r.back[layer])
        for layer, out in enumerate((r.out0, r.out1)):
            result = None
            for y, start in enumerate(static_maps(layer)[0]):
                part = pad_lanes(r.rows[layer, pl.ds(y, HEADS, stride=GRID), :], WIDE)
                moved = pltpu.roll(part, int(COLS * start) % WIDE, 1)
                result = moved if result is None else result + moved
            out[...] = result

    out = call(
        "tables",
        kernel,
        1,
        me,
        [("grad0", zero, None), ("grad1", one, None), ("back", back, None)],
        [("out0", (HEADS, WIDE), F32, None), ("out1", (HEADS, WIDE), F32, None)],
        [("rows", (LAYERS, HEADS * GRID, KEYS), F32)],
        5,
    )
    return [out.out0, out.out1]


def pieces_of(shards, group):
    narrow, wide = D // shards, FF // shards
    sizes = [("qkv", narrow, 3), ("proj", narrow, 1), ("up", narrow, 3), ("down", wide, 1)]
    if group == 0:
        sizes = [("conv", 9 * CIN // shards, 1)] + sizes
    else:
        sizes = sizes + [("head", narrow, 4)]
    out, at = {}, 0
    for name, rows, blocks in sizes:
        out[name] = (at, rows, blocks)
        at += rows * blocks
    return out, at


SHARDS = 8
COUNT_ROWS = 16
NAMES = ("conv", "qkv", "proj", "up", "down", "head")
WHOLE_NAMES = ("conv", "head")


def pack(parts):
    out = []
    for part in parts:
        if part.shape[1] == CLASSES:
            part = jnp.pad(part, ((0, 0), (0, CPAD - CLASSES)))
        out += [part[:, c : c + D] for c in range(0, part.shape[1], D)]
    return jnp.concatenate(out, axis=0)


def pack_weights(weights, counts):
    def kernel(r):
        for group, packed in ((0, r.packed0), (1, r.packed1)):
            for name, (at, rows, blocks) in pieces_of(SHARDS, group)[0].items():
                ref = getattr(r, name)
                for c in range(blocks):
                    width = min(D, ref.shape[-1] - c * D)
                    cols = slice(c * D, c * D + width)
                    value = ref[:, cols] if name in WHOLE_NAMES else ref[group, :, cols]
                    value = value.astype(BF16)
                    if width < D:
                        value = jnp.concatenate([value, jnp.zeros((rows, D - width), BF16)], axis=1)
                    packed[at + c * rows : at + (c + 1) * rows, :] = value
        end = pieces_of(SHARDS, 0)[1]
        r.packed0[end : end + COUNT_ROWS, :] = jnp.broadcast_to(r.count[...].astype(F32), (COUNT_ROWS, D)).astype(BF16)

    ends = [pieces_of(SHARDS, group)[1] for group in range(2)]
    out = call(
        "pack",
        kernel,
        1,
        jnp.zeros((1,), jnp.int32),
        [*[(n, w, None) for n, w in zip(NAMES, weights)], ("count", counts, None)],
        [("packed0", (ends[0] + COUNT_ROWS, D), BF16, None), ("packed1", (ends[1], D), BF16, None)],
        [],
        2,
    )
    return out.packed0, out.packed1


def unpack_weights(me, sources, targets, group):
    layout, _ = pieces_of(SHARDS, group)
    for ref, low, high, offsets in sources:
        for p, offset in enumerate(offsets):
            owner = me ^ offset
            for name, target in targets.items():
                at, rows, blocks = layout[name]
                if not low <= at < high:
                    continue
                place = pl.ds(pl.multiple_of(owner * rows, 16), rows)
                for c in range(blocks):
                    first = at - low + c * rows
                    target[place, c * D : (c + 1) * D] = ref[p, first : first + rows, :]


def units(layer, items):
    return [(n, n * TOK, group, hf) for n in range(items) for group in GROUPS[layer] for hf in range(2)]


def lanes_of(which, hf):
    return slice(which * D + hf * HALF, which * D + (hf + 1) * HALF)


def scores_of(hf):
    return slice(hf * 4 * KEYS, (hf + 1) * 4 * KEYS)


def attend(layer, items, joined_ref, bias_ref, score_ref, probs_ref, mixed_ref):
    masks = head_masks()
    for item, base, (q0, nq, k0), hf in units(layer, items):
        query = joined_ref[base + q0 : base + q0 + nq, lanes_of(0, hf)]
        keys = spread_heads(joined_ref[base + k0 : base + k0 + KEYS, lanes_of(1, hf)], masks)
        score_ref[item, q0 : q0 + nq, scores_of(hf)] = dot_nt(query, keys)
    for item in range(items):
        for q0, nq, k0 in GROUPS[layer]:
            for head in range(HEADS):
                place = (item, slice(q0, q0 + nq), slice(head * KEYS, (head + 1) * KEYS))
                s = score_ref[place] * (SCALE * LOG2E) + bias_ref[0, head, q0 : q0 + nq, :]
                e = jnp.exp2(s - jnp.max(s, axis=-1, keepdims=True))
                probs_ref[place] = (e * (1.0 / jnp.sum(e, axis=-1, keepdims=True))).astype(BF16)
    for item, base, (q0, nq, k0), hf in units(layer, items):
        values = spread_heads(joined_ref[base + k0 : base + k0 + KEYS, lanes_of(2, hf)], masks)
        mixed = dot_nn(probs_ref[item, q0 : q0 + nq, scores_of(hf)], values)
        mixed_ref[base + q0 : base + q0 + nq, lanes_of(0, hf)] = mixed.astype(BF16)


def layer_forward(layer, hidden, vec_ref, weights, bias_ref, outs, work, items):
    joined_ref, probs_ref, mixed_ref, after_ref, slope_ref, active_ref = outs
    score_ref, pre_ref = work
    vec = lambda i: vec_ref[LAYER_AT[layer] + i : LAYER_AT[layer] + i + 1, :]
    xhat, _ = norm_stats(hidden)
    normed = (xhat * vec(0) + vec(1)).astype(BF16)
    for c in range(3):
        part = dot_nn(normed, weights["qkv"][:, c * D : (c + 1) * D])
        if c != 1:
            part = part + vec(2 if c == 0 else 3)
        joined_ref[:, c * D : (c + 1) * D] = part.astype(BF16)
    attend(layer, items, joined_ref, bias_ref, score_ref, probs_ref, mixed_ref)
    after = hidden + (dot_nn(mixed_ref[...], weights["proj"][...]) + vec(4))
    after_ref[...] = after
    xhat, _ = norm_stats(after)
    normed = (xhat * vec(5) + vec(6)).astype(BF16)
    for c in range(3):
        cols = slice(c * D, (c + 1) * D)
        pre_ref[:, cols] = dot_nn(normed, weights["up"][:, cols])
    for c in range(3):
        cols = slice(c * D, (c + 1) * D)
        active, slope = gelu_parts(pre_ref[:, cols] + vec(8 + c))
        slope_ref[:, cols] = slope.astype(BF16)
        active_ref[:, cols] = active.astype(BF16)
    return after_ref[...] + (dot_nn(active_ref[...], weights["down"][...]) + vec(7))


def conv_taps(patch_ref, item):
    odd = patch_ref[item, 1]
    up = jnp.concatenate([jnp.zeros((COLS, PARTS), BF16), odd[: TOK - COLS]], axis=0)
    return up, patch_ref[item, 0], odd


CACHE = (
    ("joined", 3 * D, BF16),
    ("probs", None, BF16),
    ("mixed", D, BF16),
    ("after", D, F32),
    ("slope", FF, BF16),
    ("active", FF, BF16),
)
MATRICES = (("qkv", (D, FF)), ("proj", (D, D)), ("up", (D, FF)), ("down", (FF, D)))
MATRIX_NAMES = [m[0] for m in MATRICES]


def token_spec(items, width=D):
    return pl.BlockSpec((items * TOK, width), lambda i, *_: (i, 0))


def cache_entries(slots, items):
    out = []
    for name, width, dtype in CACHE:
        if width is None:
            spec = pl.BlockSpec((items, TOK, HEADS * KEYS), lambda i, *_: (i, 0, 0))
            out.append((name, (slots, TOK, HEADS * KEYS), dtype, spec))
        else:
            out.append((name, (slots * TOK, width), dtype, token_spec(items, width)))
    return out


def forward_scratch(items):
    return [("scores", (items, TOK, HEADS * KEYS), F32), ("pre", (items * TOK, FF), F32)]


def caches_of(r):
    return tuple(getattr(r, entry[0]) for entry in CACHE)


def bias_spec(layer):
    return pl.BlockSpec((1, HEADS, TOK, KEYS), lambda i, *_: (layer, 0, 0, 0))


def patch_spec(items):
    return pl.BlockSpec((items, 2, TOK, PARTS), lambda i, *_: (i, 0, 0, 0))


def source_entries(sources):
    return [(f"source{i}", array, None) for i, (array, *_) in enumerate(sources)]


def sources_of(r, sources):
    return [(getattr(r, f"source{i}"), *entry[1:]) for i, entry in enumerate(sources)]


def count_of(sources):
    total = jnp.zeros((1, 1), F32)
    for ref, _, high, offsets in sources:
        if ref.shape[1] > high:
            for p in range(len(offsets)):
                total = total + ref[p, high : high + COUNT_ROWS, :].astype(F32)[0:1, 0:1]
    return total


CONV_AT, LAYER_AT, FINAL_AT, BIAS_AT = 0, (3, 14), 25, 27


def forward_zero(me, patches, sources, vecs, bias, items):
    slots = patches.shape[0]

    def kernel(r):
        names = ["conv_w", *MATRIX_NAMES]
        weights = {n: getattr(r, n) for n in names}

        @pl.when(pl.program_id(0) == 0)
        def _():
            targets = {n.removesuffix("_w"): ref for n, ref in weights.items()}
            unpack_weights(r.me[0], sources_of(r, sources), targets, 0)
            r.count[...] = jnp.broadcast_to(count_of(sources_of(r, sources)), r.count.shape)

        for item in range(items):
            taps = conv_taps(r.patch, item)
            total = None
            for a in range(3):
                part = dot_nn(taps[a], r.conv_w[a * PARTS : (a + 1) * PARTS, :])
                total = part if total is None else total + part
            r.conv[item * TOK : (item + 1) * TOK, :] = total + r.vecs[CONV_AT : CONV_AT + 1, :]
        xhat, _ = norm_stats(r.conv[...])
        hidden = xhat * r.vecs[CONV_AT + 1 : CONV_AT + 2, :] + r.vecs[CONV_AT + 2 : CONV_AT + 3, :]
        hidden = layer_forward(0, hidden, r.vecs, weights, r.bias, caches_of(r), (r.scores, r.pre), items)
        for item in range(items):
            for place, row in enumerate(row_order(1)):
                r.hidden[item * TOK + place * COLS : item * TOK + (place + 1) * COLS, :] = hidden[
                    item * TOK + row * COLS : item * TOK + (row + 1) * COLS
                ]

    return call(
        "fwd0",
        kernel,
        slots // items,
        me,
        [
            ("patch", patches, patch_spec(items)),
            *source_entries(sources),
            ("vecs", vecs, None),
            ("bias", bias, bias_spec(0)),
        ],
        [
            ("hidden", (slots * TOK, D), F32, token_spec(items)),
            ("conv", (slots * TOK, D), F32, token_spec(items)),
            *cache_entries(slots, items),
            *[(n, shape, BF16, None) for n, shape in MATRICES],
            ("count", (8, 128), F32, None),
        ],
        [("conv_w", (9 * CIN, D), BF16), *forward_scratch(items)],
        30,
    )


def real_cells():
    place = lax.broadcasted_iota(jnp.int32, (TOK, 1), 0)
    return jnp.where(place % COLS < GRID, 1.0, 0.0)


def classify(r, slots, counts):
    rows = r.pooled.shape[0]
    place = lax.broadcasted_iota(jnp.int32, (rows, 1), 0)
    label = jnp.full((rows, 1), -1, jnp.int32)
    for i in range(slots):
        label = jnp.where(place == i, r.me[2 + i], label)
    live = jnp.where(place < r.me[1], 1.0, 0.0)
    count = sum([getattr(r, f"count{i}")[0:1, 0:1] for i in range(counts)])
    pooled = r.pooled[...].astype(BF16)
    head_bias = jnp.concatenate([r.vecs[BIAS_AT + c : BIAS_AT + c + 1, :] for c in range(CPAD // D)], axis=1)
    logits = dot_nn(pooled, r.head[...]) + head_bias
    peak = jnp.max(logits, axis=-1, keepdims=True)
    log_total = peak + jnp.log(jnp.sum(jnp.exp(logits - peak), axis=-1, keepdims=True))
    lane = lax.broadcasted_iota(jnp.int32, logits.shape, 1)
    onehot = jnp.where(label == lane, 1.0, 0.0)
    picked = jnp.sum(onehot * logits, axis=-1, keepdims=True)
    loss = col_sum(live * (log_total - picked))
    row = lax.broadcasted_iota(jnp.int32, (8, 128), 0)
    r.sums[...] = jnp.where(row == 0, loss, jnp.where(row == 1, col_sum(live), count))
    d_logits = (jnp.exp(logits - log_total) - onehot) * ((1.0 / count) * live)
    d_logits = jnp.where(lane < CLASSES, d_logits, 0.0).astype(BF16)
    r.head_grad[...] = dot_tn(pooled, d_logits)
    r.hb_grad[...] = col_sum(d_logits.astype(F32))
    r.d_pooled[...] = dot_nt(d_logits, r.head[...]) * (1.0 / PIX)


def forward_one(me, hidden, sources, vecs, bias, items):
    slots = hidden.shape[0] // TOK
    rows = -(-slots // 16) * 16

    def kernel(r):
        weights = {n: getattr(r, n) for n in MATRIX_NAMES}
        step = pl.program_id(0)

        @pl.when(step == 0)
        def _():
            unpack_weights(r.me[0], sources_of(r, sources), weights | dict(head=r.head), 1)
            r.pooled[...] = jnp.zeros_like(r.pooled)

        out = layer_forward(1, r.hidden[...], r.vecs, weights, r.bias, caches_of(r), (r.scores, r.pre), items)
        r.out[...] = out
        xhat, _ = norm_stats(out)
        normed = xhat * r.vecs[FINAL_AT : FINAL_AT + 1, :] + r.vecs[FINAL_AT + 1 : FINAL_AT + 2, :]
        real = real_cells()
        for item in range(items):
            mean = col_sum(normed[item * TOK : (item + 1) * TOK] * real) * (1.0 / PIX)
            r.pooled[pl.ds(step * items + item, 1), :] = mean

    return call(
        "fwd1",
        kernel,
        slots // items,
        me,
        [
            ("hidden", hidden, token_spec(items)),
            *source_entries(sources),
            ("vecs", vecs, None),
            ("bias", bias, bias_spec(1)),
        ],
        [
            ("out", (slots * TOK, D), F32, token_spec(items)),
            *cache_entries(slots, items),
            *[(n, shape, BF16, None) for n, shape in MATRICES],
            ("head", (D, CPAD), BF16, None),
            ("pooled", (rows, D), F32, None),
        ],
        forward_scratch(items),
        28,
    )


def attend_back(layer, items, joined_ref, probs_ref, dmix_ref, djoin_ref, dkv_ref, dprob_ref, dscore_ref, bgrad_ref):
    masks = head_masks()
    for item, base, (q0, nq, k0), hf in units(layer, items):
        values = spread_heads(joined_ref[base + k0 : base + k0 + KEYS, lanes_of(2, hf)], masks)
        d_mix = dmix_ref[base + q0 : base + q0 + nq, lanes_of(0, hf)]
        dprob_ref[item, q0 : q0 + nq, scores_of(hf)] = dot_nt(d_mix, values)
    for q0, nq, k0 in GROUPS[layer]:
        for head in range(HEADS):
            total = None
            for item in range(items):
                place = (item, slice(q0, q0 + nq), slice(head * KEYS, (head + 1) * KEYS))
                p, dp = probs_ref[place].astype(F32), dprob_ref[place]
                ds = (p * (dp - jnp.sum(dp * p, axis=-1, keepdims=True))).astype(BF16)
                dscore_ref[place] = ds
                ds = ds.astype(F32)
                total = ds if total is None else total + ds
            bgrad_ref[head * TOK + q0 : head * TOK + q0 + nq, :] += total
    for item, base, (q0, nq, k0), hf in units(layer, items):
        keys = spread_heads(joined_ref[base + k0 : base + k0 + KEYS, lanes_of(1, hf)], masks)
        d_query = dot_nn(dscore_ref[item, q0 : q0 + nq, scores_of(hf)], keys) * SCALE
        djoin_ref[base + q0 : base + q0 + nq, lanes_of(0, hf)] = d_query.astype(BF16)
    dkv_ref[...] = jnp.zeros_like(dkv_ref)
    for item, base, (q0, nq, k0), hf in units(layer, items):
        qrows, krows = slice(base + q0, base + q0 + nq), slice(base + k0, base + k0 + KEYS)
        heads = [slice(h * KEYS, (h + 1) * KEYS) for h in range(hf * 4, hf * 4 + 4)]
        for which, left, right in ((0, joined_ref, dscore_ref), (1, dmix_ref, probs_ref)):
            turned = jnp.transpose(left[qrows, lanes_of(0, hf)])
            parts = []
            for h in range(4):
                parts.append(dot_nn(turned[h * HEAD : (h + 1) * HEAD], right[item, q0 : q0 + nq, heads[h]]))
            dkv_ref[krows, lanes_of(which, hf)] += jnp.transpose(jnp.concatenate(parts, axis=0))
    djoin_ref[:, D : 2 * D] = (dkv_ref[:, 0:D] * SCALE).astype(BF16)
    djoin_ref[:, 2 * D : 3 * D] = dkv_ref[:, D : 2 * D].astype(BF16)


def layer_backward(layer, d_out, hidden, vec_ref, weights, caches, work, grads, vgrad_ref, bgrad_ref, items):
    joined_ref, probs_ref, mixed_ref, after_ref, slope_ref, active_ref = caches
    dpre_ref, *work = work
    dmix_ref, djoin_ref = work[:2]
    vec = lambda i: vec_ref[LAYER_AT[layer] + i : LAYER_AT[layer] + i + 1, :]

    def add(row, value):
        vgrad_ref[row : row + 1, :] += value

    d_branch = d_out.astype(BF16)
    add(7, col_sum(d_branch.astype(F32)))
    for c in range(3):
        cols = slice(c * D, (c + 1) * D)
        dpre_ref[:, cols] = dot_nt(d_branch, weights["down"][cols, :])
    grads["down"][...] += dot_tn(d_branch, active_ref[...])
    for c in range(3):
        cols = slice(c * D, (c + 1) * D)
        d_pre = (dpre_ref[:, cols] * slope_ref[:, cols].astype(F32)).astype(BF16)
        djoin_ref[:, cols] = d_pre
        add(8 + c, col_sum(d_pre.astype(F32)))
    xhat, rstd = norm_stats(after_ref[...])
    normed = (xhat * vec(5) + vec(6)).astype(BF16)
    grads["up"][...] += dot_tn(normed, djoin_ref[...])
    d_normed = dot_nt(djoin_ref[...], weights["up"][...])
    add(5, col_sum(d_normed * xhat))
    add(6, col_sum(d_normed))
    d_after = d_out + norm_back(d_normed, xhat, rstd, vec(5))
    d_proj = d_after.astype(BF16)
    add(4, col_sum(d_proj.astype(F32)))
    grads["proj"][...] += dot_tn(mixed_ref[...], d_proj)
    dmix_ref[...] = dot_nt(d_proj, weights["proj"][...]).astype(BF16)
    attend_back(layer, items, joined_ref, probs_ref, *work, bgrad_ref)
    add(2, col_sum(djoin_ref[:, 0:D].astype(F32)))
    add(3, col_sum(djoin_ref[:, 2 * D : 3 * D].astype(F32)))
    xhat, rstd = norm_stats(hidden)
    normed = (xhat * vec(0) + vec(1)).astype(BF16)
    grads["qkv"][...] += dot_tn(normed, djoin_ref[...])
    d_normed = dot_nt(djoin_ref[...], weights["qkv"][...])
    add(0, col_sum(d_normed * xhat))
    add(1, col_sum(d_normed))
    return d_after + norm_back(d_normed, xhat, rstd, vec(0))


def split_two(x):
    high = x.astype(BF16)
    return high, (x - high.astype(F32)).astype(BF16)


def wide_dot(dot, rows, matrix):
    stacked = split_three(rows)
    high, low = split_two(matrix)
    out = dot(stacked, high) + dot(stacked, low)
    return out[0:RANK] + out[RANK : 2 * RANK] + out[2 * RANK : 3 * RANK]


def block_of(whole_ref, entry, c):
    at, rows, _ = entry
    return jnp.concatenate(
        [whole_ref[s, at + c * rows : at + (c + 1) * rows, :] for s in range(SHARDS)], axis=0
    )


def factor_of(r, group, name):
    ref = getattr(r, "fac_" + name)
    return ref[...] if name in WHOLE_NAMES else ref[group]


def finish_grads(r, group, grads):
    layout, _ = pieces_of(SHARDS, group)
    me = r.me[0]
    for name, (at, rows, blocks) in layout.items():
        matrix = grads[name]
        if name in ("down", "conv"):
            matrix = jnp.transpose(matrix[...])
        for s in range(SHARDS):
            for c in range(blocks):
                piece = matrix[s * rows : (s + 1) * rows, c * D : (c + 1) * D]
                r.sums_of[s, at + c * rows : at + (c + 1) * rows, :] = piece
    for name, (at, rows, blocks) in layout.items():
        err = getattr(r, "err_" + name)
        for c in range(blocks):
            width = min(D, err.shape[-1] - c * D)
            cols = slice(c * D, c * D + width)
            value = err[0, :, cols] if name in WHOLE_NAMES else err[0, group, :, cols]
            place = slice(at + c * rows, at + (c + 1) * rows)
            r.sums_of[me, place, 0:width] += value
    r.own[...] = r.sums_of[me]
    r.whole[...] = r.sums_of[...].astype(r.whole.dtype)
    if group == 0:
        for i, chip in enumerate((0, 2, 4, 6)):
            r.far[i] = r.sums_of[me ^ chip ^ 1].astype(BF16)
            if chip:
                r.near[i - 1] = r.sums_of[me ^ chip].astype(BF16)
    else:
        r.sent1[...] = r.sums_of[me ^ 1].astype(BF16)
        for chip in (2, 4, 6):
            for core in range(2):
                getattr(r, f"sent{chip}")[core] = r.sums_of[me ^ chip ^ core].astype(BF16)
    at_lane, lefts = 0, []
    for name, entry in layout.items():
        total = None
        for c in range(entry[2]):
            fac = factor_of(r, group, name)
            width = min(D, fac.shape[-1] - c * D)
            block = block_of(r.sums_of, entry, c)
            part = wide_dot(dot_nt, fac[:, c * D : c * D + width], block[:, :width])
            total = part if total is None else total + part
        lefts.append(total)
    return jnp.concatenate(lefts, axis=1)


def left_lanes(group):
    return sum(rows * SHARDS for _, rows, _ in pieces_of(SHARDS, group)[0].values())


def right_lanes(group):
    return sum(blocks * D for _, _, blocks in pieces_of(SHARDS, group)[0].values())


SMALLS = 2 * 512 + 128 + 128
HALF_LEFT = (left_lanes(0) + left_lanes(1) + SMALLS) // 2
HALF_RIGHT = (right_lanes(0) + right_lanes(1) + 2 * WIDE) // 2


def pad_lanes(x, lanes):
    return jnp.concatenate([x, jnp.zeros((x.shape[0], lanes - x.shape[1]), x.dtype)], axis=1)


def put_halves(r, whole):
    n = whole.shape[1] // 2
    first, second = whole[:, :n], whole[:, n:]
    odd = (r.me[0] & 1) == 1
    r.mine[...] = jnp.where(odd, second, first)
    r.other[...] = jnp.where(odd, first, second)


def get_halves(r, mine, other):
    odd = (r.me[0] & 1) == 1
    mine, other = mine[...], other[...]
    return jnp.concatenate([jnp.where(odd, other, mine), jnp.where(odd, mine, other)], axis=1)


def backward_outs(group, dtype):
    rows = pieces_of(SHARDS, group)[1]
    return [
        ("vgrad", (16, D), F32, None),
        ("bgrad", (HEADS * TOK, KEYS), F32, None),
        ("whole", (SHARDS, rows, D), dtype, None),
        ("own", (rows, D), F32, None),
    ]


def factor_inputs(group, errs, facs):
    out = []
    for name, err, fac in zip(NAMES, errs, facs):
        if name in pieces_of(SHARDS, group)[0]:
            out += [("err_" + name, err, None), ("fac_" + name, fac, None)]
    return out


def backward_scratch(items, group):
    return [
        ("sums_of", (SHARDS, pieces_of(SHARDS, group)[1], D), F32),
        ("d_pre", (items * TOK, FF), F32),
        ("d_mixed", (items * TOK, D), BF16),
        ("d_joined", (items * TOK, 3 * D), BF16),
        ("d_keys", (items * TOK, 2 * D), F32),
        ("d_probs", (items, TOK, HEADS * KEYS), F32),
        ("d_scores", (items, TOK, HEADS * KEYS), BF16),
        ("g_qkv", (D, FF), F32),
        ("g_proj", (D, D), F32),
        ("g_up", (D, FF), F32),
        ("g_down", (D, FF), F32),
    ]


def start_backward(r, grads):
    r.vgrad[...] = jnp.zeros_like(r.vgrad)
    r.bgrad[...] = jnp.zeros_like(r.bgrad)
    for ref in grads.values():
        ref[...] = jnp.zeros_like(ref)


def cache_inputs(caches, slots, items):
    return [(e[0], getattr(caches, e[0]), e[3]) for e in cache_entries(slots, items)]


def matrix_inputs(caches):
    return [(n, getattr(caches, n), None) for n in MATRIX_NAMES]


def backward_one(me, hidden, forward, vecs, count, errs, facs, items, dtype):
    slots = hidden.shape[0] // TOK

    def kernel(r):
        weights = {n: getattr(r, n) for n in MATRIX_NAMES}
        grads = {n: getattr(r, "g_" + n) for n in MATRIX_NAMES}
        step = pl.program_id(0)

        @pl.when(step == 0)
        def _():
            start_backward(r, grads)
            classify(r, slots, len(count))

        real = real_cells()
        d_final = jnp.concatenate(
            [real * r.d_pooled[pl.ds(step * items + item, 1), :] for item in range(items)], axis=0
        )
        xhat, rstd = norm_stats(r.out[...])
        r.vgrad[11:12, :] += col_sum(d_final * xhat)
        r.vgrad[12:13, :] += col_sum(d_final)
        d_out = norm_back(d_final, xhat, rstd, r.vecs[FINAL_AT : FINAL_AT + 1, :])
        work = (r.d_pre, r.d_mixed, r.d_joined, r.d_keys, r.d_probs, r.d_scores)
        r.d_hidden[...] = layer_backward(
            1, d_out, r.hidden[...], r.vecs, weights, caches_of(r), work, grads, r.vgrad, r.bgrad, items
        )

        @pl.when(step == pl.num_programs(0) - 1)
        def _():
            r.left[...] = finish_grads(r, 1, grads | dict(head=r.head_grad))

    return call(
        "back1",
        kernel,
        slots // items,
        me,
        [
            ("out", forward.out, token_spec(items)),
            ("pooled", forward.pooled, None),
            *[(f"count{i}", c, None) for i, c in enumerate(count)],
            ("hidden", hidden, token_spec(items)),
            *matrix_inputs(forward),
            ("head", forward.head, None),
            ("vecs", vecs, None),
            *cache_inputs(forward, slots, items),
            *factor_inputs(1, errs, facs),
        ],
        [
            ("d_hidden", hidden.shape, F32, token_spec(items)),
            *backward_outs(1, dtype),
            ("left", (RANK, left_lanes(1)), F32, None),
            ("sums", (8, 128), F32, None),
            ("hb_grad", (1, CPAD), F32, None),
            *[(f"sent{chip}", (2, pieces_of(SHARDS, 1)[1], D), BF16, None) for chip in (2, 4, 6)],
            ("sent1", (pieces_of(SHARDS, 1)[1], D), BF16, None),
        ],
        [*backward_scratch(items, 1), ("head_grad", (D, CPAD), F32), ("d_pooled", forward.pooled.shape, F32)],
        46,
    )


def backward_zero(me, back_one, forward, patches, vecs, errs, facs, items, dtype):
    slots = patches.shape[0]

    def kernel(r):
        weights = {n: getattr(r, n) for n in MATRIX_NAMES}
        grads = {n: getattr(r, "g_" + n) for n in [*MATRIX_NAMES, "conv"]}
        step = pl.program_id(0)

        @pl.when(step == 0)
        def _():
            start_backward(r, grads)

        order = row_order(1)
        rows = []
        for item in range(items):
            for row in range(GRID):
                first = item * TOK + order.index(row) * COLS
                rows.append(r.d_hidden[first : first + COLS, :])
        d_out = jnp.concatenate(rows, axis=0)
        conv_hat, conv_rstd = norm_stats(r.conv[...])
        gain = r.vecs[CONV_AT + 1 : CONV_AT + 2, :]
        hidden = conv_hat * gain + r.vecs[CONV_AT + 2 : CONV_AT + 3, :]
        work = (r.d_pre, r.d_mixed, r.d_joined, r.d_keys, r.d_probs, r.d_scores)
        d_conv = layer_backward(
            0, d_out, hidden, r.vecs, weights, caches_of(r), work, grads, r.vgrad, r.bgrad, items
        )
        r.vgrad[12:13, :] += col_sum(d_conv * conv_hat)
        r.vgrad[13:14, :] += col_sum(d_conv)
        d_conv = norm_back(d_conv, conv_hat, conv_rstd, gain).astype(BF16)
        r.vgrad[11:12, :] += col_sum(d_conv.astype(F32))
        for item in range(items):
            taps = conv_taps(r.patch, item)
            part = jnp.transpose(d_conv[item * TOK : (item + 1) * TOK])
            for a in range(3):
                grads["conv"][:, a * PARTS : (a + 1) * PARTS] += dot_nn(part, taps[a])

        @pl.when(step == pl.num_programs(0) - 1)
        def _():
            parts = [finish_grads(r, 0, grads), r.left_one[...]]
            for ref in (r.vgrad, r.vgrad_one):
                parts += [ref[0:8, :], ref[8:16, :]]
            put_halves(r, jnp.concatenate([*parts, r.head_bias[...], r.sums[...]], axis=1))

    return call(
        "back0",
        kernel,
        slots // items,
        me,
        [
            ("d_hidden", back_one.d_hidden, token_spec(items)),
            ("conv", forward.conv, token_spec(items)),
            ("patch", patches, patch_spec(items)),
            *matrix_inputs(forward),
            ("vecs", vecs, None),
            *cache_inputs(forward, slots, items),
            ("left_one", back_one.left, None),
            ("vgrad_one", back_one.vgrad, None),
            ("head_bias", back_one.hb_grad.reshape(8, 128), None),
            ("sums", back_one.sums, None),
            *factor_inputs(0, errs, facs),
        ],
        [
            *backward_outs(0, dtype),
            ("far", (4, pieces_of(SHARDS, 0)[1], D), BF16, None),
            ("near", (3, pieces_of(SHARDS, 0)[1], D), BF16, None),
            ("mine", (RANK, HALF_LEFT), F32, None),
            ("other", (RANK, HALF_LEFT), F32, None),
        ],
        [*backward_scratch(items, 0), ("g_conv", (D, 9 * CIN), F32)],
        63,
    )


def inverse_cholesky(gram):
    row = lax.broadcasted_iota(jnp.int32, (1, RANK, 2 * RANK), 1)
    lane = lax.broadcasted_iota(jnp.int32, (1, RANK, 2 * RANK), 2)
    eye = jnp.broadcast_to(jnp.where(lane == row + RANK, 1.0, 0.0), (gram.shape[0], RANK, 2 * RANK))
    work = jnp.concatenate([gram, jnp.zeros_like(gram)], axis=2) + eye
    for k in range(RANK):
        scale = 1.0 / jnp.sqrt(work[:, k : k + 1, k : k + 1])
        pivot = work[:, k : k + 1, :] * scale
        column = work[:, :, k : k + 1] * scale
        work = jnp.where(row > k, work - column * pivot, jnp.where(row == k, pivot, work))
    return work[:, :, RANK : 2 * RANK]


def basis_lanes(group):
    return sum(rows for _, rows, _ in pieces_of(SHARDS, group)[0].values())


def right_factors(me, left, whole_zero, whole_one, tables):
    def kernel(r):
        groups = (r.whole0, r.whole1)
        left = get_halves(r, r.left_mine, r.left_other)
        entries, at = [], 0
        for group in range(2):
            for entry in pieces_of(SHARDS, group)[0].values():
                entries.append((group, entry, left[:, at : at + entry[1] * SHARDS]))
                at += entry[1] * SHARDS
        grams = jnp.stack([dot_nt(x, x, precision=PRECISE) for _, _, x in entries])
        inverses = inverse_cholesky(grams)
        rows_of = [[], []]
        parts = []
        for i, (group, entry, x) in enumerate(entries):
            basis = dot_nn(inverses[i], x, precision=PRECISE)
            rows_of[group].append((basis, entry[1]))
            for c in range(entry[2]):
                parts.append(exact_dot(dot_nn, basis, block_of(groups[group], entry, c)))
        for group, out in ((0, r.basis0), (1, r.basis1)):
            for s in range(SHARDS):
                at = 0
                for basis, rows in rows_of[group]:
                    out[s, :, at : at + rows] = basis[:, s * rows : (s + 1) * rows]
                    at += rows
        put_halves(r, jnp.concatenate([*parts, r.table0[...], r.table1[...]], axis=1))

    return call(
        "right",
        kernel,
        1,
        me,
        [
            ("left_mine", left[0], None),
            ("left_other", left[1], None),
            ("whole0", whole_zero, None),
            ("whole1", whole_one, None),
            ("table0", tables[0], None),
            ("table1", tables[1], None),
        ],
        [
            ("mine", (RANK, HALF_RIGHT), F32, None),
            ("other", (RANK, HALF_RIGHT), F32, None),
            ("basis0", (SHARDS, RANK, basis_lanes(0)), F32, None),
            ("basis1", (SHARDS, RANK, basis_lanes(1)), F32, None),
        ],
        [],
        6,
        SMALL_LIMIT,
    )


def six_products(x, other):
    high = x.astype(BF16).astype(F32)
    mid = (x - high).astype(BF16).astype(F32)
    low = x - high - mid
    terms = [high, mid, high, mid, low, high] if other else [high, high, mid, mid, high, low]
    return jnp.concatenate(terms, axis=0).astype(BF16)


def apply_update(me, weights, moms, facs, right, factors, own, received):
    def kernel(r):
        right_mine = get_halves(r, r.rep_mine, r.rep_other)
        right_all = get_halves(r, r.all_mine, r.all_other)
        at_col = 0
        for group in range(2):
            total = getattr(r, f"own{group}")[...] + getattr(r, f"sib{group}")[0].astype(F32)
            for chip in (2, 4, 6):
                total = total + getattr(r, f"got{group}_{chip}")[0].astype(F32)
            basis = getattr(r, f"basis{group}")
            at_row = 0
            for name, (at, rows, blocks) in pieces_of(SHARDS, group)[0].items():
                left = six_products(basis[0, :, at_row : at_row + rows], False)
                at_row += rows
                single = name in WHOLE_NAMES
                for c in range(blocks):
                    width = min(D, (CLASSES if name == "head" else blocks * D) - c * D)
                    cols = slice(c * D, c * D + width)
                    place = (slice(None), cols) if single else (group, slice(None), cols)
                    err_place = (0, slice(None), cols) if single else (0, group, slice(None), cols)
                    right = slice(at_col, at_col + D)
                    at_col += D
                    getattr(r, "new_fac_" + name)[place] = right_all[:, right][:, :width]
                    mine = dot_tn(left, six_products(right_mine[:, right], True))
                    every = dot_tn(left, six_products(right_all[:, right], True))
                    merged = total[at + c * rows : at + (c + 1) * rows]
                    getattr(r, "err_" + name)[err_place] = (merged - mine)[:, :width]
                    mom = MOMENTUM * getattr(r, "mom_" + name)[place] + every[:, :width]
                    getattr(r, "new_mom_" + name)[place] = mom
                    getattr(r, "new_" + name)[place] = getattr(r, "w_" + name)[place] - LEARN_RATE * mom
        r.small[...] = right_all[:, at_col:]

    first = lambda x: pl.BlockSpec((1,) + x.shape[1:], lambda *_: (0, 0, 0))
    mine_spec = lambda x: pl.BlockSpec((1,) + x.shape[1:], lambda i, m: (m[0], 0, 0))
    small = 2 * HALF_RIGHT - right_lanes(0) - right_lanes(1)
    return call(
        "update",
        kernel,
        1,
        me,
        [
            *[("w_" + n, w, None) for n, w in zip(NAMES, weights)],
            *[("mom_" + n, m, None) for n, m in zip(NAMES, moms)],
            *zip(("rep_mine", "rep_other", "all_mine", "all_other"), right, [None] * 4),
            ("basis0", factors[0], mine_spec(factors[0])),
            ("basis1", factors[1], mine_spec(factors[1])),
            ("own0", own[0], None),
            ("own1", own[1], None),
            *[(f"got{g}_{c}", received[g][c], first(received[g][c])) for g in range(2) for c in (2, 4, 6)],
            *[(f"sib{g}", received[g][1], first(received[g][1])) for g in range(2)],
        ],
        [
            *[("new_" + n, w.shape, F32, None) for n, w in zip(NAMES, weights)],
            *[("new_mom_" + n, w.shape, F32, None) for n, w in zip(NAMES, weights)],
            *[("err_" + n, (1,) + w.shape, F32, None) for n, w in zip(NAMES, weights)],
            *[("new_fac_" + n, f.shape, F32, None) for n, f in zip(NAMES, facs)],
            ("small", (RANK, small), F32, None),
        ],
        [],
        5,
    )


def swap(x, offset):
    return lax.ppermute(x, FSDP, [(i, i ^ offset) for i in range(SHARDS)])


def swap_rep(x, offset, reps):
    return lax.ppermute(x, REP, [(i, i ^ offset) for i in range(reps)])


def gather_chips(packed):
    return [packed, *[swap(packed, chip) for chip in (2, 4, 6)]]


def with_sibling(near, end):
    near = jnp.stack(near)
    return [(near, 0, end, (0, 2, 4, 6)), (swap(near, 1), 0, end, (1, 3, 5, 7))]


def gather_pair(packed):
    return jnp.stack([packed, swap(packed, 1)])


def spread_pair(pair, end):
    out = [(pair, 0, end, (0, 1))]
    return out + [(swap(pair, chip), 0, end, (chip, chip ^ 1)) for chip in (2, 4, 6)]


def sum_chips(x):
    return (x + swap(x, 2)) + (swap(x, 4) + swap(x, 6))


def sum_replica(mine, other):
    return sum_chips(mine + swap(other, 1))


def sum_replicas(x, reps):
    bit = 1
    while bit < reps:
        x = x + swap_rep(x, bit, reps)
        bit *= 2
    return x


def scatter_chips(back):
    return {chip: swap(getattr(back, f"sent{chip}"), chip) for chip in (2, 4, 6)}


def scatter_cores(back, received):
    total = back.sent1.astype(F32)
    for chip in (2, 4, 6):
        total = total + received[chip][1].astype(F32)
    return received | {1: swap(total.astype(BF16), 1)[None]}


def scatter_chip_sums(got, near):
    received = {1: got}
    for i, chip in enumerate((2, 4, 6)):
        total = near[i].astype(F32) + got[i + 1].astype(F32)
        received[chip] = swap(total.astype(BF16)[None], chip)
    return received


def table_at(layer):
    return 3 * D + layer * (11 * D + HEADS * RB)


def small_blocks(small):
    parts, tables = [small[: 3 * D]], []
    for layer in range(LAYERS):
        at = table_at(layer)
        parts.append(small[at : at + 11 * D])
        tables.append(small[at + 11 * D : at + 11 * D + HEADS * RB])
    parts += [small[table_at(LAYERS) :], jnp.full((CPAD - CLASSES,), -1e30, F32)]
    vecs = jnp.concatenate(parts)
    tables = jnp.stack(tables).reshape(LAYERS, HEADS, 2 * KER - 1, 2 * KER - 1)
    tables = jnp.pad(tables, ((0, 0), (0, 0), (0, 3), (0, 3))).reshape(LAYERS, HEADS, WIDE)
    return vecs.reshape(-1, D), tables


def small_vector(vgrads, tables, head_bias):
    parts = [vgrads[0][11:14].reshape(-1)]
    for layer in range(LAYERS):
        table = tables[layer].reshape(HEADS, 16, 16)[:, : 2 * KER - 1, : 2 * KER - 1]
        parts += [vgrads[layer][:11].reshape(-1), table.reshape(-1)]
    return jnp.concatenate([*parts, vgrads[1][11:13].reshape(-1), head_bias[:CLASSES]])


def group_parts(group, conv, qkv, proj, up, down, head):
    layer = [m[group] for m in (qkv, proj, up, down)]
    return [conv] + layer if group == 0 else layer + [head]


def step(mesh, args):
    (
        features, labels, counts, tables, *rest
    ) = args
    weights, moms, errs, facs = rest[0:6], rest[6:12], rest[12:18], rest[18:24]
    small_params, small_mom = rest[24:]
    reps = mesh.shape[REP]
    quick = mesh.shape[FSDP] == SHARDS and reps & (reps - 1) == 0
    slots = features.shape[0]
    ahead = max(n for n in (1, 2, 3, 4) if slots % n == 0)
    items = max(n for n in (1, 2, 3) if slots % n == 0)

    if quick:
        ends = [pieces_of(SHARDS, group)[1] for group in range(2)]
        packed, second = pack_weights(weights, counts)
        near = gather_chips(packed)
        near[0], second, features, labels, counts, small_params = lax.optimization_barrier(
            (packed, second, features, labels, counts, small_params)
        )
        me = lax.axis_index(FSDP).astype(jnp.int32)[None]
        me = jnp.concatenate([me, counts[0], labels])
        vecs, bias_tables = small_blocks(small_params)
        patches = make_patches(features)
        bias = make_bias(me, bias_tables)
        pair, patches, bias, vecs, *near = lax.optimization_barrier((gather_pair(second), patches, bias, vecs, *near))
        sources0 = with_sibling(near, ends[0])
        sources1 = spread_pair(pair, ends[1])
    else:
        me = jnp.concatenate([jnp.zeros((1,), jnp.int32), counts[0], labels])
        sides = [lax.all_gather(w.astype(BF16), FSDP, axis=w.ndim - 2, tiled=True) for w in weights]
        sources = []
        for group in range(2):
            parts = group_parts(group, *sides)
            shards = [pack([p.reshape(SHARDS, -1, p.shape[1])[s] for p in parts]) for s in range(SHARDS)]
            sources.append([(jnp.stack(shards), 0, shards[0].shape[0], tuple(range(SHARDS)))])
        sources0, sources1 = sources

    if not quick:
        vecs, bias_tables = small_blocks(small_params)
        bias = make_bias(me, bias_tables)
        patches = make_patches(features)
    zero = forward_zero(me, patches, sources0, vecs, bias, ahead)
    one = forward_one(me, zero.hidden, sources1, vecs, bias, ahead)
    if quick:
        count = [zero.count, *[swap_rep(zero.count, offset, reps) for offset in range(1, reps)]]
        count, *held = lax.optimization_barrier((count, *vars(one).values()))
        one = types.SimpleNamespace(**dict(zip(vars(one), held)))
    else:
        count = [jnp.broadcast_to(lax.psum(counts.astype(F32), (REP, FSDP)), (8, 128))]
    turned = [jnp.swapaxes(f, -1, -2) for f in facs]
    sum_type = BF16 if quick else F32
    own_errs = errs
    if not quick:
        own_errs = [jnp.zeros((1,) + (w.shape[:-2] + (full // SHARDS, w.shape[-1])), F32) for w, full in zip(weights, FULL_ROWS)]
    back_one = backward_one(me, zero.hidden, one, vecs, count, own_errs, turned, items, sum_type)
    if quick:
        received = [None, scatter_chips(back_one)]
    back_zero = backward_zero(me, back_one, zero, patches, vecs, own_errs, turned, items, sum_type)
    if quick:
        received[1], *held = lax.optimization_barrier((received[1], *vars(back_zero).values()))
        back_zero = types.SimpleNamespace(**dict(zip(vars(back_zero), held)))
    tables_grad = table_grads(me, back_zero.bgrad, back_one.bgrad)
    if not quick:
        grads = [whole_matrices(group, b.whole) for group, b in ((0, back_zero), (1, back_one))]
        small = small_vector((back_zero.vgrad, back_one.vgrad), tables_grad, back_one.hb_grad[0])
        loss, item_count = lax.psum(back_one.sums[0, 0], (REP, FSDP)), back_one.sums[2, 0]
        return (loss, item_count, *general_tail(grads, weights, moms, errs, facs, small, small_params, small_mom))

    far = swap(back_zero.far, 1)
    left = back_zero.mine + swap(back_zero.other, 1)
    left = sum_chips(left)
    left, *tables_grad = lax.optimization_barrier((left, *tables_grad))
    far, _ = lax.optimization_barrier((far, left))
    received[0] = scatter_chip_sums(far, back_zero.near)
    bit, early = 1, iter((2, 4))
    while bit < reps:
        left = left + swap_rep(left, bit, reps)
        chip = next(early, 6)
        left, received[0][chip] = lax.optimization_barrier((left, received[0][chip]))
        bit *= 2
    left_other = swap(left, 1)
    left, left_other, received[0] = lax.optimization_barrier((left, left_other, received[0]))
    factors = right_factors(me, (left, left_other), back_zero.whole, back_one.whole, tables_grad)
    received[1] = scatter_cores(back_one, received[1])
    mine = sum_replica(factors.mine, factors.other)
    every = sum_replicas(mine, reps)
    updated = apply_update(
        me,
        weights,
        moms,
        turned,
        (mine, swap(mine, 1), every, swap(every, 1)),
        (factors.basis0, factors.basis1),
        (back_zero.own, back_one.own),
        received,
    )
    odd = (me[0] & 1) == 1
    summed = jnp.where(odd, left, left_other)[:, HALF_LEFT - SMALLS :]
    vgrads = []
    for layer in range(LAYERS):
        first, second = summed[:, 512 * layer : 512 * layer + D], summed[:, 512 * layer + D : 512 * (layer + 1)]
        vgrads.append(jnp.concatenate([first, second], axis=0))
    head_bias_grad = summed[:, 1024 : 1024 + 128].reshape(-1)
    loss, item_count = summed[0, 1024 + 128], summed[1, 1024 + 128]
    table_sums = [updated.small[:, WIDE * i : WIDE * (i + 1)] for i in range(2)]
    new_small_mom = MOMENTUM * small_mom + small_vector(vgrads, table_sums, head_bias_grad)
    return (
        loss,
        item_count,
        *[getattr(updated, "new_" + n) for n in NAMES],
        *[getattr(updated, "new_mom_" + n) for n in NAMES],
        *[getattr(updated, "err_" + n) for n in NAMES],
        *[jnp.swapaxes(getattr(updated, "new_fac_" + n), -1, -2) for n in NAMES],
        small_params - SMALL_RATE * new_small_mom,
        new_small_mom,
    )


FULL_ROWS = (9 * CIN, D, D, D, FF, D)


def whole_matrices(group, packed):
    out = {}
    for name, (at, rows, blocks) in pieces_of(SHARDS, group)[0].items():
        cols = [packed[:, at + c * rows : at + (c + 1) * rows, :].reshape(SHARDS * rows, D) for c in range(blocks)]
        out[name] = jnp.concatenate(cols, axis=1)
    return out


def orthonormal(product, gram_mat):
    lower_tri = jnp.linalg.cholesky(gram_mat)
    return jnp.swapaxes(
        jax.scipy.linalg.solve_triangular(lower_tri, jnp.swapaxes(product, 1, 2), lower=True), 1, 2
    )


def general_tail(grads, weights, moms, errs, facs, small, small_params, small_mom):
    layer = [jnp.stack([grads[g][n] for g in range(2)]) for n in MATRIX_NAMES]
    wholes = [grads[0]["conv"][None], *layer, grads[1]["head"][None, :, :CLASSES]]
    lift = lambda xs: [xs[0][None], *xs[1:5], xs[5][None]]
    weights, moms, facs = lift(weights), lift(moms), lift(facs)
    errors = [errs[0], *[e[0] for e in errs[1:5]], errs[5]]
    merged = [
        lax.psum_scatter(g, FSDP, scatter_dimension=1, tiled=True) + e for g, e in zip(wholes, errors)
    ]
    lefts = lax.psum(
        [jnp.einsum("bio,bok->bik", m, f, precision=PRECISE) for m, f in zip(merged, facs)], "rep"
    )
    grams = lax.psum([jnp.einsum("bik,bil->bkl", p, p, precision=PRECISE) for p in lefts], FSDP)
    bases = [orthonormal(p, g) for p, g in zip(lefts, grams)]
    local = [jnp.einsum("bio,bik->bok", m, b, precision=PRECISE) for m, b in zip(merged, bases)]
    mine = lax.psum([*local, small], FSDP)
    every = lax.psum(mine, REP)
    product = lambda b, q: jnp.einsum("bik,bok->bio", b, q, precision=PRECISE)
    new_errs = [m - product(b, q) for m, b, q in zip(merged, bases, mine)]
    new_moms = [MOMENTUM * m + product(b, q) for m, b, q in zip(moms, bases, every)]
    new_weights = [w - LEARN_RATE * m for w, m in zip(weights, new_moms)]
    drop = lambda xs: [xs[0][0], *xs[1:5], xs[5][0]]
    new_small_mom = MOMENTUM * small_mom + every[6]
    return (
        *drop(new_weights),
        *drop(new_moms),
        new_errs[0],
        *[e[None] for e in new_errs[1:5]],
        new_errs[5],
        *drop(every[:6]),
        small_params - SMALL_RATE * new_small_mom,
        new_small_mom,
    )


def solution(mesh):
    rows, mids = P(FSDP, None), P(None, FSDP, None)
    matrices = (rows, mids, mids, mids, mids, rows)
    errors = (
        P(REP, FSDP, None),
        *[P(REP, None, FSDP, None)] * 4,
        P(REP, FSDP, None),
    )
    return jax.shard_map(
        lambda *args: step(mesh, args),
        mesh=mesh,
        in_specs=(
            P((REP, FSDP), None, None, None),
            P((REP, FSDP)),
            P(REP, FSDP),
            P(),
            *matrices,
            *matrices,
            *errors,
            *[P()] * 8,
        ),
        out_specs=(P(), P(), *matrices, *matrices, *errors, *[P()] * 8),
        check_vma=False,
    )
```
